128 devices in a mesh: lat: 16 (over z, y_hi, core), lon: 8 (over x, y_lo).
Axes of the slice: x: 4, y: 4 (y_hi: 2, y_lo: 2; y = y_hi * 2 + y_lo), z: 4, core: 2. Of those that a mesh axis runs over, the one named last changes fastest.
Arguments:
- tokens: bfloat16 [2, 192, 384, 512], P(None, 'lat', 'lon'), may hold values from -610 to 610
- cotangent: bfloat16 [2, 192, 384, 512], P(None, 'lat', 'lon'), may hold values from -6 to 6
- w_qkv: bfloat16 [512, 1536], replicated, may hold values from -0.25 to 0.25
- w_proj: bfloat16 [512, 512], replicated, may hold values from -0.25 to 0.25
- w_up: bfloat16 [512, 2048], replicated, may hold values from -0.25 to 0.25
- w_down: bfloat16 [2048, 512], replicated, may hold values from -0.125 to 0.125
- pair_bias: float32 [8, 144, 144], replicated, may hold values from -4 to 320
- gain_one: float32 [512], replicated, may hold values from 0.5 to 1.5
- gain_two: float32 [512], replicated, may hold values from 0.5 to 1.5
Outputs:
- grad_tokens: bfloat16 [2, 192, 384, 512], P(None, 'lat', 'lon')
- grad_w_qkv: float32 [512, 1536], replicated
- grad_w_proj: float32 [512, 512], replicated
- grad_w_up: float32 [512, 2048], replicated
- grad_w_down: float32 [2048, 512], replicated
- grad_pair_bias: float32 [8, 144, 144], replicated
- grad_gain_one: float32 [512], replicated
- grad_gain_two: float32 [512], replicated
The draws below stay inside these ranges and needn't reach their ends.
All inputs are finite; a program needn't handle non-finite values.
Results may differ from the reference program's by a relative error of at most 0.015.
Values may be sent and summed in bfloat16 or wider, within the bound.
No kernel may reach another device: no remote copies, remote signals or barrier semaphores. Data moves between devices by JAX's collectives and lax.ppermute only.
A program may use at most 128 MiB of HBM per device.

```python
import jax
import jax.numpy as jnp
from jax import lax

D = 512
HEADS = 8
FF = 2048
LEV = 2
WLAT = 6
WLON = 12
NLAT = 192
NLON = 384
WT = 144
TOKENS = 147456


def draw_tokens(key, part):
    key = jax.random.fold_in(key, 5)
    subkeys = jax.random.split(key, 1)
    values = jnp.clip(jax.random.normal(subkeys[0], (LEV, NLAT, NLON, D), jnp.float32), -6.0, 6.0)
    return values.astype(jnp.bfloat16)


def draw_pair_bias(key, part):
    key = jax.random.fold_in(key, 9)
    subkeys = jax.random.split(key, 1)
    values = jnp.clip(jax.random.normal(subkeys[0], (HEADS, WT, WT), jnp.float32), -4.0, 4.0)
    return values


def steps_of(stream_key, extent, pieces, low, high):
    factor_of = 1.0
    for position, shards_of in pieces:
        steps = jax.random.uniform(jax.random.fold_in(jax.random.fold_in(stream_key, 6), position), (shards_of,), jnp.float32, low / len(pieces), high / len(pieces))
        factor_of = factor_of * jnp.repeat(jnp.exp(steps), extent[position] // shards_of).reshape((-1,) + (1,) * (len(extent) - 1 - position))
    return factor_of


def normal_values(rng, extent, scale, most, cuts=(), held_as=jnp.bfloat16):
    array = scale * jax.random.normal(rng, extent, jnp.float32)
    if cuts:
        array = array * steps_of(rng, extent, cuts, -0.22, 0.18)
    return jnp.clip(array, -most, most).astype(held_as)


def setup_inputs(seed: int = 0) -> dict:
    key_list = jax.random.split(jax.random.key(seed), 10)
    tokens = draw_tokens(jax.random.fold_in(key_list[9], 71), 0)
    cotangent = normal_values(key_list[1], (LEV, NLAT, NLON, D), 1.0, 6.0, ((1, 16), (2, 8)))
    w_qkv = normal_values(key_list[2], (D, 3 * D), D ** -0.5, 0.25)
    w_proj = normal_values(key_list[3], (D, D), D ** -0.5, 0.25)
    w_up = normal_values(key_list[4], (D, FF), D ** -0.5, 0.25)
    w_down = normal_values(key_list[5], (FF, D), FF ** -0.5, 0.125)
    pair_bias = draw_pair_bias(jax.random.fold_in(key_list[9], 71), 0)
    gain_one = jnp.clip(jax.random.uniform(key_list[7], (D,), jnp.float32, 0.5, 1.5), 0.5, 1.5)
    gain_two = jnp.clip(jax.random.uniform(key_list[8], (D,), jnp.float32, 0.5, 1.5), 0.5, 1.5)
    return {"tokens": tokens, "cotangent": cotangent, "w_qkv": w_qkv, "w_proj": w_proj, "w_up": w_up, "w_down": w_down, "pair_bias": pair_bias, "gain_one": gain_one, "gain_two": gain_two}


EPSILON = 1e-05
MASKED = -1e+30

def layer_stats(values):
    average = lax.optimization_barrier(jnp.mean(values, -1, keepdims=True))
    centred = values - average
    variance = lax.optimization_barrier(jnp.mean(centred * centred, -1, keepdims=True))
    inv_std = lax.rsqrt(variance + EPSILON)
    return (centred * inv_std, inv_std)

def layer_back(grad_out, gain_vec, normed, inv_std):
    scaled = grad_out * gain_vec
    centred_grad = scaled - lax.optimization_barrier(jnp.mean(scaled, -1, keepdims=True)) - normed * lax.optimization_barrier(jnp.mean(scaled * normed, -1, keepdims=True))
    return centred_grad * inv_std

def gelu_back(hidden, grad_act):
    _, pullback = jax.vjp(jax.nn.gelu, hidden)
    return pullback(grad_act)[0]

def split_windows(tensor):
    levels, height, breadth, channels = tensor.shape
    rows_win = height // WLAT
    columns_win = breadth // WLON
    tensor = tensor.reshape(levels, rows_win, WLAT, columns_win, WLON, channels)
    return tensor.transpose(1, 3, 0, 2, 4, 5).reshape(rows_win * columns_win, levels * WLAT * WLON, channels)

def join_windows(windows, levels, height, breadth):
    channels = windows.shape[-1]
    rows_win = height // WLAT
    columns_win = breadth // WLON
    windows = windows.reshape(rows_win, columns_win, levels, WLAT, WLON, channels)
    return windows.transpose(2, 0, 3, 1, 4, 5).reshape(levels, height, breadth, channels)

def window_forward(qkv_win, pair_bias, same_region):
    count_win, window_len, triple = qkv_win.shape
    features = triple // 3
    head_size = features // HEADS
    score_scale = head_size ** (-0.5)
    head_parts = lax.optimization_barrier(qkv_win).reshape(count_win, window_len, 3, HEADS, head_size).astype(jnp.float32)
    queries = head_parts[:, :, 0]
    key_part = head_parts[:, :, 1]
    val_part = head_parts[:, :, 2]
    scores = jnp.einsum('wqhd,wkhd->whqk', queries, key_part) * score_scale + pair_bias[None]
    scores = jnp.where(same_region[:, None], scores, MASKED)
    row_top = lax.optimization_barrier(jnp.max(scores, -1, keepdims=True))
    exponent = jnp.exp(scores - row_top)
    attention = exponent / lax.optimization_barrier(jnp.sum(exponent, -1, keepdims=True))
    attention_low = lax.optimization_barrier(attention.astype(jnp.bfloat16))
    mix_out = jnp.einsum('whqk,wkhd->wqhd', attention_low.astype(jnp.float32), val_part)
    return (mix_out.reshape(count_win, window_len, features).astype(jnp.bfloat16), attention, attention_low)

def window_backward(qkv_win, attention, attention_low, grad_win):
    count_win, window_len, triple = qkv_win.shape
    features = triple // 3
    head_size = features // HEADS
    score_scale = head_size ** (-0.5)
    head_parts = lax.optimization_barrier(qkv_win).reshape(count_win, window_len, 3, HEADS, head_size).astype(jnp.float32)
    queries = head_parts[:, :, 0]
    key_part = head_parts[:, :, 1]
    val_part = head_parts[:, :, 2]
    grad_heads = lax.optimization_barrier(grad_win).reshape(count_win, window_len, HEADS, head_size).astype(jnp.float32)
    grad_probs = jnp.einsum('wqhd,wkhd->whqk', grad_heads, val_part)
    grad_val = jnp.einsum('whqk,wqhd->wkhd', attention_low.astype(jnp.float32), grad_heads)
    grad_scores = attention * (grad_probs - lax.optimization_barrier(jnp.sum(grad_probs * attention, -1, keepdims=True)))
    low_scores = lax.optimization_barrier(grad_scores.astype(jnp.bfloat16)).astype(jnp.float32)
    grad_query = jnp.einsum('whqk,wkhd->wqhd', low_scores, key_part) * score_scale
    grad_key = jnp.einsum('whqk,wqhd->wkhd', low_scores, queries) * score_scale
    grad_qkv = jnp.stack([grad_query, grad_key, grad_val], 2).reshape(count_win, window_len, triple).astype(jnp.bfloat16)
    return (grad_qkv, lax.optimization_barrier(jnp.sum(grad_scores, 0)))

def attn_forward(shifted, lat_rows, lat_total, gain_one, w_qkv, pair_bias):
    levels, height, breadth, features = shifted.shape
    normed, inv_std = layer_stats(shifted.astype(jnp.float32).reshape(-1, features))
    act_one = (normed * gain_one).astype(jnp.bfloat16)
    qkv = jnp.dot(act_one, w_qkv, preferred_element_type=jnp.float32).astype(jnp.bfloat16)
    qkv_win = split_windows(qkv.reshape(levels, height, breadth, 3 * features))
    region = (lat_rows >= lat_total - WLAT).astype(jnp.int32) + (lat_rows >= lat_total - WLAT // 2).astype(jnp.int32)
    labels = split_windows(jnp.broadcast_to(region[None, :, None, None], (levels, height, breadth, 1)))[:, :, 0]
    same_region = labels[:, :, None] == labels[:, None, :]
    mix_win, attention, attention_low = window_forward(qkv_win, pair_bias, same_region)
    mix_out = join_windows(mix_win, levels, height, breadth).reshape(-1, features)
    return (mix_out, (normed, inv_std, act_one, qkv_win, attention, attention_low))

def attn_backward(saved, grad_mixed, block_dims, gain_one, w_qkv):
    normed, inv_std, act_one, qkv_win, attention, attention_low = saved
    levels, height, breadth = block_dims
    features = grad_mixed.shape[-1]
    grad_win = split_windows(grad_mixed.reshape(levels, height, breadth, features))
    grad_qkv_win, sum_bias = window_backward(qkv_win, attention, attention_low, grad_win)
    grad_qkv = join_windows(grad_qkv_win, levels, height, breadth).reshape(-1, 3 * features)
    sum_qkv = jnp.dot(act_one.T, grad_qkv, preferred_element_type=jnp.float32)
    grad_act_one = jnp.dot(grad_qkv, w_qkv.T, preferred_element_type=jnp.float32)
    sum_gain = lax.optimization_barrier(jnp.sum(grad_act_one * normed, 0))
    grad_branch = layer_back(grad_act_one, gain_one, normed, inv_std).astype(jnp.bfloat16)
    return (grad_branch, (sum_qkv, sum_bias, sum_gain))

def mlp_part(inputs, mix_out, cotan_rows, w_proj, gain_two, w_up, w_down):
    residual = inputs.astype(jnp.float32) + jnp.dot(mix_out, w_proj, preferred_element_type=jnp.float32)
    normed, inv_std = layer_stats(residual)
    act_two = (normed * gain_two).astype(jnp.bfloat16)
    hidden = jnp.dot(act_two, w_up, preferred_element_type=jnp.float32)
    activated = jax.nn.gelu(hidden).astype(jnp.bfloat16)
    grad_act = jnp.dot(cotan_rows, w_down.T, preferred_element_type=jnp.float32)
    grad_hidden = gelu_back(hidden, grad_act).astype(jnp.bfloat16)
    sum_down = jnp.dot(activated.T, cotan_rows, preferred_element_type=jnp.float32)
    sum_up = jnp.dot(act_two.T, grad_hidden, preferred_element_type=jnp.float32)
    grad_norm = jnp.dot(grad_hidden, w_up.T, preferred_element_type=jnp.float32)
    sum_gain = lax.optimization_barrier(jnp.sum(grad_norm * normed, 0))
    grad_residual = cotan_rows.astype(jnp.float32) + layer_back(grad_norm, gain_two, normed, inv_std)
    residual_low = grad_residual.astype(jnp.bfloat16)
    sum_proj = jnp.dot(mix_out.T, residual_low, preferred_element_type=jnp.float32)
    grad_mixed = jnp.dot(residual_low, w_proj.T, preferred_element_type=jnp.float32).astype(jnp.bfloat16)
    return (grad_residual, grad_mixed, (sum_proj, sum_up, sum_down, sum_gain))

def reference(tokens, cotangent, w_qkv, w_proj, w_up, w_down, pair_bias, gain_one, gain_two):
    rolled = jnp.roll(tokens, (-(WLAT // 2), -(WLON // 2)), (1, 2))
    rolled_cot = jnp.roll(cotangent, (-(WLAT // 2), -(WLON // 2)), (1, 2))
    band_count = NLAT // WLAT

    def to_bands(tensor):
        return tensor.reshape(LEV, band_count, WLAT, NLON, D).transpose(1, 0, 2, 3, 4)
    totals_in = (jnp.zeros((D, 3 * D), jnp.float32), jnp.zeros((D, D), jnp.float32), jnp.zeros((D, FF), jnp.float32), jnp.zeros((FF, D), jnp.float32), jnp.zeros((HEADS, WT, WT), jnp.float32), jnp.zeros((D,), jnp.float32), jnp.zeros((D,), jnp.float32))

    def band_step(totals, band_item):
        band_tok, band_cot, band_index = band_item
        lat_rows = band_index * WLAT + jnp.arange(WLAT, dtype=jnp.int32)
        mix_out, saved = attn_forward(band_tok, lat_rows, NLAT, gain_one, w_qkv, pair_bias)
        grad_residual, grad_mixed, mlp_sums = mlp_part(band_tok.reshape(-1, D), mix_out, band_cot.reshape(-1, D), w_proj, gain_two, w_up, w_down)
        grad_branch, attn_sums = attn_backward(saved, grad_mixed, (LEV, WLAT, NLON), gain_one, w_qkv)
        branch_wide = lax.optimization_barrier(grad_branch).astype(jnp.float32)
        grad_band = (grad_residual + branch_wide).astype(jnp.bfloat16).reshape(LEV, WLAT, NLON, D)
        totals_out = (totals[0] + attn_sums[0], totals[1] + mlp_sums[0], totals[2] + mlp_sums[1], totals[3] + mlp_sums[2], totals[4] + attn_sums[1], totals[5] + attn_sums[2], totals[6] + mlp_sums[3])
        return (totals_out, grad_band)
    totals, grad_bands = lax.scan(band_step, totals_in, (to_bands(rolled), to_bands(rolled_cot), jnp.arange(band_count, dtype=jnp.int32)))
    grad_rolled = grad_bands.transpose(1, 0, 2, 3, 4).reshape(LEV, NLAT, NLON, D)
    grad_tokens = jnp.roll(grad_rolled, (WLAT // 2, WLON // 2), (1, 2))
    weight_scale = TOKENS ** (-0.5)
    bias_scale = WT * weight_scale
    return (grad_tokens, totals[0] * weight_scale, totals[1] * weight_scale, totals[2] * weight_scale, totals[3] * weight_scale, totals[4] * bias_scale, totals[5] * weight_scale, totals[6] * weight_scale)
```

```python
import functools

import jax
import jax.numpy as jnp
from jax import lax
from jax.experimental import pallas as pl
from jax.experimental.pallas import tpu as pltpu
from jax.sharding import PartitionSpec as P

HEADS = 8
WLAT = 6
WLON = 12
WT = 144
D = 512
QKV = 1536
FF = 2048
LEVELS = 2
HEIGHT = 12
BREADTH = 48
WINDOWS = 8
ROWS = WINDOWS * WT
EPSILON = 1e-05
MASKED = -1e30
F32 = jnp.float32
BF16 = jnp.bfloat16
PIECES = 32
ONE_ROWS = 512
TWO_ROWS = 304
PROJ_AT = 6144
BIAS_AT = 8192
REST_AT = 9344
GAIN_AT = 9488
TWO_TOTAL = PIECES * TWO_ROWS
VMEM_LIMIT = 56 * 1024 * 1024

NN = (((1,), (0,)), ((), ()))
NT = (((1,), (1,)), ((), ()))
TN = (((0,), (0,)), ((), ()))


def mm(a, b, dims=NN):
    return lax.dot_general(a, b, dims, preferred_element_type=F32)


def stats_of(values):
    average = jnp.mean(values, -1, keepdims=True)
    centred = values - average
    variance = jnp.mean(centred * centred, -1, keepdims=True)
    inv_std = lax.rsqrt(variance + EPSILON)
    return centred * inv_std, inv_std


def back_of(grad_out, gain_vec, normed, inv_std):
    scaled = grad_out * gain_vec
    return (
        scaled
        - jnp.mean(scaled, -1, keepdims=True)
        - normed * jnp.mean(scaled * normed, -1, keepdims=True)
    ) * inv_std


def run_at(level, row, column):
    window = (row // WLAT) * 4 + column
    return window * WT + level * (WT // 2) + (row % WLAT) * WLON


def gather_windows(main_ref, lon_ref, lat_ref, both_ref, line, wide, out_ref):
    for level in range(LEVELS):
        for row in range(HEIGHT):
            if row < HEIGHT - WLAT // 2:
                line[0:BREADTH] = main_ref[level, row + WLAT // 2].astype(F32)
                line[BREADTH : BREADTH + 6] = lon_ref[level, row + WLAT // 2].astype(F32)
            else:
                line[0:BREADTH] = lat_ref[level, row - (HEIGHT - WLAT // 2)].astype(F32)
                line[BREADTH : BREADTH + 6] = both_ref[level, row - (HEIGHT - WLAT // 2)].astype(F32)
            for column in range(4):
                at = run_at(level, row, column)
                wide[at : at + WLON] = line[6 + WLON * column : 18 + WLON * column]

    def narrow(window, _):
        rows = pl.ds(pl.multiple_of(window * WT, 16), WT)
        out_ref[rows] = wide[rows].astype(BF16)
        return 0

    lax.fori_loop(0, WINDOWS, narrow, 0)


def slot_of(place_ref, block):
    core = block // 16
    return (
        ((core + 2 - place_ref[0]) % 2) * 16
        + (((block // 4) % 4 + 4 - place_ref[1 + core]) % 4) * 4
        + (block % 4 + 4 - place_ref[2 + core]) % 4
    )


def slot_from(place_ref, block):
    core = block // 16
    return (
        ((place_ref[0] + 2 - core) % 2) * 16
        + ((place_ref[1 + core] + 4 - (block // 4) % 4) % 4) * 4
        + (place_ref[2 + core] + 4 - block % 4) % 4
    )


def window_rows(window):
    return pl.ds(pl.multiple_of(window * WT, 16), WT)


def forward_kernel(
    place_ref, tok, tok_lon, tok_lat, tok_both, cot, cot_lon, cot_lat, cot_both,
    w_qkv, w_proj, w_up, w_down, bias_t, mask_t, gain_one, gain_two,
    xw, qkv, probs, grad_mixed, grad_res, sums_one, sum_proj, sum_gain,
    line, wide, cotw, act, mix, normed, inv_two, act_t, activated, grad_hidden, grad_norm,
):
    gather_windows(tok, tok_lon, tok_lat, tok_both, line, wide, xw)
    gather_windows(cot, cot_lon, cot_lat, cot_both, line, wide, cotw)

    def norm_one(window, _):
        rows = window_rows(window)
        values, _ = stats_of(xw[rows].astype(F32))
        act[rows] = (values * gain_one[...]).astype(BF16)
        return 0

    lax.fori_loop(0, WINDOWS, norm_one, 0)

    def project(n, _):
        cols = pl.ds(pl.multiple_of(n * 256, 256), 256)
        qkv[:, cols] = mm(act[...], w_qkv[:, cols]).astype(BF16)
        return 0

    lax.fori_loop(0, QKV // 256, project, 0)

    lane = lax.broadcasted_iota(jnp.int32, (1, 128), 1)
    first = lane < 64
    halves = (first.astype(BF16), (lane >= 64).astype(BF16))

    def attend(window, _):
        rows = window_rows(window)
        for pair in range(HEADS // 2):
            cols = slice(128 * pair, 128 * pair + 128)
            query = qkv[rows, cols]
            key = qkv[rows, 512 + 128 * pair : 640 + 128 * pair]
            val = qkv[rows, 1024 + 128 * pair : 1152 + 128 * pair]
            mixed = []
            for half in range(2):
                head = 2 * pair + half
                scores = mm(key, query * halves[half], NT) * 0.125 + bias_t[head]
                scores = scores + jnp.where(window >= 4, mask_t[...], 0.0)
                top = jnp.max(scores, 0, keepdims=True)
                exponent = jnp.exp(scores - top)
                total = jnp.sum(exponent, 0, keepdims=True)
                weights = (exponent * (1.0 / total)).astype(BF16)
                probs[window, head] = weights
                mixed.append(mm(weights, val, TN))
            mix[rows, cols] = jnp.where(first, mixed[0], mixed[1]).astype(BF16)
        return 0

    lax.fori_loop(0, WINDOWS, attend, 0)

    def norm_two(window, _):
        rows = window_rows(window)
        residual = xw[rows].astype(F32) + mm(mix[rows], w_proj[...])
        values, inv_std = stats_of(residual)
        normed[rows] = values
        inv_two[rows] = inv_std
        act[rows] = (values * gain_two[...]).astype(BF16)
        grad_norm[rows] = jnp.zeros((WT, D), F32)
        return 0

    lax.fori_loop(0, WINDOWS, norm_two, 0)
    act_t[...] = act[...].T

    c0 = 0.7978845608028654
    c1 = c0 * 0.044715

    def mlp(f, _):
        cols = pl.ds(pl.multiple_of(f * 512, 512), 512)

        def rows_of(r, _):
            rows = pl.ds(pl.multiple_of(r * WT, 16), WT)
            u = mm(act[rows], w_up[:, cols])
            grad_act = mm(cotw[rows], w_down[cols, :], NT)
            square = u * u
            gate = 0.5 + 0.5 * jnp.tanh(u * (c0 + c1 * square))
            value = u * gate
            activated[rows] = value.astype(BF16)
            slope = gate + value * (1.0 - gate) * (2.0 * c0 + 6.0 * c1 * square)
            grad_hidden[rows] = (grad_act * slope).astype(BF16)
            return 0

        lax.fori_loop(0, WINDOWS, rows_of, 0)
        down = mm(activated[...], cotw[...], TN).astype(BF16)
        for j in range(4):
            sums_one[slot_of(place_ref, 16 + f * 4 + j)] = down[:, 128 * j : 128 * j + 128]
        up = mm(act_t[...], grad_hidden[...]).astype(BF16)
        for j in range(4):
            sums_one[slot_of(place_ref, f * 4 + j)] = up[:, 128 * j : 128 * j + 128]

        def norm_rows(r, _):
            rows = pl.ds(pl.multiple_of(r * WT, 16), WT)
            grad_norm[rows] += mm(grad_hidden[rows], w_up[:, cols], NT)
            return 0

        lax.fori_loop(0, WINDOWS, norm_rows, 0)
        return 0

    lax.fori_loop(0, FF // 512, mlp, 0)

    def back(window, total):
        rows = window_rows(window)
        grads = grad_norm[rows]
        values = normed[rows]
        total = total + jnp.sum(grads * values, 0, keepdims=True)
        residual = cotw[rows].astype(F32) + back_of(grads, gain_two[...], values, inv_two[rows])
        grad_res[rows] = residual
        low = residual.astype(BF16)
        act[rows] = low
        grad_mixed[rows] = mm(low, w_proj[...], NT).astype(BF16)
        return total

    sum_gain[...] = lax.fori_loop(0, WINDOWS, back, jnp.zeros((1, D), F32))
    proj = mm(mix[...], act[...], TN).astype(BF16)
    for j in range(4):
        sum_proj[j] = proj[:, 128 * j : 128 * j + 128]


def backward_kernel(
    place_ref, xw, qkv, probs, grad_mixed, grad_res, sum_proj, sum_gain_two, w_qkv, gain_one,
    grad_grid, sums_two,
    act, act_t, grad_qkv, bias_acc, wide, line, flat,
):
    lane = lax.broadcasted_iota(jnp.int32, (1, 128), 1)
    first = lane < 64
    halves = (first.astype(BF16), (lane >= 64).astype(BF16))
    bias_acc[...] = jnp.zeros_like(bias_acc)

    def attend(window, _):
        rows = window_rows(window)
        for pair in range(HEADS // 2):
            cols = slice(128 * pair, 128 * pair + 128)
            kcols = slice(512 + 128 * pair, 640 + 128 * pair)
            vcols = slice(1024 + 128 * pair, 1152 + 128 * pair)
            query = qkv[rows, cols]
            key = qkv[rows, kcols]
            val = qkv[rows, vcols]
            out = grad_mixed[rows, cols]
            got = []
            for half in range(2):
                head = 2 * pair + half
                grad_probs = mm(val, out * halves[half], NT)
                low_probs = probs[window, head]
                weights = low_probs.astype(F32)
                product = grad_probs * weights
                grads = product - weights * jnp.sum(product, 0, keepdims=True)
                bias_acc[head] += grads
                low = grads.astype(BF16)
                got.append((mm(low, key, TN), mm(low, query), mm(low_probs, out)))
            grad_qkv[rows, cols] = (jnp.where(first, got[0][0], got[1][0]) * 0.125).astype(BF16)
            grad_qkv[rows, kcols] = (jnp.where(first, got[0][1], got[1][1]) * 0.125).astype(BF16)
            grad_qkv[rows, vcols] = jnp.where(first, got[0][2], got[1][2]).astype(BF16)
        return 0

    lax.fori_loop(0, WINDOWS, attend, 0)

    def branch(window, total):
        rows = window_rows(window)
        values, inv_std = stats_of(xw[rows].astype(F32))
        act[rows] = (values * gain_one[...]).astype(BF16)
        grads = mm(grad_qkv[rows], w_qkv[...], NT)
        total = total + jnp.sum(grads * values, 0, keepdims=True)
        low = back_of(grads, gain_one[...], values, inv_std).astype(BF16)
        wide[rows] = grad_res[rows] + low.astype(F32)
        return total

    total = lax.fori_loop(0, WINDOWS, branch, jnp.zeros((1, D), F32))
    act_t[...] = act[...].T

    def weights(n, _):
        cols = pl.ds(pl.multiple_of(n * 256, 256), 256)
        part = mm(act_t[...], grad_qkv[:, cols]).astype(BF16)
        for j in range(2):
            at = pl.multiple_of((n * 2 + j) * 512, 512)
            flat[pl.ds(at, 512)] = part[:, 128 * j : 128 * j + 128]
        return 0

    lax.fori_loop(0, QKV // 256, weights, 0)
    for j in range(4):
        flat[PROJ_AT + 512 * j : PROJ_AT + 512 * j + 512] = sum_proj[j]
    for head in range(HEADS):
        at = BIAS_AT + WT * head
        flat[at : at + WT] = bias_acc[head, :, 0:128].astype(BF16)
    rest = jnp.concatenate([bias_acc[head, :, 128:144] for head in range(HEADS)], 1)
    flat[REST_AT : REST_AT + WT] = rest.astype(BF16)
    gains = [v[:, 128 * j : 128 * j + 128] for v in (total, sum_gain_two[...]) for j in range(4)]
    gains = jnp.concatenate(gains + [jnp.zeros((8, 128), F32)], 0)
    flat[GAIN_AT : GAIN_AT + 16] = gains.astype(BF16)
    flat[GAIN_AT + 16 :] = jnp.zeros((TWO_TOTAL - GAIN_AT - 16, 128), BF16)
    for piece in range(PIECES):
        sums_two[slot_of(place_ref, piece)] = flat[piece * TWO_ROWS : (piece + 1) * TWO_ROWS]

    for level in range(LEVELS):
        for row in range(HEIGHT):
            for column in range(4):
                at = run_at(level, row, column)
                line[WLON * column : WLON * column + WLON] = wide[at : at + WLON]
            grad_grid[level, row] = line[0:BREADTH].astype(BF16)


def finish_one_kernel(scale, place_ref, up_in, down_in, up_out, down_out):
    up_out[...] = up_in[0].astype(F32) * scale
    down_out[...] = down_in[0].astype(F32) * scale


def finish_two_kernel(scale, place_ref, sums, qkv, proj, bias, gain_one, gain_two, flat, arrived):
    copies = []
    for piece in range(PIECES):
        copy = pltpu.make_async_copy(
            sums.at[slot_from(place_ref, piece), pl.ds(ONE_ROWS, TWO_ROWS)],
            flat.at[pl.ds(piece * TWO_ROWS, TWO_ROWS)],
            arrived.at[piece],
        )
        copy.start()
        copies.append(copy)
    for copy in copies:
        copy.wait()
    for j in range(12):
        qkv[:, 128 * j : 128 * j + 128] = flat[512 * j : 512 * j + 512].astype(F32) * scale
    for j in range(4):
        at = PROJ_AT + 512 * j
        proj[:, 128 * j : 128 * j + 128] = flat[at : at + 512].astype(F32) * scale
    rest = flat[REST_AT : REST_AT + WT].astype(F32) * (scale * WT)
    for head in range(HEADS):
        at = BIAS_AT + WT * head
        bias[head, :, 0:128] = flat[at : at + WT].astype(F32) * (scale * WT)
        bias[head, :, 128:144] = rest[:, 16 * head : 16 * head + 16]
    gains = flat[GAIN_AT : GAIN_AT + 16].astype(F32) * scale
    for j in range(4):
        gain_one[:, 128 * j : 128 * j + 128] = gains[j : j + 1]
        gain_two[:, 128 * j : 128 * j + 128] = gains[4 + j : 5 + j]


def shape(*dims, dtype=BF16):
    return jax.ShapeDtypeStruct(dims, dtype)


def params():
    return pltpu.CompilerParams(vmem_limit_bytes=VMEM_LIMIT)


def specs(count):
    return [pl.BlockSpec(memory_space=pltpu.SMEM)] + [
        pl.BlockSpec(memory_space=pltpu.VMEM) for _ in range(count)
    ]


def forward(*operands):
    return pl.pallas_call(
        forward_kernel,
        out_shape=(
            shape(ROWS, D), shape(ROWS, QKV), shape(WINDOWS, HEADS, WT, WT), shape(ROWS, D),
            shape(ROWS, D, dtype=F32), shape(PIECES, ONE_ROWS, 128), shape(4, 512, 128),
            shape(1, D, dtype=F32),
        ),
        in_specs=specs(len(operands) - 1),
        scratch_shapes=[
            pltpu.VMEM((56, D), F32),
            pltpu.VMEM((ROWS, D), F32),
            pltpu.VMEM((ROWS, D), BF16),
            pltpu.VMEM((ROWS, D), BF16),
            pltpu.VMEM((ROWS, D), BF16),
            pltpu.VMEM((ROWS, D), F32),
            pltpu.VMEM((ROWS, 1), F32),
            pltpu.VMEM((D, ROWS), BF16),
            pltpu.VMEM((ROWS, 512), BF16),
            pltpu.VMEM((ROWS, 512), BF16),
            pltpu.VMEM((ROWS, D), F32),
        ],
        compiler_params=params(),
        name="forward_mlp",
    )(*operands)


def backward(*operands):
    return pl.pallas_call(
        backward_kernel,
        out_shape=(shape(LEVELS, HEIGHT, BREADTH, D), shape(PIECES, TWO_ROWS, 128)),
        in_specs=specs(len(operands) - 1),
        scratch_shapes=[
            pltpu.VMEM((ROWS, D), BF16),
            pltpu.VMEM((D, ROWS), BF16),
            pltpu.VMEM((ROWS, QKV), BF16),
            pltpu.VMEM((HEADS, WT, WT), F32),
            pltpu.VMEM((ROWS, D), F32),
            pltpu.VMEM((48, D), F32),
            pltpu.VMEM((TWO_TOTAL, 128), BF16),
        ],
        compiler_params=params(),
        name="attention_back",
    )(*operands)


def finish_one(place, sums, scale):
    return pl.pallas_call(
        functools.partial(finish_one_kernel, scale),
        out_shape=(shape(D, FF, dtype=F32), shape(FF, D, dtype=F32)),
        grid_spec=pltpu.PrefetchScalarGridSpec(
            num_scalar_prefetch=1,
            grid=(16,),
            in_specs=[
                pl.BlockSpec((1, 512, 128), lambda i, place: (slot_from(place, i), 0, 0)),
                pl.BlockSpec((1, 512, 128), lambda i, place: (slot_from(place, i + 16), 0, 0)),
            ],
            out_specs=[
                pl.BlockSpec((512, 128), lambda i, place: (0, i)),
                pl.BlockSpec((512, 128), lambda i, place: (i // 4, i % 4)),
            ],
        ),
        compiler_params=params(),
        name="finish_mlp",
    )(place, sums, sums)


def finish_two(place, sums, scale):
    return pl.pallas_call(
        functools.partial(finish_two_kernel, scale),
        out_shape=(
            shape(D, QKV, dtype=F32), shape(D, D, dtype=F32), shape(HEADS, WT, WT, dtype=F32),
            shape(1, D, dtype=F32), shape(1, D, dtype=F32),
        ),
        in_specs=[pl.BlockSpec(memory_space=pltpu.SMEM), pl.BlockSpec(memory_space=pl.ANY)],
        scratch_shapes=[
            pltpu.VMEM((TWO_TOTAL, 128), BF16),
            pltpu.SemaphoreType.DMA((PIECES,)),
        ],
        compiler_params=params(),
        name="finish_attention",
    )(place, sums)


def neighbour(array, lat_by, lon_by):
    lat_count, lon_count = lax.axis_size("lat"), lax.axis_size("lon")
    pairs = []
    for i in range(lat_count):
        for j in range(lon_count):
            to = ((i + lat_by) % lat_count) * lon_count + (j + lon_by) % lon_count
            pairs.append((i * lon_count + j, to))
    return lax.ppermute(array, ("lat", "lon"), pairs)


def halos(tensor):
    edge, top = WLON // 2, WLAT // 2
    return (
        neighbour(tensor[:, :, :edge], 0, -1),
        neighbour(tensor[:, :top], -1, 0),
        neighbour(tensor[:, :top, :edge], -1, -1),
    )


def bring_home(grid):
    edge, top = WLON // 2, WLAT // 2
    from_lon = neighbour(grid[:, :-top, -edge:], 0, 1)
    from_lat = neighbour(grid[:, -top:, :-edge], 1, 0)
    from_both = neighbour(grid[:, -top:, -edge:], 1, 1)
    upper = jnp.concatenate([from_both, from_lat], 2)
    lower = jnp.concatenate([from_lon, grid[:, :-top, :-edge]], 2)
    return jnp.concatenate([upper, lower], 1)


def position(lat, lon):
    return lat % 2, (lon // 2, (lat // 2) % 2 * 2 + lon % 2, lat // 4)


ORDERS = ((0, 1, 2), (1, 2, 0))


def place_of():
    core, chip = position(lax.axis_index("lat"), lax.axis_index("lon"))
    return jnp.stack([core, *chip]).astype(jnp.int32)


def along(array, stage, by):
    pairs = []
    for lat in range(16):
        for lon in range(8):
            core, chip = position(lat, lon)
            chip = list(chip)
            axis = ORDERS[core][stage]
            chip[axis] = (chip[axis] + by) % 4
            x, y, z = chip
            to = (z * 4 + y // 2 * 2 + core) * 8 + x * 2 + y % 2
            pairs.append((lat * 8 + lon, to))
    return lax.ppermute(array, ("lat", "lon"), pairs)


def other_core(array):
    return lax.ppermute(array, "lat", [(i, i ^ 1) for i in range(16)])


def added(*terms):
    total = terms[0].astype(F32)
    for term in terms[1:]:
        total = total + term.astype(F32)
    return total.astype(BF16)


def scatter_sum(sums):
    held = added(sums[:16], other_core(sums[16:]))
    held = added(held[:4], *[along(held[4 * k : 4 * k + 4], 0, k) for k in (1, 2, 3)])
    return added(held[0], *[along(held[k], 1, k) for k in (1, 2, 3)])


def all_sum(sums_one, sums_two):
    share = jnp.concatenate([scatter_sum(sums_one), scatter_sum(sums_two)], 0)
    share = lax.optimization_barrier(share)
    one, two, three = [along(share, 2, k).astype(F32) for k in (1, 2, 3)]
    share = ((share.astype(F32) + two) + (one + three)).astype(BF16)
    held = jnp.stack([share] + [along(share, 1, k) for k in (1, 2, 3)])
    held = jnp.concatenate([held] + [along(held, 0, k) for k in (1, 2, 3)])
    return jnp.concatenate([held, other_core(held)])


def local(tokens, cotangent, w_qkv, w_proj, w_up, w_down, pair_bias, gain_one, gain_two):
    total_tokens = ROWS * lax.axis_size("lat") * lax.axis_size("lon")
    scale = total_tokens ** (-0.5)
    place = place_of()
    token = jnp.arange(WT, dtype=jnp.int32)
    lower = (token // WLON) % WLAT >= WLAT // 2
    apart = (lower[:, None] != lower[None, :]) & (
        lax.axis_index("lat") == lax.axis_size("lat") - 1
    )
    mask_t = jnp.where(apart, MASKED, 0.0).astype(F32)
    bias_t = jnp.swapaxes(pair_bias, 1, 2)
    gain_one = gain_one.reshape(1, D)
    gain_two = gain_two.reshape(1, D)
    xw, qkv, probs, grad_mixed, grad_res, sums_one, sum_proj, sum_gain_two = forward(
        place, tokens, *halos(tokens), cotangent, *halos(cotangent),
        w_qkv, w_proj, w_up, w_down, bias_t, mask_t, gain_one, gain_two,
    )
    grad_grid, sums_two = backward(
        place, xw, qkv, probs, grad_mixed, grad_res, sum_proj, sum_gain_two, w_qkv, gain_one
    )
    grad_tokens = bring_home(grad_grid)
    sums = all_sum(sums_one, sums_two)
    sum_up, sum_down = finish_one(place, sums, scale)
    sum_qkv, sum_proj, sum_bias, sum_one, sum_two = finish_two(place, sums, scale)
    return (
        grad_tokens,
        sum_qkv,
        sum_proj,
        sum_up,
        sum_down,
        jnp.swapaxes(sum_bias, 1, 2),
        sum_one.reshape(D),
        sum_two.reshape(D),
    )


def solution(mesh):
    grid = P(None, "lat", "lon", None)
    in_specs = (grid, grid, P(), P(), P(), P(), P(), P(), P())
    out_specs = (grid, P(), P(), P(), P(), P(), P(), P())
    return jax.shard_map(local, mesh=mesh, in_specs=in_specs, out_specs=out_specs, check_vma=False)
```

```python
import functools

import jax
import jax.numpy as jnp
from jax import lax
from jax.experimental import pallas as pl
from jax.experimental.pallas import tpu as pltpu
from jax.sharding import PartitionSpec as P

HEADS = 8
WLAT = 6
WLON = 12
WT = 144
D = 512
QKV = 1536
FF = 2048
LEVELS = 2
HEIGHT = 12
BREADTH = 48
WINDOWS = 8
ROWS = WINDOWS * WT
EPSILON = 1e-05
MASKED = -1e30
F32 = jnp.float32
BF16 = jnp.bfloat16
PIECES = 32
ONE_ROWS = 512
TWO_ROWS = 304
PROJ_AT = 6144
BIAS_AT = 8192
REST_AT = 9344
GAIN_AT = 9488
TWO_TOTAL = PIECES * TWO_ROWS
VMEM_LIMIT = 56 * 1024 * 1024
M_NORM = 576
M_UP = 1152
M_BACK = 576
M_BRANCH = 576
G_FORWARD = 4
G_BACKWARD = 2
F_STEP = 512

NN = (((1,), (0,)), ((), ()))
NT = (((1,), (1,)), ((), ()))
TN = (((0,), (0,)), ((), ()))


def mm(a, b, dims=NN):
    return lax.dot_general(a, b, dims, preferred_element_type=F32)


def stats_of(values):
    average = jnp.mean(values, -1, keepdims=True)
    centred = values - average
    variance = jnp.mean(centred * centred, -1, keepdims=True)
    inv_std = lax.rsqrt(variance + EPSILON)
    return centred * inv_std, inv_std


def back_of(grad_out, gain_vec, normed, inv_std):
    scaled = grad_out * gain_vec
    return (
        scaled
        - jnp.mean(scaled, -1, keepdims=True)
        - normed * jnp.mean(scaled * normed, -1, keepdims=True)
    ) * inv_std


def run_at(level, row, column):
    window = (row // WLAT) * 4 + column
    return window * WT + level * (WT // 2) + (row % WLAT) * WLON


def gather_windows(main_ref, lon_ref, lat_ref, both_ref, line, wide, out_ref):
    for level in range(LEVELS):
        for row in range(HEIGHT):
            if row < HEIGHT - WLAT // 2:
                line[0:BREADTH] = main_ref[level, row + WLAT // 2].astype(F32)
                line[BREADTH : BREADTH + 6] = lon_ref[level, row + WLAT // 2].astype(F32)
            else:
                line[0:BREADTH] = lat_ref[level, row - (HEIGHT - WLAT // 2)].astype(F32)
                line[BREADTH : BREADTH + 6] = both_ref[level, row - (HEIGHT - WLAT // 2)].astype(F32)
            for column in range(4):
                at = run_at(level, row, column)
                wide[at : at + WLON] = line[6 + WLON * column : 18 + WLON * column]

    def narrow(window, _):
        rows = pl.ds(pl.multiple_of(window * WT, 16), WT)
        out_ref[rows] = wide[rows].astype(BF16)
        return 0

    lax.fori_loop(0, WINDOWS, narrow, 0)


def slot_of(place_ref, block):
    core = block // 16
    return (
        ((core + 2 - place_ref[0]) % 2) * 16
        + (((block // 4) % 4 + 4 - place_ref[1 + core]) % 4) * 4
        + (block % 4 + 4 - place_ref[2 + core]) % 4
    )


def slot_from(place_ref, block):
    core = block // 16
    return (
        ((place_ref[0] + 2 - core) % 2) * 16
        + ((place_ref[1 + core] + 4 - (block // 4) % 4) % 4) * 4
        + (place_ref[2 + core] + 4 - block % 4) % 4
    )


def window_rows(window):
    return pl.ds(pl.multiple_of(window * WT, 16), WT)


def softmax_first(scores):
    top = jnp.max(scores, 0, keepdims=True)
    exponent = jnp.exp(scores - top)
    total = jnp.sum(exponent, 0, keepdims=True)
    return (exponent * (1.0 / total)).astype(BF16)


def head_masks():
    lane = lax.broadcasted_iota(jnp.int32, (1, 128), 1)
    first = lane < 64
    row = lax.broadcasted_iota(jnp.int32, (128, D), 0) // 16
    column = lax.broadcasted_iota(jnp.int32, (128, D), 1) // 64
    halves = (first.astype(F32).astype(BF16), (lane >= 64).astype(F32).astype(BF16))
    return first, halves, (row == column).astype(F32)


def tiled(block):
    return jnp.concatenate([block] * HEADS, 0)


def pair_of(head):
    return slice(head // 2 * 128, head // 2 * 128 + 128)


def tail_sum(block, tail):
    return jnp.sum((block * tail).reshape(HEADS, 16, D), 0)


def attention_kernel(
    tok, tok_lon, tok_lat, tok_both, w_qkv, pair_bias, mask, gain_one,
    xw, mix, act_t, qkv_out, probs_out,
    line, wide, act, qkv, probs, bias, sent,
):
    gather_windows(tok, tok_lon, tok_lat, tok_both, line, wide, xw)

    def norm_one(window, _):
        rows = window_rows(window)
        values, _ = stats_of(xw[rows].astype(F32))
        act[rows] = (values * gain_one[...]).astype(BF16)
        return 0

    lax.fori_loop(0, WINDOWS, norm_one, 0)

    def project(n, _):
        cols = pl.ds(pl.multiple_of(n * 256, 256), 256)
        qkv[:, cols] = mm(act[...], w_qkv[:, cols]).astype(BF16)
        return 0

    lax.fori_loop(0, QKV // 256, project, 0)
    copies = [pltpu.make_async_copy(qkv, qkv_out, sent.at[WINDOWS])]
    copies[0].start()
    act_t[...] = act[...].T

    mask_main = mask[:, 0:128]
    mask_tail = tiled(mask[128:WT]).T
    for head in range(HEADS):
        block = pair_bias[head, 0:128].T
        bias[0, head] = block
        bias[1, head] = block + mask_main
    block = jnp.concatenate([pair_bias[head, 128:WT] for head in range(HEADS)], 0).T
    bias[0, HEADS] = block
    bias[1, HEADS] = block + mask_tail

    first, halves, tail = head_masks()
    halves = [half * 0.125 for half in halves]
    tail_low = (tail * 0.125).astype(BF16)

    def attend(group, _):
        windows = [group * G_FORWARD + i for i in range(G_FORWARD)]
        heads = [(i, head) for i in range(G_FORWARD) for head in range(HEADS)]
        rows = [window_rows(window) for window in windows]
        main = [pl.ds(pl.multiple_of(window * WT, 16), 128) for window in windows]
        last = [pl.ds(pl.multiple_of(window * WT + 128, 16), 16) for window in windows]
        key = [qkv[r, D : 2 * D] for r in rows]
        val = [qkv[r, 2 * D : 3 * D] for r in rows]
        tail_scores = [
            mm(k, tiled(qkv[r, 0:D]) * tail_low, NT) for k, r in zip(key, last)
        ]
        scores = [
            mm(key[i][:, pair_of(head)], qkv[main[i], pair_of(head)] * halves[head % 2], NT)
            for i, head in heads
        ]
        tail_weights = [
            softmax_first(t + bias[window // 4, HEADS]) for t, window in zip(tail_scores, windows)
        ]
        weights = [
            softmax_first(t + bias[windows[i] // 4, head]) for t, (i, head) in zip(scores, heads)
        ]
        tail_mixed = [mm(w, v, TN) for w, v in zip(tail_weights, val)]
        mixed = [mm(w, val[i][:, pair_of(head)], TN) for w, (i, head) in zip(weights, heads)]
        for i, window in enumerate(windows):
            probs[window, HEADS] = tail_weights[i]
            mix[last[i]] = tail_sum(tail_mixed[i], tail).astype(BF16)
        for w, (i, head) in zip(weights, heads):
            probs[windows[i], head] = w
        for n, (i, head) in enumerate(heads):
            if head % 2 == 0:
                mix[main[i], pair_of(head)] = jnp.where(first, mixed[n], mixed[n + 1]).astype(BF16)
        for window in windows:
            pltpu.make_async_copy(probs.at[window], probs_out.at[window], sent.at[window]).start()
        return 0

    lax.fori_loop(0, WINDOWS // G_FORWARD, attend, 0)
    copies[0].wait()
    for window in range(WINDOWS):
        pltpu.make_async_copy(probs.at[window], probs_out.at[window], sent.at[window]).wait()


def mlp_kernel(
    place_ref, xw, mix, cot, cot_lon, cot_lat, cot_both, w_proj, w_up_in, w_down_in, gain_two,
    grad_mixed, grad_res, sums_out, sum_proj, sum_gain,
    line, wide, cotw, act, normed, inv_two, act_t, activated, grad_hidden, sums, w_up, w_down,
    got, sent,
):
    loads = [
        pltpu.make_async_copy(w_up_in, w_up, got.at[0]),
        pltpu.make_async_copy(w_down_in, w_down, got.at[1]),
    ]
    for load in loads:
        load.start()
    gather_windows(cot, cot_lon, cot_lat, cot_both, line, wide, cotw)

    def norm_two(part, _):
        rows = pl.ds(pl.multiple_of(part * M_NORM, 16), M_NORM)
        residual = xw[rows].astype(F32) + mm(mix[rows], w_proj[...])
        values, inv_std = stats_of(residual)
        normed[rows] = values
        inv_two[rows] = inv_std
        act[rows] = (values * gain_two[...]).astype(BF16)
        return 0

    lax.fori_loop(0, ROWS // M_NORM, norm_two, 0)
    act_t[...] = act[...].T
    for load in loads:
        load.wait()

    c0 = 0.7978845608028654
    c1 = c0 * 0.044715

    def mlp(f, _):
        cols = pl.ds(pl.multiple_of(f * F_STEP, F_STEP), F_STEP)

        def rows_of(r, _):
            rows = pl.ds(pl.multiple_of(r * M_UP, 16), M_UP)
            u = mm(act[rows], w_up[:, cols])
            grad_act = mm(cotw[rows], w_down[cols, :], NT)
            square = u * u
            gate = 0.5 + 0.5 * jnp.tanh(u * (c0 + c1 * square))
            value = u * gate
            activated[rows] = value.astype(BF16)
            slope = gate + value * (1.0 - gate) * (2.0 * c0 + 6.0 * c1 * square)
            grad_hidden[rows, cols] = (grad_act * slope).astype(BF16)
            return 0

        lax.fori_loop(0, ROWS // M_UP, rows_of, 0)
        blocks = F_STEP // 128
        up = mm(act_t[...], grad_hidden[:, cols]).astype(BF16)
        for j in range(blocks):
            sums[f * blocks + j] = up[:, 128 * j : 128 * j + 128]
        down = mm(activated[...], cotw[...], TN).astype(BF16)
        at = pl.ds(pl.multiple_of(f % (512 // F_STEP) * F_STEP, F_STEP), F_STEP)
        for j in range(4):
            sums[16 + f // (512 // F_STEP) * 4 + j, at] = down[:, 128 * j : 128 * j + 128]
        return 0

    lax.fori_loop(0, FF // F_STEP, mlp, 0)

    def send(piece):
        return pltpu.make_async_copy(
            sums.at[piece], sums_out.at[slot_of(place_ref, piece)], sent.at[piece]
        )

    for piece in range(PIECES):
        send(piece).start()

    def back(part, total):
        rows = pl.ds(pl.multiple_of(part * M_BACK, 16), M_BACK)
        grads = mm(grad_hidden[rows], w_up[...], NT)
        values = normed[rows]
        total = total + jnp.sum(grads * values, 0, keepdims=True)
        residual = cotw[rows].astype(F32) + back_of(grads, gain_two[...], values, inv_two[rows])
        grad_res[rows] = residual
        low = residual.astype(BF16)
        act[rows] = low
        grad_mixed[rows] = mm(low, w_proj[...], NT).astype(BF16)
        return total

    sum_gain[...] = lax.fori_loop(0, ROWS // M_BACK, back, jnp.zeros((1, D), F32))
    proj = mm(mix[...], act[...], TN).astype(BF16)
    for j in range(4):
        sum_proj[j] = proj[:, 128 * j : 128 * j + 128]
    for piece in range(PIECES):
        send(piece).wait()


def window_back_kernel(
    place_ref, qkv, probs, grad_mixed, act_t, sum_proj, sum_gain_two,
    grad_qkv, sums_two,
    grads_all, bias, flat,
):
    step = pl.program_id(0)
    first, halves, tail = head_masks()
    tail_low = tail.astype(BF16)

    @pl.when(step == 0)
    def _():
        bias[...] = jnp.zeros_like(bias)

    group = range(G_BACKWARD)
    heads = [(i, head) for i in group for head in range(HEADS)]
    rows = [slice(i * WT, i * WT + WT) for i in group]
    main = [slice(i * WT, i * WT + 128) for i in group]
    last = [slice(i * WT + 128, i * WT + WT) for i in group]
    key = [qkv[r, D : 2 * D] for r in rows]
    val = [qkv[r, 2 * D : 3 * D] for r in rows]
    query_tail = [tiled(qkv[r, 0:D]) * tail_low for r in last]
    out_tail = [tiled(grad_mixed[r]) * tail_low for r in last]
    query = [qkv[main[i], pair_of(head)] * halves[head % 2] for i, head in heads]
    out = [grad_mixed[main[i], pair_of(head)] * halves[head % 2] for i, head in heads]

    tail_probs = [mm(v, o, NT) for v, o in zip(val, out_tail)]
    grad_probs = [mm(val[i][:, pair_of(head)], o, NT) for o, (i, head) in zip(out, heads)]

    def score_grads(low_probs, grad_probs):
        weights = low_probs.astype(F32)
        product = grad_probs * weights
        return product - weights * jnp.sum(product, 0, keepdims=True)

    tail_low_probs = [probs[i, HEADS] for i in group]
    low_probs = [probs[i, head] for i, head in heads]
    tail_grads = [score_grads(p, g) for p, g in zip(tail_low_probs, tail_probs)]
    grads = [score_grads(p, g) for p, g in zip(low_probs, grad_probs)]
    bias[HEADS] += sum(tail_grads[1:], tail_grads[0])
    for head in range(HEADS):
        mine = grads[head::HEADS]
        bias[head] += sum(mine[1:], mine[0])
    tail_grads = [g.astype(BF16) for g in tail_grads]
    grads = [g.astype(BF16) for g in grads]

    query_last = [mm(g, k, TN) for g, k in zip(tail_grads, key)]
    key_more = [mm(g, q) for g, q in zip(tail_grads, query_tail)]
    val_more = [mm(p, o) for p, o in zip(tail_low_probs, out_tail)]
    query_parts = [mm(g, key[i][:, pair_of(head)], TN) for g, (i, head) in zip(grads, heads)]
    key_parts = [mm(g, q) for g, q in zip(grads, query)]
    val_parts = [mm(p, o) for p, o in zip(low_probs, out)]
    for i in group:
        grad_qkv[last[i], 0:D] = (tail_sum(query_last[i], tail) * 0.125).astype(BF16)
    for n, (i, head) in enumerate(heads):
        if head % 2:
            continue
        cols = pair_of(head)
        at = head // 2 * 128
        part = jnp.where(first, query_parts[n], query_parts[n + 1]) * 0.125
        grad_qkv[main[i], cols] = part.astype(BF16)
        part = (key_parts[n] + key_parts[n + 1] + key_more[i][:, cols]) * 0.125
        grad_qkv[rows[i], D + at : D + at + 128] = part.astype(BF16)
        part = val_parts[n] + val_parts[n + 1] + val_more[i][:, cols]
        grad_qkv[rows[i], 2 * D + at : 2 * D + at + 128] = part.astype(BF16)
    size = G_BACKWARD * WT
    grads_all[pl.ds(pl.multiple_of(step * size, 16), size)] = grad_qkv[...]

    @pl.when(step == WINDOWS // G_BACKWARD - 1)
    def _():
        def weights(n, _):
            cols = pl.ds(pl.multiple_of(n * 256, 256), 256)
            part = mm(act_t[...], grads_all[:, cols]).astype(BF16)
            for j in range(2):
                at = pl.multiple_of((n * 2 + j) * 512, 512)
                flat[pl.ds(at, 512)] = part[:, 128 * j : 128 * j + 128]
            return 0

        lax.fori_loop(0, QKV // 256, weights, 0)
        for j in range(4):
            flat[PROJ_AT + 512 * j : PROJ_AT + 512 * j + 512] = sum_proj[j]
        for block in range(HEADS + 1):
            at = BIAS_AT + WT * block
            flat[at : at + WT] = bias[block].astype(BF16)
        gains = [sum_gain_two[:, 128 * j : 128 * j + 128] for j in range(4)]
        gains = jnp.concatenate(gains + [jnp.zeros((12, 128), F32)], 0)
        flat[GAIN_AT : GAIN_AT + 16] = gains.astype(BF16)
        flat[GAIN_AT + 16 :] = jnp.zeros((TWO_TOTAL - GAIN_AT - 16, 128), BF16)
        for piece in range(PIECES):
            sums_two[slot_of(place_ref, piece)] = flat[piece * TWO_ROWS : (piece + 1) * TWO_ROWS]


def branch_kernel(xw, grad_qkv, grad_res, w_qkv, gain_one, grad_grid, wide, line):
    def branch(part, _):
        rows = pl.ds(pl.multiple_of(part * M_BRANCH, 16), M_BRANCH)
        values, inv_std = stats_of(xw[rows].astype(F32))
        grads = mm(grad_qkv[rows], w_qkv[...], NT)
        low = back_of(grads, gain_one[...], values, inv_std).astype(BF16)
        wide[rows] = grad_res[rows] + low.astype(F32)
        return 0

    lax.fori_loop(0, ROWS // M_BRANCH, branch, 0)
    for level in range(LEVELS):
        for row in range(HEIGHT):
            for column in range(4):
                at = run_at(level, row, column)
                line[WLON * column : WLON * column + WLON] = wide[at : at + WLON]
            grad_grid[level, row] = line[0:BREADTH].astype(BF16)


def finish_one_kernel(scale, place_ref, up_in, down_in, up_out, down_out):
    up_out[...] = up_in[0].astype(F32) * scale
    down_out[...] = down_in[0].astype(F32) * scale


def finish_two_kernel(
    scale, place_ref, sums, w_qkv, gain_vec, qkv, proj, bias, gain_one, gain_two, flat, arrived
):
    copies = []
    for piece in range(PIECES):
        copy = pltpu.make_async_copy(
            sums.at[slot_from(place_ref, piece), pl.ds(ONE_ROWS, TWO_ROWS)],
            flat.at[pl.ds(piece * TWO_ROWS, TWO_ROWS)],
            arrived.at[piece],
        )
        copy.start()
        copies.append(copy)
    for copy in copies:
        copy.wait()
    total = jnp.zeros((D, 128), F32)
    for j in range(12):
        cols = slice(128 * j, 128 * j + 128)
        part = flat[512 * j : 512 * j + 512].astype(F32) * scale
        qkv[:, cols] = part
        total = total + part * w_qkv[:, cols].astype(F32)
    gain_one[...] = jnp.sum(total.T, 0, keepdims=True) / gain_vec[...]
    for j in range(4):
        at = PROJ_AT + 512 * j
        proj[:, 128 * j : 128 * j + 128] = flat[at : at + 512].astype(F32) * scale
    for head in range(HEADS):
        at = BIAS_AT + WT * head
        bias[head, 0:128] = flat[at : at + WT].astype(F32).T * (scale * WT)
    rest = flat[REST_AT : REST_AT + WT].astype(F32).T * (scale * WT)
    for head in range(HEADS):
        bias[head, 128:WT] = rest[16 * head : 16 * head + 16]
    gains = flat[GAIN_AT : GAIN_AT + 16].astype(F32) * scale
    for j in range(4):
        gain_two[:, 128 * j : 128 * j + 128] = gains[j : j + 1]


def shape(*dims, dtype=BF16):
    return jax.ShapeDtypeStruct(dims, dtype)


def params():
    return pltpu.CompilerParams(vmem_limit_bytes=VMEM_LIMIT)


def vmem(*dims, dtype=BF16):
    return pltpu.VMEM(dims, dtype)


def cost(flops, moved):
    return pl.CostEstimate(flops=flops, bytes_accessed=moved, transcendentals=0)


ANY = pl.BlockSpec(memory_space=pl.ANY)
INSIDE = pl.BlockSpec(memory_space=pltpu.VMEM)
SCALARS = pl.BlockSpec(memory_space=pltpu.SMEM)


def attention(*operands):
    return pl.pallas_call(
        attention_kernel,
        out_shape=(
            shape(ROWS, D), shape(ROWS, D), shape(D, ROWS), shape(ROWS, QKV),
            shape(WINDOWS, HEADS + 1, WT, 128),
        ),
        in_specs=[INSIDE] * len(operands),
        out_specs=[INSIDE, INSIDE, INSIDE, ANY, ANY],
        scratch_shapes=[
            vmem(56, D, dtype=F32), vmem(ROWS, D, dtype=F32), vmem(ROWS, D), vmem(ROWS, QKV),
            vmem(WINDOWS, HEADS + 1, WT, 128), vmem(2, HEADS + 1, WT, 128, dtype=F32),
            pltpu.SemaphoreType.DMA((WINDOWS + 1,)),
        ],
        compiler_params=params(),
        cost_estimate=cost(ROWS * D * QKV * 2 * 4, 20_000_000),
        name="attention",
    )(*operands)


def mlp_call(*operands):
    return pl.pallas_call(
        mlp_kernel,
        out_shape=(
            shape(ROWS, D), shape(ROWS, D, dtype=F32), shape(PIECES, ONE_ROWS, 128),
            shape(4, 512, 128), shape(1, D, dtype=F32),
        ),
        in_specs=[SCALARS] + [INSIDE] * 7 + [ANY, ANY, INSIDE],
        out_specs=[INSIDE, INSIDE, ANY, INSIDE, INSIDE],
        scratch_shapes=[
            vmem(56, D, dtype=F32), vmem(ROWS, D, dtype=F32), vmem(ROWS, D), vmem(ROWS, D),
            vmem(ROWS, D, dtype=F32), vmem(ROWS, 1, dtype=F32), vmem(D, ROWS),
            vmem(ROWS, F_STEP), vmem(ROWS, FF), vmem(PIECES, ONE_ROWS, 128),
            vmem(D, FF), vmem(FF, D),
            pltpu.SemaphoreType.DMA((2,)), pltpu.SemaphoreType.DMA((PIECES,)),
        ],
        compiler_params=params(),
        cost_estimate=cost(ROWS * D * FF * 2 * 8, 40_000_000),
        name="mlp",
    )(*operands)


def window_back(place, qkv, probs, grad_mixed, act_t, sum_proj, sum_gain_two):
    return pl.pallas_call(
        window_back_kernel,
        out_shape=(shape(ROWS, QKV), shape(PIECES, TWO_ROWS, 128)),
        grid=(WINDOWS // G_BACKWARD,),
        in_specs=[
            SCALARS,
            pl.BlockSpec((G_BACKWARD * WT, QKV), lambda i: (i, 0)),
            pl.BlockSpec((G_BACKWARD, HEADS + 1, WT, 128), lambda i: (i, 0, 0, 0)),
            pl.BlockSpec((G_BACKWARD * WT, D), lambda i: (i, 0)),
            INSIDE, INSIDE, INSIDE,
        ],
        out_specs=[pl.BlockSpec((G_BACKWARD * WT, QKV), lambda i: (i, 0)), INSIDE],
        scratch_shapes=[
            vmem(ROWS, QKV), vmem(HEADS + 1, WT, 128, dtype=F32), vmem(TWO_TOTAL, 128),
        ],
        compiler_params=params(),
        cost_estimate=cost(ROWS * D * QKV * 2 * 6, 20_000_000),
        name="window_back",
    )(place, qkv, probs, grad_mixed, act_t, sum_proj, sum_gain_two)


def branch(*operands):
    return pl.pallas_call(
        branch_kernel,
        out_shape=shape(LEVELS, HEIGHT, BREADTH, D),
        in_specs=[INSIDE] * len(operands),
        out_specs=INSIDE,
        scratch_shapes=[vmem(ROWS, D, dtype=F32), vmem(48, D, dtype=F32)],
        compiler_params=params(),
        cost_estimate=cost(ROWS * D * QKV * 2 * 4, 10_000_000),
        name="branch",
    )(*operands)


def finish_one(place, sums, scale):
    return pl.pallas_call(
        functools.partial(finish_one_kernel, scale),
        out_shape=(shape(D, FF, dtype=F32), shape(FF, D, dtype=F32)),
        grid_spec=pltpu.PrefetchScalarGridSpec(
            num_scalar_prefetch=1,
            grid=(16,),
            in_specs=[
                pl.BlockSpec((1, 512, 128), lambda i, place: (slot_from(place, i), 0, 0)),
                pl.BlockSpec((1, 512, 128), lambda i, place: (slot_from(place, i + 16), 0, 0)),
            ],
            out_specs=[
                pl.BlockSpec((512, 128), lambda i, place: (0, i)),
                pl.BlockSpec((512, 128), lambda i, place: (i // 4, i % 4)),
            ],
        ),
        compiler_params=params(),
        name="finish_mlp",
    )(place, sums, sums)


def finish_two(place, sums, w_qkv, gain_one, scale):
    return pl.pallas_call(
        functools.partial(finish_two_kernel, scale),
        out_shape=(
            shape(D, QKV, dtype=F32), shape(D, D, dtype=F32), shape(HEADS, WT, WT, dtype=F32),
            shape(1, D, dtype=F32), shape(1, D, dtype=F32),
        ),
        in_specs=[SCALARS, ANY, INSIDE, INSIDE],
        scratch_shapes=[
            pltpu.VMEM((TWO_TOTAL, 128), BF16),
            pltpu.SemaphoreType.DMA((PIECES,)),
        ],
        compiler_params=params(),
        name="finish_attention",
    )(place, sums, w_qkv, gain_one)


def neighbour(array, lat_by, lon_by):
    lat_count, lon_count = lax.axis_size("lat"), lax.axis_size("lon")
    pairs = []
    for i in range(lat_count):
        for j in range(lon_count):
            to = ((i + lat_by) % lat_count) * lon_count + (j + lon_by) % lon_count
            pairs.append((i * lon_count + j, to))
    return lax.ppermute(array, ("lat", "lon"), pairs)


def halos(tensor):
    edge, top = WLON // 2, WLAT // 2
    return (
        neighbour(tensor[:, :, :edge], 0, -1),
        neighbour(tensor[:, :top], -1, 0),
        neighbour(tensor[:, :top, :edge], -1, -1),
    )


def bring_home(grid):
    edge, top = WLON // 2, WLAT // 2
    from_lon = neighbour(grid[:, :-top, -edge:], 0, 1)
    from_lat = neighbour(grid[:, -top:, :-edge], 1, 0)
    from_both = neighbour(grid[:, -top:, -edge:], 1, 1)
    upper = jnp.concatenate([from_both, from_lat], 2)
    lower = jnp.concatenate([from_lon, grid[:, :-top, :-edge]], 2)
    return jnp.concatenate([upper, lower], 1)


def position(lat, lon):
    return lat % 2, (lon // 2, (lat // 2) % 2 * 2 + lon % 2, lat // 4)


ORDERS = ((0, 1, 2), (1, 2, 0))


def place_of():
    core, chip = position(lax.axis_index("lat"), lax.axis_index("lon"))
    return jnp.stack([core, *chip]).astype(jnp.int32)


def along(array, stage, by):
    pairs = []
    for lat in range(16):
        for lon in range(8):
            core, chip = position(lat, lon)
            chip = list(chip)
            axis = ORDERS[core][stage]
            chip[axis] = (chip[axis] + by) % 4
            x, y, z = chip
            to = (z * 4 + y // 2 * 2 + core) * 8 + x * 2 + y % 2
            pairs.append((lat * 8 + lon, to))
    return lax.ppermute(array, ("lat", "lon"), pairs)


def other_core(array):
    return lax.ppermute(array, "lat", [(i, i ^ 1) for i in range(16)])


def added(*terms):
    total = terms[0].astype(F32)
    for term in terms[1:]:
        total = total + term.astype(F32)
    return total.astype(BF16)


def scatter_sum(sums):
    held = added(sums[:16], other_core(sums[16:]))
    held = added(held[:4], *[along(held[4 * k : 4 * k + 4], 0, k) for k in (1, 2, 3)])
    return added(held[0], *[along(held[k], 1, k) for k in (1, 2, 3)])


def all_sum(sums_one, sums_two):
    share = jnp.concatenate([scatter_sum(sums_one), scatter_sum(sums_two)], 0)
    share = lax.optimization_barrier(share)
    one, two, three = [along(share, 2, k).astype(F32) for k in (1, 2, 3)]
    share = ((share.astype(F32) + two) + (one + three)).astype(BF16)
    held = jnp.stack([share] + [along(share, 1, k) for k in (1, 2, 3)])
    held = jnp.concatenate([held] + [along(held, 0, k) for k in (1, 2, 3)])
    return jnp.concatenate([held, other_core(held)])


def local(tokens, cotangent, w_qkv, w_proj, w_up, w_down, pair_bias, gain_one, gain_two):
    total_tokens = ROWS * lax.axis_size("lat") * lax.axis_size("lon")
    scale = total_tokens ** (-0.5)
    place = place_of()
    token = jnp.arange(WT, dtype=jnp.int32)
    lower = (token // WLON) % WLAT >= WLAT // 2
    apart = (lower[:, None] != lower[None, :]) & (
        lax.axis_index("lat") == lax.axis_size("lat") - 1
    )
    mask = jnp.where(apart, MASKED, 0.0).astype(F32)
    gain_one = gain_one.reshape(1, D)
    gain_two = gain_two.reshape(1, D)
    xw, mix, act_t, qkv, probs = attention(
        tokens, *halos(tokens), w_qkv, pair_bias, mask, gain_one
    )
    grad_mixed, grad_res, sums_one, sum_proj, sum_gain_two = mlp_call(
        place, xw, mix, cotangent, *halos(cotangent), w_proj, w_up, w_down, gain_two
    )
    grad_qkv, sums_two = window_back(
        place, qkv, probs, grad_mixed, act_t, sum_proj, sum_gain_two
    )
    grad_tokens = bring_home(branch(xw, grad_qkv, grad_res, w_qkv, gain_one))
    sums = all_sum(sums_one, sums_two)
    sum_up, sum_down = finish_one(place, sums, scale)
    sum_qkv, sum_proj, sum_bias, sum_one, sum_two = finish_two(
        place, sums, w_qkv, gain_one, scale
    )
    return (
        grad_tokens,
        sum_qkv,
        sum_proj,
        sum_up,
        sum_down,
        sum_bias,
        sum_one.reshape(D),
        sum_two.reshape(D),
    )


def solution(mesh):
    grid = P(None, "lat", "lon", None)
    in_specs = (grid, grid, P(), P(), P(), P(), P(), P(), P())
    out_specs = (grid, P(), P(), P(), P(), P(), P(), P())
    return jax.shard_map(local, mesh=mesh, in_specs=in_specs, out_specs=out_specs, check_vma=False)
```

```python
import functools

import jax
import jax.numpy as jnp
from jax import lax
from jax.experimental import pallas as pl
from jax.experimental.pallas import tpu as pltpu
from jax.sharding import PartitionSpec as P

HEADS = 8
WLAT = 6
WLON = 12
WT = 144
D = 512
QKV = 1536
FF = 2048
LEVELS = 2
HEIGHT = 12
BREADTH = 48
WINDOWS = 8
ROWS = WINDOWS * WT
EPSILON = 1e-05
MASKED = -1e30
F32 = jnp.float32
BF16 = jnp.bfloat16
PIECES = 32
BAND_ROWS = 512
PROJ_ROWS = 64
ONE_ROWS = BAND_ROWS + PROJ_ROWS
QKV_ROWS = 192
REST_ROWS = 48
TWO_ROWS = QKV_ROWS + REST_ROWS
ALL_ROWS = ONE_ROWS + TWO_ROWS
GAIN_AT = (HEADS + 1) * WT
MIB = 1024 * 1024
M_NORM = 576
M_UP = 1152
M_BACK = 576
M_BRANCH = 576
G_FORWARD = 4
G_BACKWARD = 2
F_STEP = 512

NN = (((1,), (0,)), ((), ()))
NT = (((1,), (1,)), ((), ()))
TN = (((0,), (0,)), ((), ()))


def mm(a, b, dims=NN):
    return lax.dot_general(a, b, dims, preferred_element_type=F32)


def stats_of(values):
    average = jnp.mean(values, -1, keepdims=True)
    centred = values - average
    variance = jnp.mean(centred * centred, -1, keepdims=True)
    inv_std = lax.rsqrt(variance + EPSILON)
    return centred * inv_std, inv_std


def back_of(grad_out, gain_vec, normed, inv_std):
    scaled = grad_out * gain_vec
    return (
        scaled
        - jnp.mean(scaled, -1, keepdims=True)
        - normed * jnp.mean(scaled * normed, -1, keepdims=True)
    ) * inv_std


def run_at(level, row, column):
    window = (row // WLAT) * 4 + column
    return window * WT + level * (WT // 2) + (row % WLAT) * WLON


def gather_windows(main_ref, lon_ref, lat_ref, both_ref, which, line, wide, out_ref):
    for level in range(LEVELS):
        for row in range(HEIGHT):
            if row < HEIGHT - WLAT // 2:
                line[0:BREADTH] = main_ref[level, row + WLAT // 2].astype(F32)
                line[BREADTH : BREADTH + 6] = lon_ref[which, level, row + WLAT // 2].astype(F32)
            else:
                line[0:BREADTH] = lat_ref[which, level, row - (HEIGHT - WLAT // 2)].astype(F32)
                line[BREADTH : BREADTH + 6] = both_ref[which, level, row - (HEIGHT - WLAT // 2)].astype(F32)
            for column in range(4):
                at = run_at(level, row, column)
                wide[at : at + WLON] = line[6 + WLON * column : 18 + WLON * column]

    def narrow(window, _):
        rows = pl.ds(pl.multiple_of(window * WT, 16), WT)
        out_ref[rows] = wide[rows].astype(BF16)
        return 0

    lax.fori_loop(0, WINDOWS, narrow, 0)


def position(lat, lon):
    return lat % 2, (lon // 2, (lat // 2) % 2 * 2 + lon % 2, lat // 4)


ORDERS = ((0, 1, 2), (1, 2, 0))


def here():
    return position(lax.axis_index("lat"), lax.axis_index("lon"))


def slot_of(core, block):
    _, chip = here()
    first, second = chip[ORDERS[core][0]], chip[ORDERS[core][1]]
    return (block // 4 + 4 - first) % 4 * 4 + (block % 4 + 4 - second) % 4


def block_at(core, first_by, second_by):
    _, chip = here()
    first = jnp.where(core == 0, chip[ORDERS[0][0]], chip[ORDERS[1][0]])
    second = jnp.where(core == 0, chip[ORDERS[0][1]], chip[ORDERS[1][1]])
    return (first + 4 - first_by) % 4 * 4 + (second + 4 - second_by) % 4


def window_rows(window):
    return pl.ds(pl.multiple_of(window * WT, 16), WT)


def softmax_first(scores):
    top = jnp.max(scores, 0, keepdims=True)
    exponent = jnp.exp(scores - top)
    total = jnp.sum(exponent, 0, keepdims=True)
    return (exponent * (1.0 / total)).astype(BF16)


def head_masks():
    lane = lax.broadcasted_iota(jnp.int32, (1, 128), 1)
    first = lane < 64
    row = lax.broadcasted_iota(jnp.int32, (128, D), 0) // 16
    column = lax.broadcasted_iota(jnp.int32, (128, D), 1) // 64
    halves = (first.astype(F32).astype(BF16), (lane >= 64).astype(F32).astype(BF16))
    return first, halves, (row == column).astype(F32)


def tiled(block):
    return jnp.concatenate([block] * HEADS, 0)


def pair_of(head):
    return slice(head // 2 * 128, head // 2 * 128 + 128)


def tail_sum(block, tail):
    return jnp.sum((block * tail).reshape(HEADS, 16, D), 0)


def pack_kernel(tok, cot, lon, lat, both):
    edge, top = WLON // 2, WLAT // 2
    for which, ref in enumerate((tok, cot)):
        lat[which] = ref[:, :top]
        for level in range(LEVELS):
            for row in range(HEIGHT):
                lon[which, level, row] = ref[level, row, :edge]
            for row in range(top):
                both[which, level, row] = ref[level, row, :edge]


def attention_kernel(
    tok, tok_lon, tok_lat, tok_both, w_qkv, pair_bias, gain_one,
    xw, mix, act_t, qkv_out, probs_out,
    line, wide, act, qkv, probs, bias, sent,
):
    gather_windows(tok, tok_lon, tok_lat, tok_both, 0, line, wide, xw)

    def norm_one(window, _):
        rows = window_rows(window)
        values, _ = stats_of(xw[rows].astype(F32))
        act[rows] = (values * gain_one[...]).astype(BF16)
        return 0

    lax.fori_loop(0, WINDOWS, norm_one, 0)

    def project(n, _):
        cols = pl.ds(pl.multiple_of(n * 256, 256), 256)
        qkv[:, cols] = mm(act[...], w_qkv[:, cols]).astype(BF16)
        return 0

    lax.fori_loop(0, QKV // 256, project, 0)
    copies = [pltpu.make_async_copy(qkv, qkv_out, sent.at[WINDOWS])]
    copies[0].start()
    act_t[...] = act[...].T

    is_last = lax.axis_index("lat") == lax.axis_size("lat") - 1
    key_at = lax.broadcasted_iota(jnp.int32, (WT, 128), 0)
    query_at = lax.broadcasted_iota(jnp.int32, (WT, 128), 1)

    def masked(query_at):
        apart = (key_at // WLON % WLAT >= WLAT // 2) != (query_at // WLON % WLAT >= WLAT // 2)
        return jnp.where(apart & is_last, MASKED, 0.0)

    mask_main = masked(query_at)
    mask_tail = masked(128 + query_at % 16)
    for head in range(HEADS):
        block = pair_bias[head, 0:128].T
        bias[0, head] = block
        bias[1, head] = block + mask_main
    block = jnp.concatenate([pair_bias[head, 128:WT] for head in range(HEADS)], 0).T
    bias[0, HEADS] = block
    bias[1, HEADS] = block + mask_tail

    first, halves, tail = head_masks()
    halves = [half * 0.125 for half in halves]
    tail_low = (tail * 0.125).astype(BF16)

    def attend(group, _):
        windows = [group * G_FORWARD + i for i in range(G_FORWARD)]
        heads = [(i, head) for i in range(G_FORWARD) for head in range(HEADS)]
        rows = [window_rows(window) for window in windows]
        main = [pl.ds(pl.multiple_of(window * WT, 16), 128) for window in windows]
        last = [pl.ds(pl.multiple_of(window * WT + 128, 16), 16) for window in windows]
        key = [qkv[r, D : 2 * D] for r in rows]
        val = [qkv[r, 2 * D : 3 * D] for r in rows]
        tail_scores = [
            mm(k, tiled(qkv[r, 0:D]) * tail_low, NT) for k, r in zip(key, last)
        ]
        scores = [
            mm(key[i][:, pair_of(head)], qkv[main[i], pair_of(head)] * halves[head % 2], NT)
            for i, head in heads
        ]
        tail_weights = [
            softmax_first(t + bias[window // 4, HEADS]) for t, window in zip(tail_scores, windows)
        ]
        weights = [
            softmax_first(t + bias[windows[i] // 4, head]) for t, (i, head) in zip(scores, heads)
        ]
        tail_mixed = [mm(w, v, TN) for w, v in zip(tail_weights, val)]
        mixed = [mm(w, val[i][:, pair_of(head)], TN) for w, (i, head) in zip(weights, heads)]
        for i, window in enumerate(windows):
            probs[window, HEADS] = tail_weights[i]
            mix[last[i]] = tail_sum(tail_mixed[i], tail).astype(BF16)
        for w, (i, head) in zip(weights, heads):
            probs[windows[i], head] = w
        for n, (i, head) in enumerate(heads):
            if head % 2 == 0:
                mix[main[i], pair_of(head)] = jnp.where(first, mixed[n], mixed[n + 1]).astype(BF16)
        for window in windows:
            pltpu.make_async_copy(probs.at[window], probs_out.at[window], sent.at[window]).start()
        return 0

    lax.fori_loop(0, WINDOWS // G_FORWARD, attend, 0)
    copies[0].wait()
    for window in range(WINDOWS):
        pltpu.make_async_copy(probs.at[window], probs_out.at[window], sent.at[window]).wait()


def mlp_kernel(
    xw, mix, cot, cot_lon, cot_lat, cot_both, w_proj, w_up_in, w_down_in, gain_two,
    grad_mixed, grad_res, keep_one, send_one, sum_gain,
    line, wide, cotw, act, normed, inv_two, act_t, activated, grad_hidden, sums, w_up, w_down,
    got, sent,
):
    loads = [
        pltpu.make_async_copy(w_up_in, w_up, got.at[0]),
        pltpu.make_async_copy(w_down_in, w_down, got.at[1]),
    ]
    for load in loads:
        load.start()
    gather_windows(cot, cot_lon, cot_lat, cot_both, 1, line, wide, cotw)

    def norm_two(part, _):
        rows = pl.ds(pl.multiple_of(part * M_NORM, 16), M_NORM)
        residual = xw[rows].astype(F32) + mm(mix[rows], w_proj[...])
        values, inv_std = stats_of(residual)
        normed[rows] = values
        inv_two[rows] = inv_std
        act[rows] = (values * gain_two[...]).astype(BF16)
        return 0

    lax.fori_loop(0, ROWS // M_NORM, norm_two, 0)
    act_t[...] = act[...].T
    for load in loads:
        load.wait()

    c0 = 0.7978845608028654
    c1 = c0 * 0.044715

    def mlp(f, _):
        cols = pl.ds(pl.multiple_of(f * F_STEP, F_STEP), F_STEP)

        def rows_of(r, _):
            rows = pl.ds(pl.multiple_of(r * M_UP, 16), M_UP)
            u = mm(act[rows], w_up[:, cols])
            grad_act = mm(cotw[rows], w_down[cols, :], NT)
            square = u * u
            gate = 0.5 + 0.5 * jnp.tanh(u * (c0 + c1 * square))
            value = u * gate
            activated[rows] = value.astype(BF16)
            slope = gate + value * (1.0 - gate) * (2.0 * c0 + 6.0 * c1 * square)
            grad_hidden[rows, cols] = (grad_act * slope).astype(BF16)
            return 0

        lax.fori_loop(0, ROWS // M_UP, rows_of, 0)
        up = mm(act_t[...], grad_hidden[:, cols]).astype(BF16)
        for j in range(4):
            at = pl.ds(pl.multiple_of(f * 128 + 32 * j, 32), 32)
            sums[0:16, at] = up[:, 128 * j : 128 * j + 128].reshape(16, 32, 128)
        down = mm(activated[...], cotw[...], TN).astype(BF16)
        for i in range(4):
            for j in range(4):
                part = down[128 * i : 128 * i + 128, 128 * j : 128 * j + 128]
                sums[16 + f * 4 + i, 128 * j : 128 * j + 128] = part
        return 0

    lax.fori_loop(0, FF // F_STEP, mlp, 0)

    core, _ = here()

    def send(rows, at, act_on):
        for owner in range(2):
            for block in range(16):
                piece = owner * 16 + block
                slot = slot_of(owner, block)

                def copy_to(out):
                    return pltpu.make_async_copy(
                        sums.at[piece, rows], out.at[slot, rows], sent.at[at, piece]
                    )

                @pl.when(core == owner)
                def _():
                    act_on(copy_to(keep_one))

                @pl.when(core != owner)
                def _():
                    act_on(copy_to(send_one))

    bands, tails = pl.ds(0, BAND_ROWS), pl.ds(BAND_ROWS, PROJ_ROWS)
    send(bands, 0, lambda copy: copy.start())

    def back(part, total):
        rows = pl.ds(pl.multiple_of(part * M_BACK, 16), M_BACK)
        grads = mm(grad_hidden[rows], w_up[...], NT)
        values = normed[rows]
        total = total + jnp.sum(grads * values, 0, keepdims=True)
        residual = cotw[rows].astype(F32) + back_of(grads, gain_two[...], values, inv_two[rows])
        grad_res[rows] = residual
        low = residual.astype(BF16)
        act[rows] = low
        grad_mixed[rows] = mm(low, w_proj[...], NT).astype(BF16)
        return total

    sum_gain[...] = lax.fori_loop(0, ROWS // M_BACK, back, jnp.zeros((1, D), F32))
    proj = mm(mix[...], act[...], TN).astype(BF16)
    for j in range(4):
        at = slice(BAND_ROWS + 16 * j, BAND_ROWS + 16 * j + 16)
        sums[:, at] = proj[:, 128 * j : 128 * j + 128].reshape(PIECES, 16, 128)
    send(tails, 1, lambda copy: copy.start())
    send(bands, 0, lambda copy: copy.wait())
    send(tails, 1, lambda copy: copy.wait())


def first_back_kernel(qkv, probs, grad_mixed, grad_qkv, bias):
    window_back(qkv, probs, grad_mixed, grad_qkv, bias, None)


def second_back_kernel(
    qkv, probs, grad_mixed, act_t, sum_gain_two, bias_before, grads_before,
    grad_qkv, keep_two, send_two,
    grads_all, bias, flat,
):
    step = pl.program_id(0)

    @pl.when(step == 0)
    def _():
        grads_all[0 : ROWS // 2] = grads_before[...]

    window_back(qkv, probs, grad_mixed, grad_qkv, bias, bias_before)
    size = G_BACKWARD * WT
    at = pl.multiple_of(ROWS // 2 + step * size, 16)
    grads_all[pl.ds(at, size)] = grad_qkv[...]

    @pl.when(step == WINDOWS // 2 // G_BACKWARD - 1)
    def _():
        for n in range(QKV // 512):
            part = mm(act_t[...], grads_all[:, 512 * n : 512 * n + 512]).astype(BF16)
            for j in range(4):
                at = (n * 4 + j) * 16
                flat[:, at : at + 16] = part[:, 128 * j : 128 * j + 128].reshape(PIECES, 16, 128)
        gains = [sum_gain_two[:, 128 * j : 128 * j + 128] for j in range(4)]
        gains = jnp.concatenate(gains + [jnp.zeros((12, 128), F32)], 0)
        rest = [bias[block].astype(BF16) for block in range(HEADS + 1)] + [gains.astype(BF16)]
        rest.append(jnp.zeros((PIECES * REST_ROWS - GAIN_AT - 16, 128), BF16))
        rest = jnp.concatenate(rest, 0)
        flat[:, QKV_ROWS:TWO_ROWS] = rest.reshape(PIECES, REST_ROWS, 128)
        core, _ = here()
        for owner in range(2):
            for block in range(16):
                slot = slot_of(owner, block)
                piece = flat[owner * 16 + block]

                @pl.when(core == owner)
                def _():
                    keep_two[slot] = piece

                @pl.when(core != owner)
                def _():
                    send_two[slot] = piece


def window_back(qkv, probs, grad_mixed, grad_qkv, bias, bias_before):
    step = pl.program_id(0)
    first, halves, tail = head_masks()
    tail_low = tail.astype(BF16)

    @pl.when(step == 0)
    def _():
        bias[...] = jnp.zeros_like(bias) if bias_before is None else bias_before[...]

    group = range(G_BACKWARD)
    heads = [(i, head) for i in group for head in range(HEADS)]
    rows = [slice(i * WT, i * WT + WT) for i in group]
    main = [slice(i * WT, i * WT + 128) for i in group]
    last = [slice(i * WT + 128, i * WT + WT) for i in group]
    key = [qkv[r, D : 2 * D] for r in rows]
    val = [qkv[r, 2 * D : 3 * D] for r in rows]
    query_tail = [tiled(qkv[r, 0:D]) * tail_low for r in last]
    out_tail = [tiled(grad_mixed[r]) * tail_low for r in last]
    query = [qkv[main[i], pair_of(head)] * halves[head % 2] for i, head in heads]
    out = [grad_mixed[main[i], pair_of(head)] * halves[head % 2] for i, head in heads]

    tail_probs = [mm(v, o, NT) for v, o in zip(val, out_tail)]
    grad_probs = [mm(val[i][:, pair_of(head)], o, NT) for o, (i, head) in zip(out, heads)]

    def score_grads(low_probs, grad_probs):
        weights = low_probs.astype(F32)
        product = grad_probs * weights
        return product - weights * jnp.sum(product, 0, keepdims=True)

    tail_low_probs = [probs[i, HEADS] for i in group]
    low_probs = [probs[i, head] for i, head in heads]
    tail_grads = [score_grads(p, g) for p, g in zip(tail_low_probs, tail_probs)]
    grads = [score_grads(p, g) for p, g in zip(low_probs, grad_probs)]
    bias[HEADS] += sum(tail_grads[1:], tail_grads[0])
    for head in range(HEADS):
        mine = grads[head::HEADS]
        bias[head] += sum(mine[1:], mine[0])
    tail_grads = [g.astype(BF16) for g in tail_grads]
    grads = [g.astype(BF16) for g in grads]

    query_last = [mm(g, k, TN) for g, k in zip(tail_grads, key)]
    key_more = [mm(g, q) for g, q in zip(tail_grads, query_tail)]
    val_more = [mm(p, o) for p, o in zip(tail_low_probs, out_tail)]
    query_parts = [mm(g, key[i][:, pair_of(head)], TN) for g, (i, head) in zip(grads, heads)]
    key_parts = [mm(g, q) for g, q in zip(grads, query)]
    val_parts = [mm(p, o) for p, o in zip(low_probs, out)]
    for i in group:
        grad_qkv[last[i], 0:D] = (tail_sum(query_last[i], tail) * 0.125).astype(BF16)
    for n, (i, head) in enumerate(heads):
        if head % 2:
            continue
        cols = pair_of(head)
        at = head // 2 * 128
        part = jnp.where(first, query_parts[n], query_parts[n + 1]) * 0.125
        grad_qkv[main[i], cols] = part.astype(BF16)
        part = (key_parts[n] + key_parts[n + 1] + key_more[i][:, cols]) * 0.125
        grad_qkv[rows[i], D + at : D + at + 128] = part.astype(BF16)
        part = val_parts[n] + val_parts[n + 1] + val_more[i][:, cols]
        grad_qkv[rows[i], 2 * D + at : 2 * D + at + 128] = part.astype(BF16)

def branch_kernel(xw, grads_first, grads_second, grad_res, w_qkv, gain_one, main, lon, lat, both, wide, line):
    for part, grad_qkv in enumerate((grads_first, grads_second)):
        rows = slice(part * ROWS // 2, (part + 1) * ROWS // 2)
        values, inv_std = stats_of(xw[rows].astype(F32))
        grads = mm(grad_qkv[...], w_qkv[...], NT)
        low = back_of(grads, gain_one[...], values, inv_std).astype(BF16)
        wide[rows] = grad_res[rows] + low.astype(F32)

    for level in range(LEVELS):
        for row in range(HEIGHT):
            for column in range(4):
                at = run_at(level, row, column)
                line[WLON * column : WLON * column + WLON] = wide[at : at + WLON]
            inner, outer = (main, lon) if row < HEIGHT - WLAT // 2 else (lat, both)
            at = row if row < HEIGHT - WLAT // 2 else row - (HEIGHT - WLAT // 2)
            inner[level, at] = line[0 : BREADTH - 6].astype(BF16)
            outer[level, at] = line[BREADTH - 6 : BREADTH].astype(BF16)


def write_bands(scale, owner, pieces, up_out, down_out, buffer_up, buffer_down, sent):
    depth = buffer_up.shape[0]

    def run(buffer, rows, fill, out):
        def copy(n, block):
            at = pl.ds(pl.multiple_of(block * rows, rows), rows)
            return pltpu.make_async_copy(buffer.at[n % depth], out.at[at], sent.at[n % depth])

        for n in range(16):
            block = block_at(owner, n // 4, n % 4)
            if n >= depth:
                copy(n, block).wait()
            fill(n)
            copy(n, block).start()
        for n in range(16 - depth, 16):
            copy(n, block_at(owner, n // 4, n % 4)).wait()

    def fill_up(n):
        for j in range(16):
            part = pieces[n // 4][n % 4, 32 * j : 32 * j + 32]
            buffer_up[n % depth, :, 128 * j : 128 * j + 128] = part.astype(F32) * scale

    def fill_down(n):
        for j in range(4):
            part = pieces[n // 4][n % 4, 128 * j : 128 * j + 128]
            buffer_down[n % depth, :, 128 * j : 128 * j + 128] = part.astype(F32) * scale

    @pl.when(owner == 0)
    def _():
        run(buffer_up, 32, fill_up, up_out)

    @pl.when(owner == 1)
    def _():
        run(buffer_down, 128, fill_down, down_out)


def finish_own_kernel(scale, *refs):
    pieces, (up_out, down_out, buffer_up, buffer_down, sent) = refs[:4], refs[4:]
    write_bands(scale, here()[0], pieces, up_out, down_out, buffer_up, buffer_down, sent)


def finish_kernel(scale, *refs):
    own, other, (up_in, down_in, w_qkv, gain_vec) = refs[:4], refs[4:8], refs[8:12]
    up_out, down_out, qkv, proj, bias, gain_one, gain_two = refs[12:19]
    buffer_up, buffer_down, sent, rest, sums = refs[19:]
    core, _ = here()
    write_bands(scale, 1 - core, other, up_out, down_out, buffer_up, buffer_down, sent)
    for owner, pieces in ((core, own), (1 - core, other)):
        for n in range(16):
            piece = owner * 16 + block_at(owner, n // 4, n % 4)
            rows = pl.ds(pl.multiple_of(piece * 16, 16), 16)
            held = pieces[n // 4]
            for j in range(4):
                at = BAND_ROWS + 16 * j
                part = held[n % 4, at : at + 16].astype(F32) * scale
                proj[rows, 128 * j : 128 * j + 128] = part
            total = jnp.zeros((16, 128), F32)
            for j in range(12):
                cols = slice(128 * j, 128 * j + 128)
                at = ONE_ROWS + 16 * j
                part = held[n % 4, at : at + 16].astype(F32) * scale
                qkv[rows, cols] = part
                total = total + part * w_qkv[rows, cols].astype(F32)
            sums[rows] = total
            rest[piece] = held[n % 4, ONE_ROWS + QKV_ROWS : ALL_ROWS]
    gain_one[...] = jnp.sum(sums[...].T, 0, keepdims=True) / gain_vec[...]
    flat = rest[...].reshape(PIECES * REST_ROWS, 128).astype(F32)
    last = flat[HEADS * WT : GAIN_AT].T * (scale * WT)
    for head in range(HEADS):
        bias[head, 0:128] = flat[head * WT : head * WT + WT].T * (scale * WT)
        bias[head, 128:WT] = last[16 * head : 16 * head + 16]
    for j in range(4):
        part = flat[GAIN_AT + j : GAIN_AT + j + 1] * scale
        gain_two[:, 128 * j : 128 * j + 128] = part


def shape(*dims, dtype=BF16):
    return jax.ShapeDtypeStruct(dims, dtype)


def params(mib):
    return pltpu.CompilerParams(vmem_limit_bytes=mib * MIB)


def vmem(*dims, dtype=BF16):
    return pltpu.VMEM(dims, dtype)


def cost(flops, moved):
    return pl.CostEstimate(flops=flops, bytes_accessed=moved, transcendentals=0)


ANY = pl.BlockSpec(memory_space=pl.ANY)
INSIDE = pl.BlockSpec(memory_space=pltpu.VMEM)
SCALARS = pl.BlockSpec(memory_space=pltpu.SMEM)


def pack(tokens, cotangent):
    edge, top = WLON // 2, WLAT // 2
    return pl.pallas_call(
        pack_kernel,
        out_shape=(
            shape(2, LEVELS, HEIGHT, edge, D), shape(2, LEVELS, top, BREADTH, D),
            shape(2, LEVELS, top, edge, D),
        ),
        in_specs=[INSIDE] * 2,
        out_specs=[INSIDE] * 3,
        compiler_params=params(16),
        name="pack",
    )(tokens, cotangent)


def attention(*operands):
    return pl.pallas_call(
        attention_kernel,
        out_shape=(
            shape(ROWS, D), shape(ROWS, D), shape(D, ROWS), shape(ROWS, QKV),
            shape(WINDOWS, HEADS + 1, WT, 128),
        ),
        in_specs=[INSIDE] * len(operands),
        out_specs=[INSIDE, INSIDE, INSIDE, ANY, ANY],
        scratch_shapes=[
            vmem(56, D, dtype=F32), vmem(ROWS, D, dtype=F32), vmem(ROWS, D), vmem(ROWS, QKV),
            vmem(WINDOWS, HEADS + 1, WT, 128), vmem(2, HEADS + 1, WT, 128, dtype=F32),
            pltpu.SemaphoreType.DMA((WINDOWS + 1,)),
        ],
        compiler_params=params(48),
        cost_estimate=cost(ROWS * D * QKV * 2 * 4, 20_000_000),
        name="attention",
    )(*operands)


def mlp_call(*operands):
    return pl.pallas_call(
        mlp_kernel,
        out_shape=(
            shape(ROWS, D), shape(ROWS, D, dtype=F32), shape(16, ONE_ROWS, 128),
            shape(16, ONE_ROWS, 128), shape(1, D, dtype=F32),
        ),
        in_specs=[INSIDE] * 7 + [ANY, ANY, INSIDE],
        out_specs=[INSIDE, INSIDE, ANY, ANY, INSIDE],
        scratch_shapes=[
            vmem(56, D, dtype=F32), vmem(ROWS, D, dtype=F32), vmem(ROWS, D), vmem(ROWS, D),
            vmem(ROWS, D, dtype=F32), vmem(ROWS, 1, dtype=F32), vmem(D, ROWS),
            vmem(ROWS, F_STEP), vmem(ROWS, FF), vmem(PIECES, ONE_ROWS, 128),
            vmem(D, FF), vmem(FF, D),
            pltpu.SemaphoreType.DMA((2,)), pltpu.SemaphoreType.DMA((2, PIECES)),
        ],
        compiler_params=params(56),
        cost_estimate=cost(ROWS * D * FF * 2 * 8, 40_000_000),
        name="mlp",
    )(*operands)


def back_specs(half):
    start = half * (WINDOWS // 2 // G_BACKWARD)
    return [
        pl.BlockSpec((G_BACKWARD * WT, QKV), lambda i: (start + i, 0)),
        pl.BlockSpec((G_BACKWARD, HEADS + 1, WT, 128), lambda i: (start + i, 0, 0, 0)),
        pl.BlockSpec((G_BACKWARD * WT, D), lambda i: (start + i, 0)),
    ]


def first_back(qkv, probs, grad_mixed):
    return pl.pallas_call(
        first_back_kernel,
        out_shape=(shape(ROWS // 2, QKV), shape(HEADS + 1, WT, 128, dtype=F32)),
        grid=(WINDOWS // 2 // G_BACKWARD,),
        in_specs=back_specs(0),
        out_specs=[
            pl.BlockSpec((G_BACKWARD * WT, QKV), lambda i: (i, 0)),
            pl.BlockSpec((HEADS + 1, WT, 128), lambda i: (0, 0, 0)),
        ],
        compiler_params=params(32),
        cost_estimate=cost(ROWS * D * QKV * 2 * 3, 10_000_000),
        name="first_back",
    )(qkv, probs, grad_mixed)


def second_back(*operands):
    return pl.pallas_call(
        second_back_kernel,
        out_shape=(
            shape(ROWS // 2, QKV), shape(16, TWO_ROWS, 128), shape(16, TWO_ROWS, 128),
        ),
        grid=(WINDOWS // 2 // G_BACKWARD,),
        in_specs=back_specs(1) + [INSIDE] * 4,
        out_specs=[pl.BlockSpec((G_BACKWARD * WT, QKV), lambda i: (i, 0)), INSIDE, INSIDE],
        scratch_shapes=[
            vmem(ROWS, QKV), vmem(HEADS + 1, WT, 128, dtype=F32), vmem(PIECES, TWO_ROWS, 128),
        ],
        compiler_params=params(40),
        cost_estimate=cost(ROWS * D * QKV * 2 * 4, 10_000_000),
        name="second_back",
    )(*operands)


def branch(*operands):
    return pl.pallas_call(
        branch_kernel,
        out_shape=(
            shape(LEVELS, 9, 42, D), shape(LEVELS, 9, 6, D), shape(LEVELS, 3, 42, D),
            shape(LEVELS, 3, 6, D),
        ),
        in_specs=[INSIDE] * len(operands),
        out_specs=[INSIDE] * 4,
        scratch_shapes=[vmem(ROWS, D, dtype=F32), vmem(48, D, dtype=F32)],
        compiler_params=params(24),
        cost_estimate=cost(ROWS * D * QKV * 2 * 4, 10_000_000),
        name="branch",
    )(*operands)


BUFFERS = 4


def finish_scratch():
    return [
        vmem(BUFFERS, 32, FF, dtype=F32), vmem(BUFFERS, 128, D, dtype=F32),
        pltpu.SemaphoreType.DMA((BUFFERS,)),
    ]


def finish_own(pieces, scale):
    return pl.pallas_call(
        functools.partial(finish_own_kernel, scale),
        out_shape=(shape(D, FF, dtype=F32), shape(FF, D, dtype=F32)),
        in_specs=[INSIDE] * 4,
        out_specs=[ANY, ANY],
        scratch_shapes=finish_scratch(),
        compiler_params=params(24),
        cost_estimate=cost(10_000_000, 10_000_000),
        name="finish_own",
    )(*pieces)


def finish(own, other, up, down, w_qkv, gain_one, scale):
    return pl.pallas_call(
        functools.partial(finish_kernel, scale),
        out_shape=(
            shape(D, FF, dtype=F32), shape(FF, D, dtype=F32), shape(D, QKV, dtype=F32),
            shape(D, D, dtype=F32), shape(HEADS, WT, WT, dtype=F32), shape(1, D, dtype=F32),
            shape(1, D, dtype=F32),
        ),
        in_specs=[INSIDE] * 8 + [ANY, ANY, INSIDE, INSIDE],
        out_specs=[ANY, ANY] + [INSIDE] * 5,
        input_output_aliases={8: 0, 9: 1},
        scratch_shapes=finish_scratch() + [vmem(PIECES, REST_ROWS, 128), vmem(D, 128, dtype=F32)],
        compiler_params=params(40),
        cost_estimate=cost(10_000_000, 20_000_000),
        name="finish",
    )(*own, *other, up, down, w_qkv, gain_one)


def neighbour(array, lat_by, lon_by):
    lat_count, lon_count = lax.axis_size("lat"), lax.axis_size("lon")
    pairs = []
    for i in range(lat_count):
        for j in range(lon_count):
            to = ((i + lat_by) % lat_count) * lon_count + (j + lon_by) % lon_count
            pairs.append((i * lon_count + j, to))
    return lax.ppermute(array, ("lat", "lon"), pairs)


def halos(tokens, cotangent):
    lon, lat, both = pack(tokens, cotangent)
    return neighbour(lon, 0, -1), neighbour(lat, -1, 0), neighbour(both, -1, -1)


def send_home(main, lon, lat, both):
    return main, neighbour(lon, 0, 1), neighbour(lat, 1, 0), neighbour(both, 1, 1)


def assemble(main, lon, lat, both):
    upper = jnp.concatenate([both, lat], 2)
    lower = jnp.concatenate([lon, main], 2)
    return jnp.concatenate([upper, lower], 1)


def along(array, stage, by):
    pairs = []
    for lat in range(16):
        for lon in range(8):
            core, chip = position(lat, lon)
            chip = list(chip)
            axis = ORDERS[core][stage]
            chip[axis] = (chip[axis] + by) % 4
            x, y, z = chip
            to = (z * 4 + y // 2 * 2 + core) * 8 + x * 2 + y % 2
            pairs.append((lat * 8 + lon, to))
    return lax.ppermute(array, ("lat", "lon"), pairs)


def other_core(array):
    return lax.ppermute(array, "lat", [(i, i ^ 1) for i in range(16)])


def added(*terms):
    total = terms[0].astype(F32)
    for term in terms[1:]:
        total = total + term.astype(F32)
    return total.astype(BF16)


def after(value, *others):
    return lax.optimization_barrier((value, others))[0]


def core_sum(keep, send):
    return added(keep, other_core(send))


def first_sum(held):
    return added(held[:4], *[along(held[4 * k : 4 * k + 4], 0, k) for k in (1, 2, 3)])


def second_sum(held):
    return added(held[0], *[along(held[k], 1, k) for k in (1, 2, 3)])


def last_sum(share):
    share = lax.optimization_barrier(share)
    one, two, three = [along(share, 2, k).astype(F32) for k in (1, 2, 3)]
    return ((share.astype(F32) + two) + (one + three)).astype(BF16)


def spread(share, meanwhile):
    held = jnp.stack([share] + [along(share, 1, k) for k in (1, 2, 3)])
    result = meanwhile(held)
    own = [held] + [along(held, 0, k) for k in (1, 2, 3)]
    other = [other_core(own[0])] + [other_core(after(piece, result)) for piece in own[1:]]
    return own, other, result


def local(tokens, cotangent, w_qkv, w_proj, w_up, w_down, pair_bias, gain_one, gain_two):
    total_tokens = ROWS * lax.axis_size("lat") * lax.axis_size("lon")
    scale = total_tokens ** (-0.5)
    gain_one = gain_one.reshape(1, D)
    gain_two = gain_two.reshape(1, D)
    edges = halos(tokens, cotangent)
    xw, mix, act_t, qkv, probs = attention(tokens, *edges, w_qkv, pair_bias, gain_one)
    grad_mixed, grad_res, keep_one, send_one, sum_gain_two = mlp_call(
        xw, mix, cotangent, *edges, w_proj, w_up, w_down, gain_two
    )
    grads_first, bias = first_back(qkv, probs, grad_mixed)
    held_one = core_sum(keep_one, send_one)
    grads_second, keep_two, send_two = second_back(
        qkv, probs, grad_mixed, act_t, sum_gain_two, after(bias, held_one), grads_first
    )
    held_one = first_sum(held_one)
    held_two = first_sum(core_sum(keep_two, after(send_two, held_one)))
    share = last_sum(jnp.concatenate([second_sum(held_one), second_sum(held_two)], 0))
    own, other, home = spread(
        share,
        lambda first: branch(
            xw, after(grads_first, first), grads_second, grad_res, w_qkv, gain_one
        ),
    )
    home = send_home(*home)
    up, down = finish_own(own, scale)
    sum_up, sum_down, sum_qkv, sum_proj, sum_bias, sum_one, sum_two = finish(
        own, other, up, down, w_qkv, gain_one, scale
    )
    return (
        assemble(*[after(piece, up) for piece in home]),
        sum_qkv,
        sum_proj,
        sum_up,
        sum_down,
        sum_bias,
        sum_one.reshape(D),
        sum_two.reshape(D),
    )


def solution(mesh):
    grid = P(None, "lat", "lon", None)
    in_specs = (grid, grid, P(), P(), P(), P(), P(), P(), P())
    out_specs = (grid, P(), P(), P(), P(), P(), P(), P())
    return jax.shard_map(local, mesh=mesh, in_specs=in_specs, out_specs=out_specs, check_vma=False)
```

```python
import functools

import jax
import jax.numpy as jnp
from jax import lax
from jax.experimental import pallas as pl
from jax.experimental.pallas import tpu as pltpu
from jax.sharding import PartitionSpec as P

HEADS = 8
WLAT = 6
WLON = 12
WT = 144
D = 512
QKV = 1536
FF = 2048
LEVELS = 2
HEIGHT = 12
BREADTH = 48
WINDOWS = 8
ROWS = WINDOWS * WT
EPSILON = 1e-05
MASKED = -1e30
F32 = jnp.float32
BF16 = jnp.bfloat16
PIECES = 32
BAND_ROWS = 512
PROJ_ROWS = 64
ONE_ROWS = BAND_ROWS + PROJ_ROWS
QKV_ROWS = 192
REST_ROWS = 48
TWO_ROWS = QKV_ROWS + REST_ROWS
ALL_ROWS = ONE_ROWS + TWO_ROWS
GAIN_AT = (HEADS + 1) * WT
MIB = 1024 * 1024
M_NORM = 576
M_UP = 1152
M_BACK = 576
M_BRANCH = 576
G_FORWARD = 4
G_BACKWARD = 2
F_STEP = 512

NN = (((1,), (0,)), ((), ()))
NT = (((1,), (1,)), ((), ()))
TN = (((0,), (0,)), ((), ()))


def mm(a, b, dims=NN):
    return lax.dot_general(a, b, dims, preferred_element_type=F32)


def stats_of(values):
    average = jnp.mean(values, -1, keepdims=True)
    centred = values - average
    variance = jnp.mean(centred * centred, -1, keepdims=True)
    inv_std = lax.rsqrt(variance + EPSILON)
    return centred * inv_std, inv_std


def back_of(grad_out, gain_vec, normed, inv_std):
    scaled = grad_out * gain_vec
    return (
        scaled
        - jnp.mean(scaled, -1, keepdims=True)
        - normed * jnp.mean(scaled * normed, -1, keepdims=True)
    ) * inv_std


def run_at(level, row, column):
    window = (row // WLAT) * 4 + column
    return window * WT + level * (WT // 2) + (row % WLAT) * WLON


def gather_windows(main_ref, lon_ref, lat_ref, both_ref, line, wide, out_ref):
    for level in range(LEVELS):
        for row in range(HEIGHT):
            if row < HEIGHT - WLAT // 2:
                line[0:BREADTH] = main_ref[level, row + WLAT // 2].astype(F32)
                line[BREADTH : BREADTH + 6] = lon_ref[level, row + WLAT // 2].astype(F32)
            else:
                line[0:BREADTH] = lat_ref[level, row - (HEIGHT - WLAT // 2)].astype(F32)
                line[BREADTH : BREADTH + 6] = both_ref[level, row - (HEIGHT - WLAT // 2)].astype(F32)
            for column in range(4):
                at = run_at(level, row, column)
                wide[at : at + WLON] = line[6 + WLON * column : 18 + WLON * column]

    def narrow(window, _):
        rows = pl.ds(pl.multiple_of(window * WT, 16), WT)
        out_ref[rows] = wide[rows].astype(BF16)
        return 0

    lax.fori_loop(0, WINDOWS, narrow, 0)


def position(lat, lon):
    return lat % 2, (lon // 2, (lat // 2) % 2 * 2 + lon % 2, lat // 4)


ORDERS = ((0, 1, 2), (1, 2, 0))


def here():
    return position(lax.axis_index("lat"), lax.axis_index("lon"))


def slot_of(core, block):
    _, chip = here()
    first, second = chip[ORDERS[core][0]], chip[ORDERS[core][1]]
    return (block // 4 + 4 - first) % 4 * 4 + (block % 4 + 4 - second) % 4


def block_at(core, first_by, second_by):
    _, chip = here()
    first = jnp.where(core == 0, chip[ORDERS[0][0]], chip[ORDERS[1][0]])
    second = jnp.where(core == 0, chip[ORDERS[0][1]], chip[ORDERS[1][1]])
    return (first + 4 - first_by) % 4 * 4 + (second + 4 - second_by) % 4


def window_rows(window):
    return pl.ds(pl.multiple_of(window * WT, 16), WT)


def softmax_first(scores):
    top = jnp.max(scores, 0, keepdims=True)
    exponent = jnp.exp(scores - top)
    total = jnp.sum(exponent, 0, keepdims=True)
    return (exponent * (1.0 / total)).astype(BF16)


def head_masks():
    lane = lax.broadcasted_iota(jnp.int32, (1, 128), 1)
    first = lane < 64
    row = lax.broadcasted_iota(jnp.int32, (128, D), 0) // 16
    column = lax.broadcasted_iota(jnp.int32, (128, D), 1) // 64
    halves = (first.astype(F32).astype(BF16), (lane >= 64).astype(F32).astype(BF16))
    return first, halves, (row == column).astype(F32)


def tiled(block):
    return jnp.concatenate([block] * HEADS, 0)


def pair_of(head):
    return slice(head // 2 * 128, head // 2 * 128 + 128)


def tail_sum(block, tail):
    return jnp.sum((block * tail).reshape(HEADS, 16, D), 0)


def pack_kernel(ref, lon, lat, both):
    edge, top = WLON // 2, WLAT // 2
    lat[...] = ref[:, :top]
    for level in range(LEVELS):
        for row in range(HEIGHT):
            lon[level, row] = ref[level, row, :edge]
        for row in range(top):
            both[level, row] = ref[level, row, :edge]


def attention_kernel(
    tok, tok_lon, tok_lat, tok_both, w_qkv, pair_bias, gain_one,
    xw, mix, act_t, qkv_out, probs_out,
    line, wide, act, qkv, probs, bias, sent,
):
    gather_windows(tok, tok_lon, tok_lat, tok_both, line, wide, xw)

    def norm_one(window, _):
        rows = window_rows(window)
        values, _ = stats_of(xw[rows].astype(F32))
        act[rows] = (values * gain_one[...]).astype(BF16)
        return 0

    lax.fori_loop(0, WINDOWS, norm_one, 0)

    def project(n, _):
        cols = pl.ds(pl.multiple_of(n * 256, 256), 256)
        qkv[:, cols] = mm(act[...], w_qkv[:, cols]).astype(BF16)
        return 0

    lax.fori_loop(0, QKV // 256, project, 0)
    copies = [pltpu.make_async_copy(qkv, qkv_out, sent.at[WINDOWS])]
    copies[0].start()
    act_t[...] = act[...].T

    is_last = lax.axis_index("lat") == lax.axis_size("lat") - 1
    key_at = lax.broadcasted_iota(jnp.int32, (WT, 128), 0)
    query_at = lax.broadcasted_iota(jnp.int32, (WT, 128), 1)

    def masked(query_at):
        apart = (key_at // WLON % WLAT >= WLAT // 2) != (query_at // WLON % WLAT >= WLAT // 2)
        return jnp.where(apart & is_last, MASKED, 0.0)

    mask_main = masked(query_at)
    mask_tail = masked(128 + query_at % 16)
    for head in range(HEADS):
        block = pair_bias[head, 0:128].T
        bias[0, head] = block
        bias[1, head] = block + mask_main
    block = jnp.concatenate([pair_bias[head, 128:WT] for head in range(HEADS)], 0).T
    bias[0, HEADS] = block
    bias[1, HEADS] = block + mask_tail

    first, halves, tail = head_masks()
    halves = [half * 0.125 for half in halves]
    tail_low = (tail * 0.125).astype(BF16)

    def attend(group, _):
        windows = [group * G_FORWARD + i for i in range(G_FORWARD)]
        heads = [(i, head) for i in range(G_FORWARD) for head in range(HEADS)]
        rows = [window_rows(window) for window in windows]
        main = [pl.ds(pl.multiple_of(window * WT, 16), 128) for window in windows]
        last = [pl.ds(pl.multiple_of(window * WT + 128, 16), 16) for window in windows]
        key = [qkv[r, D : 2 * D] for r in rows]
        val = [qkv[r, 2 * D : 3 * D] for r in rows]
        tail_scores = [
            mm(k, tiled(qkv[r, 0:D]) * tail_low, NT) for k, r in zip(key, last)
        ]
        scores = [
            mm(key[i][:, pair_of(head)], qkv[main[i], pair_of(head)] * halves[head % 2], NT)
            for i, head in heads
        ]
        tail_weights = [
            softmax_first(t + bias[window // 4, HEADS]) for t, window in zip(tail_scores, windows)
        ]
        weights = [
            softmax_first(t + bias[windows[i] // 4, head]) for t, (i, head) in zip(scores, heads)
        ]
        tail_mixed = [mm(w, v, TN) for w, v in zip(tail_weights, val)]
        mixed = [mm(w, val[i][:, pair_of(head)], TN) for w, (i, head) in zip(weights, heads)]
        for i, window in enumerate(windows):
            probs[window, HEADS] = tail_weights[i]
            mix[last[i]] = tail_sum(tail_mixed[i], tail).astype(BF16)
        for w, (i, head) in zip(weights, heads):
            probs[windows[i], head] = w
        for n, (i, head) in enumerate(heads):
            if head % 2 == 0:
                mix[main[i], pair_of(head)] = jnp.where(first, mixed[n], mixed[n + 1]).astype(BF16)
        for window in windows:
            pltpu.make_async_copy(probs.at[window], probs_out.at[window], sent.at[window]).start()
        return 0

    lax.fori_loop(0, WINDOWS // G_FORWARD, attend, 0)
    copies[0].wait()
    for window in range(WINDOWS):
        pltpu.make_async_copy(probs.at[window], probs_out.at[window], sent.at[window]).wait()


def mlp_kernel(
    xw, mix, cot, cot_lon, cot_lat, cot_both, w_proj, w_up_in, w_down_in, gain_two,
    grad_mixed, grad_res, keep_one, send_one, sum_gain,
    line, wide, cotw, act, normed, inv_two, act_t, activated, grad_hidden, sums, w_up, w_down,
    got, sent,
):
    loads = [
        pltpu.make_async_copy(w_up_in, w_up, got.at[0]),
        pltpu.make_async_copy(w_down_in, w_down, got.at[1]),
    ]
    for load in loads:
        load.start()
    gather_windows(cot, cot_lon, cot_lat, cot_both, line, wide, cotw)

    def norm_two(part, _):
        rows = pl.ds(pl.multiple_of(part * M_NORM, 16), M_NORM)
        residual = xw[rows].astype(F32) + mm(mix[rows], w_proj[...])
        values, inv_std = stats_of(residual)
        normed[rows] = values
        inv_two[rows] = inv_std
        act[rows] = (values * gain_two[...]).astype(BF16)
        return 0

    lax.fori_loop(0, ROWS // M_NORM, norm_two, 0)
    act_t[...] = act[...].T
    for load in loads:
        load.wait()

    c0 = 0.7978845608028654
    c1 = c0 * 0.044715

    def mlp(f, _):
        cols = pl.ds(pl.multiple_of(f * F_STEP, F_STEP), F_STEP)

        def rows_of(r, _):
            rows = pl.ds(pl.multiple_of(r * M_UP, 16), M_UP)
            u = mm(act[rows], w_up[:, cols])
            grad_act = mm(cotw[rows], w_down[cols, :], NT)
            square = u * u
            gate = 0.5 + 0.5 * jnp.tanh(u * (c0 + c1 * square))
            value = u * gate
            activated[rows] = value.astype(BF16)
            slope = gate + value * (1.0 - gate) * (2.0 * c0 + 6.0 * c1 * square)
            grad_hidden[rows, cols] = (grad_act * slope).astype(BF16)
            return 0

        lax.fori_loop(0, ROWS // M_UP, rows_of, 0)
        up = mm(act_t[...], grad_hidden[:, cols]).astype(BF16)
        for j in range(4):
            at = pl.ds(pl.multiple_of(f * 128 + 32 * j, 32), 32)
            sums[0:16, at] = up[:, 128 * j : 128 * j + 128].reshape(16, 32, 128)
        down = mm(activated[...], cotw[...], TN).astype(BF16)
        for i in range(4):
            for j in range(4):
                part = down[128 * i : 128 * i + 128, 128 * j : 128 * j + 128]
                sums[16 + f * 4 + i, 128 * j : 128 * j + 128] = part
        return 0

    lax.fori_loop(0, FF // F_STEP, mlp, 0)

    core, _ = here()

    def send(rows, at, act_on):
        for owner in range(2):
            for block in range(16):
                piece = owner * 16 + block
                slot = slot_of(owner, block)

                def copy_to(out):
                    return pltpu.make_async_copy(
                        sums.at[piece, rows], out.at[slot, rows], sent.at[at, piece]
                    )

                @pl.when(core == owner)
                def _():
                    act_on(copy_to(keep_one))

                @pl.when(core != owner)
                def _():
                    act_on(copy_to(send_one))

    bands, tails = pl.ds(0, BAND_ROWS), pl.ds(BAND_ROWS, PROJ_ROWS)
    send(bands, 0, lambda copy: copy.start())

    def back(part, total):
        rows = pl.ds(pl.multiple_of(part * M_BACK, 16), M_BACK)
        grads = mm(grad_hidden[rows], w_up[...], NT)
        values = normed[rows]
        total = total + jnp.sum(grads * values, 0, keepdims=True)
        residual = cotw[rows].astype(F32) + back_of(grads, gain_two[...], values, inv_two[rows])
        grad_res[rows] = residual
        low = residual.astype(BF16)
        act[rows] = low
        grad_mixed[rows] = mm(low, w_proj[...], NT).astype(BF16)
        return total

    sum_gain[...] = lax.fori_loop(0, ROWS // M_BACK, back, jnp.zeros((1, D), F32))
    proj = mm(mix[...], act[...], TN).astype(BF16)
    for j in range(4):
        at = slice(BAND_ROWS + 16 * j, BAND_ROWS + 16 * j + 16)
        sums[:, at] = proj[:, 128 * j : 128 * j + 128].reshape(PIECES, 16, 128)
    send(tails, 1, lambda copy: copy.start())
    send(bands, 0, lambda copy: copy.wait())
    send(tails, 1, lambda copy: copy.wait())


def first_back_kernel(qkv, probs, grad_mixed, grad_qkv, bias):
    window_back(qkv, probs, grad_mixed, grad_qkv, bias, None)


def second_back_kernel(
    qkv, probs, grad_mixed, act_t, sum_gain_two, bias_before, grads_before,
    grad_qkv, keep_two, send_two,
    grads_all, bias, flat,
):
    step = pl.program_id(0)

    @pl.when(step == 0)
    def _():
        grads_all[0 : ROWS // 2] = grads_before[...]

    window_back(qkv, probs, grad_mixed, grad_qkv, bias, bias_before)
    size = G_BACKWARD * WT
    at = pl.multiple_of(ROWS // 2 + step * size, 16)
    grads_all[pl.ds(at, size)] = grad_qkv[...]

    @pl.when(step == WINDOWS // 2 // G_BACKWARD - 1)
    def _():
        for n in range(QKV // 512):
            part = mm(act_t[...], grads_all[:, 512 * n : 512 * n + 512]).astype(BF16)
            for j in range(4):
                at = (n * 4 + j) * 16
                flat[:, at : at + 16] = part[:, 128 * j : 128 * j + 128].reshape(PIECES, 16, 128)
        gains = [sum_gain_two[:, 128 * j : 128 * j + 128] for j in range(4)]
        gains = jnp.concatenate(gains + [jnp.zeros((12, 128), F32)], 0)
        rest = [bias[block].astype(BF16) for block in range(HEADS + 1)] + [gains.astype(BF16)]
        rest.append(jnp.zeros((PIECES * REST_ROWS - GAIN_AT - 16, 128), BF16))
        rest = jnp.concatenate(rest, 0)
        flat[:, QKV_ROWS:TWO_ROWS] = rest.reshape(PIECES, REST_ROWS, 128)
        core, _ = here()
        for owner in range(2):
            for block in range(16):
                slot = slot_of(owner, block)
                piece = flat[owner * 16 + block]

                @pl.when(core == owner)
                def _():
                    keep_two[slot] = piece

                @pl.when(core != owner)
                def _():
                    send_two[slot] = piece


def window_back(qkv, probs, grad_mixed, grad_qkv, bias, bias_before):
    step = pl.program_id(0)
    first, halves, tail = head_masks()
    tail_low = tail.astype(BF16)

    @pl.when(step == 0)
    def _():
        bias[...] = jnp.zeros_like(bias) if bias_before is None else bias_before[...]

    group = range(G_BACKWARD)
    heads = [(i, head) for i in group for head in range(HEADS)]
    rows = [slice(i * WT, i * WT + WT) for i in group]
    main = [slice(i * WT, i * WT + 128) for i in group]
    last = [slice(i * WT + 128, i * WT + WT) for i in group]
    key = [qkv[r, D : 2 * D] for r in rows]
    val = [qkv[r, 2 * D : 3 * D] for r in rows]
    query_tail = [tiled(qkv[r, 0:D]) * tail_low for r in last]
    out_tail = [tiled(grad_mixed[r]) * tail_low for r in last]
    query = [qkv[main[i], pair_of(head)] * halves[head % 2] for i, head in heads]
    out = [grad_mixed[main[i], pair_of(head)] * halves[head % 2] for i, head in heads]

    tail_probs = [mm(v, o, NT) for v, o in zip(val, out_tail)]
    grad_probs = [mm(val[i][:, pair_of(head)], o, NT) for o, (i, head) in zip(out, heads)]

    def score_grads(low_probs, grad_probs):
        weights = low_probs.astype(F32)
        product = grad_probs * weights
        return product - weights * jnp.sum(product, 0, keepdims=True)

    tail_low_probs = [probs[i, HEADS] for i in group]
    low_probs = [probs[i, head] for i, head in heads]
    tail_grads = [score_grads(p, g) for p, g in zip(tail_low_probs, tail_probs)]
    grads = [score_grads(p, g) for p, g in zip(low_probs, grad_probs)]
    bias[HEADS] += sum(tail_grads[1:], tail_grads[0])
    for head in range(HEADS):
        mine = grads[head::HEADS]
        bias[head] += sum(mine[1:], mine[0])
    tail_grads = [g.astype(BF16) for g in tail_grads]
    grads = [g.astype(BF16) for g in grads]

    query_last = [mm(g, k, TN) for g, k in zip(tail_grads, key)]
    key_more = [mm(g, q) for g, q in zip(tail_grads, query_tail)]
    val_more = [mm(p, o) for p, o in zip(tail_low_probs, out_tail)]
    query_parts = [mm(g, key[i][:, pair_of(head)], TN) for g, (i, head) in zip(grads, heads)]
    key_parts = [mm(g, q) for g, q in zip(grads, query)]
    val_parts = [mm(p, o) for p, o in zip(low_probs, out)]
    for i in group:
        grad_qkv[last[i], 0:D] = (tail_sum(query_last[i], tail) * 0.125).astype(BF16)
    for n, (i, head) in enumerate(heads):
        if head % 2:
            continue
        cols = pair_of(head)
        at = head // 2 * 128
        part = jnp.where(first, query_parts[n], query_parts[n + 1]) * 0.125
        grad_qkv[main[i], cols] = part.astype(BF16)
        part = (key_parts[n] + key_parts[n + 1] + key_more[i][:, cols]) * 0.125
        grad_qkv[rows[i], D + at : D + at + 128] = part.astype(BF16)
        part = val_parts[n] + val_parts[n + 1] + val_more[i][:, cols]
        grad_qkv[rows[i], 2 * D + at : 2 * D + at + 128] = part.astype(BF16)

def branch_kernel(xw, grads_first, grads_second, grad_res, w_qkv, gain_one, main, lon, lat, both, wide, line):
    for part, grad_qkv in enumerate((grads_first, grads_second)):
        rows = slice(part * ROWS // 2, (part + 1) * ROWS // 2)
        values, inv_std = stats_of(xw[rows].astype(F32))
        grads = mm(grad_qkv[...], w_qkv[...], NT)
        low = back_of(grads, gain_one[...], values, inv_std).astype(BF16)
        wide[rows] = grad_res[rows] + low.astype(F32)

    for level in range(LEVELS):
        for row in range(HEIGHT):
            for column in range(4):
                at = run_at(level, row, column)
                line[WLON * column : WLON * column + WLON] = wide[at : at + WLON]
            inner, outer = (main, lon) if row < HEIGHT - WLAT // 2 else (lat, both)
            at = row if row < HEIGHT - WLAT // 2 else row - (HEIGHT - WLAT // 2)
            inner[level, at] = line[0 : BREADTH - 6].astype(BF16)
            outer[level, at] = line[BREADTH - 6 : BREADTH].astype(BF16)


def write_bands(scale, owner, pieces, up_out, down_out, buffer_up, buffer_down, sent):
    depth = buffer_up.shape[0]

    def run(buffer, rows, fill, out):
        def copy(n, block):
            at = pl.ds(pl.multiple_of(block * rows, rows), rows)
            return pltpu.make_async_copy(buffer.at[n % depth], out.at[at], sent.at[n % depth])

        for n in range(16):
            block = block_at(owner, n // 4, n % 4)
            if n >= depth:
                copy(n, block).wait()
            fill(n)
            copy(n, block).start()
        for n in range(16 - depth, 16):
            copy(n, block_at(owner, n // 4, n % 4)).wait()

    def fill_up(n):
        for j in range(16):
            part = pieces[n // 4][n % 4, 32 * j : 32 * j + 32]
            buffer_up[n % depth, :, 128 * j : 128 * j + 128] = part.astype(F32) * scale

    def fill_down(n):
        for j in range(4):
            part = pieces[n // 4][n % 4, 128 * j : 128 * j + 128]
            buffer_down[n % depth, :, 128 * j : 128 * j + 128] = part.astype(F32) * scale

    @pl.when(owner == 0)
    def _():
        run(buffer_up, 32, fill_up, up_out)

    @pl.when(owner == 1)
    def _():
        run(buffer_down, 128, fill_down, down_out)


def finish_own_kernel(scale, *refs):
    pieces, (up_out, down_out, buffer_up, buffer_down, sent) = refs[:4], refs[4:]
    write_bands(scale, here()[0], pieces, up_out, down_out, buffer_up, buffer_down, sent)


def finish_kernel(scale, *refs):
    own, other, (up_in, down_in, w_qkv, gain_vec) = refs[:4], refs[4:8], refs[8:12]
    up_out, down_out, qkv, proj, bias, gain_one, gain_two = refs[12:19]
    buffer_up, buffer_down, sent, rest, sums = refs[19:]
    core, _ = here()
    write_bands(scale, 1 - core, other, up_out, down_out, buffer_up, buffer_down, sent)
    for owner, pieces in ((core, own), (1 - core, other)):
        for n in range(16):
            piece = owner * 16 + block_at(owner, n // 4, n % 4)
            rows = pl.ds(pl.multiple_of(piece * 16, 16), 16)
            held = pieces[n // 4]
            for j in range(4):
                at = BAND_ROWS + 16 * j
                part = held[n % 4, at : at + 16].astype(F32) * scale
                proj[rows, 128 * j : 128 * j + 128] = part
            total = jnp.zeros((16, 128), F32)
            for j in range(12):
                cols = slice(128 * j, 128 * j + 128)
                at = ONE_ROWS + 16 * j
                part = held[n % 4, at : at + 16].astype(F32) * scale
                qkv[rows, cols] = part
                total = total + part * w_qkv[rows, cols].astype(F32)
            sums[rows] = total
            rest[piece] = held[n % 4, ONE_ROWS + QKV_ROWS : ALL_ROWS]
    gain_one[...] = jnp.sum(sums[...].T, 0, keepdims=True) / gain_vec[...]
    flat = rest[...].reshape(PIECES * REST_ROWS, 128).astype(F32)
    last = flat[HEADS * WT : GAIN_AT].T * (scale * WT)
    for head in range(HEADS):
        bias[head, 0:128] = flat[head * WT : head * WT + WT].T * (scale * WT)
        bias[head, 128:WT] = last[16 * head : 16 * head + 16]
    for j in range(4):
        part = flat[GAIN_AT + j : GAIN_AT + j + 1] * scale
        gain_two[:, 128 * j : 128 * j + 128] = part


def shape(*dims, dtype=BF16):
    return jax.ShapeDtypeStruct(dims, dtype)


def params(mib):
    return pltpu.CompilerParams(vmem_limit_bytes=mib * MIB)


def vmem(*dims, dtype=BF16):
    return pltpu.VMEM(dims, dtype)


def cost(flops, moved):
    return pl.CostEstimate(flops=flops, bytes_accessed=moved, transcendentals=0)


ANY = pl.BlockSpec(memory_space=pl.ANY)
INSIDE = pl.BlockSpec(memory_space=pltpu.VMEM)
SCALARS = pl.BlockSpec(memory_space=pltpu.SMEM)


def pack(grid):
    edge, top = WLON // 2, WLAT // 2
    return pl.pallas_call(
        pack_kernel,
        out_shape=(
            shape(LEVELS, HEIGHT, edge, D), shape(LEVELS, top, BREADTH, D),
            shape(LEVELS, top, edge, D),
        ),
        in_specs=[INSIDE],
        out_specs=[INSIDE] * 3,
        compiler_params=params(16),
        name="pack",
    )(grid)


def attention(*operands):
    return pl.pallas_call(
        attention_kernel,
        out_shape=(
            shape(ROWS, D), shape(ROWS, D), shape(D, ROWS), shape(ROWS, QKV),
            shape(WINDOWS, HEADS + 1, WT, 128),
        ),
        in_specs=[INSIDE] * len(operands),
        out_specs=[INSIDE, INSIDE, INSIDE, ANY, ANY],
        scratch_shapes=[
            vmem(56, D, dtype=F32), vmem(ROWS, D, dtype=F32), vmem(ROWS, D), vmem(ROWS, QKV),
            vmem(WINDOWS, HEADS + 1, WT, 128), vmem(2, HEADS + 1, WT, 128, dtype=F32),
            pltpu.SemaphoreType.DMA((WINDOWS + 1,)),
        ],
        compiler_params=params(48),
        cost_estimate=cost(ROWS * D * QKV * 2 * 4, 20_000_000),
        name="attention",
    )(*operands)


def mlp_call(*operands):
    return pl.pallas_call(
        mlp_kernel,
        out_shape=(
            shape(ROWS, D), shape(ROWS, D, dtype=F32), shape(16, ONE_ROWS, 128),
            shape(16, ONE_ROWS, 128), shape(1, D, dtype=F32),
        ),
        in_specs=[INSIDE] * 7 + [ANY, ANY, INSIDE],
        out_specs=[INSIDE, INSIDE, ANY, ANY, INSIDE],
        scratch_shapes=[
            vmem(56, D, dtype=F32), vmem(ROWS, D, dtype=F32), vmem(ROWS, D), vmem(ROWS, D),
            vmem(ROWS, D, dtype=F32), vmem(ROWS, 1, dtype=F32), vmem(D, ROWS),
            vmem(ROWS, F_STEP), vmem(ROWS, FF), vmem(PIECES, ONE_ROWS, 128),
            vmem(D, FF), vmem(FF, D),
            pltpu.SemaphoreType.DMA((2,)), pltpu.SemaphoreType.DMA((2, PIECES)),
        ],
        compiler_params=params(56),
        cost_estimate=cost(ROWS * D * FF * 2 * 8, 40_000_000),
        name="mlp",
    )(*operands)


def back_specs(half):
    start = half * (WINDOWS // 2 // G_BACKWARD)
    return [
        pl.BlockSpec((G_BACKWARD * WT, QKV), lambda i: (start + i, 0)),
        pl.BlockSpec((G_BACKWARD, HEADS + 1, WT, 128), lambda i: (start + i, 0, 0, 0)),
        pl.BlockSpec((G_BACKWARD * WT, D), lambda i: (start + i, 0)),
    ]


def first_back(qkv, probs, grad_mixed):
    return pl.pallas_call(
        first_back_kernel,
        out_shape=(shape(ROWS // 2, QKV), shape(HEADS + 1, WT, 128, dtype=F32)),
        grid=(WINDOWS // 2 // G_BACKWARD,),
        in_specs=back_specs(0),
        out_specs=[
            pl.BlockSpec((G_BACKWARD * WT, QKV), lambda i: (i, 0)),
            pl.BlockSpec((HEADS + 1, WT, 128), lambda i: (0, 0, 0)),
        ],
        compiler_params=params(32),
        cost_estimate=cost(ROWS * D * QKV * 2 * 3, 10_000_000),
        name="first_back",
    )(qkv, probs, grad_mixed)


def second_back(*operands):
    return pl.pallas_call(
        second_back_kernel,
        out_shape=(
            shape(ROWS // 2, QKV), shape(16, TWO_ROWS, 128), shape(16, TWO_ROWS, 128),
        ),
        grid=(WINDOWS // 2 // G_BACKWARD,),
        in_specs=back_specs(1) + [INSIDE] * 4,
        out_specs=[pl.BlockSpec((G_BACKWARD * WT, QKV), lambda i: (i, 0)), INSIDE, INSIDE],
        scratch_shapes=[
            vmem(ROWS, QKV), vmem(HEADS + 1, WT, 128, dtype=F32), vmem(PIECES, TWO_ROWS, 128),
        ],
        compiler_params=params(40),
        cost_estimate=cost(ROWS * D * QKV * 2 * 4, 10_000_000),
        name="second_back",
    )(*operands)


def branch(*operands):
    return pl.pallas_call(
        branch_kernel,
        out_shape=(
            shape(LEVELS, 9, 42, D), shape(LEVELS, 9, 6, D), shape(LEVELS, 3, 42, D),
            shape(LEVELS, 3, 6, D),
        ),
        in_specs=[INSIDE] * len(operands),
        out_specs=[INSIDE] * 4,
        scratch_shapes=[vmem(ROWS, D, dtype=F32), vmem(48, D, dtype=F32)],
        compiler_params=params(24),
        cost_estimate=cost(ROWS * D * QKV * 2 * 4, 10_000_000),
        name="branch",
    )(*operands)


BUFFERS = 4


def finish_scratch():
    return [
        vmem(BUFFERS, 32, FF, dtype=F32), vmem(BUFFERS, 128, D, dtype=F32),
        pltpu.SemaphoreType.DMA((BUFFERS,)),
    ]


def finish_own(pieces, scale):
    return pl.pallas_call(
        functools.partial(finish_own_kernel, scale),
        out_shape=(shape(D, FF, dtype=F32), shape(FF, D, dtype=F32)),
        in_specs=[INSIDE] * 4,
        out_specs=[ANY, ANY],
        scratch_shapes=finish_scratch(),
        compiler_params=params(24),
        cost_estimate=cost(10_000_000, 10_000_000),
        name="finish_own",
    )(*pieces)


def finish(own, other, up, down, w_qkv, gain_one, scale):
    return pl.pallas_call(
        functools.partial(finish_kernel, scale),
        out_shape=(
            shape(D, FF, dtype=F32), shape(FF, D, dtype=F32), shape(D, QKV, dtype=F32),
            shape(D, D, dtype=F32), shape(HEADS, WT, WT, dtype=F32), shape(1, D, dtype=F32),
            shape(1, D, dtype=F32),
        ),
        in_specs=[INSIDE] * 8 + [ANY, ANY, INSIDE, INSIDE],
        out_specs=[ANY, ANY] + [INSIDE] * 5,
        input_output_aliases={8: 0, 9: 1},
        scratch_shapes=finish_scratch() + [vmem(PIECES, REST_ROWS, 128), vmem(D, 128, dtype=F32)],
        compiler_params=params(40),
        cost_estimate=cost(10_000_000, 20_000_000),
        name="finish",
    )(*own, *other, up, down, w_qkv, gain_one)


def neighbour(array, lat_by, lon_by):
    lat_count, lon_count = lax.axis_size("lat"), lax.axis_size("lon")
    pairs = []
    for i in range(lat_count):
        for j in range(lon_count):
            to = ((i + lat_by) % lat_count) * lon_count + (j + lon_by) % lon_count
            pairs.append((i * lon_count + j, to))
    return lax.ppermute(array, ("lat", "lon"), pairs)


def halos(grid):
    lon, lat, both = pack(grid)
    return neighbour(lat, -1, 0), neighbour(lon, 0, -1), neighbour(both, -1, -1)


def send_home(main, lon, lat, both):
    return main, neighbour(lon, 0, 1), neighbour(lat, 1, 0), neighbour(both, 1, 1)


def assemble(main, lon, lat, both):
    upper = jnp.concatenate([both, lat], 2)
    lower = jnp.concatenate([lon, main], 2)
    return jnp.concatenate([upper, lower], 1)


def along(array, stage, by):
    pairs = []
    for lat in range(16):
        for lon in range(8):
            core, chip = position(lat, lon)
            chip = list(chip)
            axis = ORDERS[core][stage]
            chip[axis] = (chip[axis] + by) % 4
            x, y, z = chip
            to = (z * 4 + y // 2 * 2 + core) * 8 + x * 2 + y % 2
            pairs.append((lat * 8 + lon, to))
    return lax.ppermute(array, ("lat", "lon"), pairs)


def other_core(array):
    return lax.ppermute(array, "lat", [(i, i ^ 1) for i in range(16)])


def added(*terms):
    total = terms[0].astype(F32)
    for term in terms[1:]:
        total = total + term.astype(F32)
    return total.astype(BF16)


def after(value, *others):
    return lax.optimization_barrier((value, others))[0]


def core_sum(keep, send):
    return added(keep, other_core(send))


def first_sum(held):
    return added(held[:4], *[along(held[4 * k : 4 * k + 4], 0, k) for k in (1, 2, 3)])


def second_sum(held):
    return added(held[0], *[along(held[k], 1, k) for k in (1, 2, 3)])


def last_sum(share):
    share = lax.optimization_barrier(share)
    one, two, three = [along(share, 2, k).astype(F32) for k in (1, 2, 3)]
    return ((share.astype(F32) + two) + (one + three)).astype(BF16)


def spread(share, meanwhile):
    held = jnp.stack([share] + [along(share, 1, k) for k in (1, 2, 3)])
    result = meanwhile(held)
    own = [held] + [along(held, 0, k) for k in (1, 2, 3)]
    other = [other_core(own[0])] + [other_core(after(piece, result)) for piece in own[1:]]
    return own, other, result


def local(tokens, cotangent, w_qkv, w_proj, w_up, w_down, pair_bias, gain_one, gain_two):
    total_tokens = ROWS * lax.axis_size("lat") * lax.axis_size("lon")
    scale = total_tokens ** (-0.5)
    gain_one = gain_one.reshape(1, D)
    gain_two = gain_two.reshape(1, D)
    lat_edge, lon_edge, corner = halos(tokens)
    cot_lat, cot_lon, cot_corner = halos(cotangent)
    xw, mix, act_t, qkv, probs = attention(
        tokens, lon_edge, lat_edge, corner, w_qkv, pair_bias, gain_one
    )
    grad_mixed, grad_res, keep_one, send_one, sum_gain_two = mlp_call(
        xw, mix, cotangent, cot_lon, cot_lat, cot_corner, w_proj, w_up, w_down, gain_two
    )
    grads_first, bias = first_back(qkv, probs, grad_mixed)
    held_one = core_sum(keep_one, send_one)
    grads_second, keep_two, send_two = second_back(
        qkv, probs, grad_mixed, act_t, sum_gain_two, after(bias, held_one), grads_first
    )
    held_one = first_sum(held_one)
    held_two = first_sum(core_sum(keep_two, after(send_two, held_one)))
    share = last_sum(second_sum(jnp.concatenate([held_one, held_two], 1)))
    own, other, home = spread(
        share,
        lambda first: send_home(
            *branch(xw, after(grads_first, first), grads_second, grad_res, w_qkv, gain_one)
        ),
    )
    up, down = finish_own(own, scale)
    sum_up, sum_down, sum_qkv, sum_proj, sum_bias, sum_one, sum_two = finish(
        own, other, up, down, w_qkv, gain_one, scale
    )
    return (
        assemble(*[after(piece, up) for piece in home]),
        sum_qkv,
        sum_proj,
        sum_up,
        sum_down,
        sum_bias,
        sum_one.reshape(D),
        sum_two.reshape(D),
    )


def solution(mesh):
    grid = P(None, "lat", "lon", None)
    in_specs = (grid, grid, P(), P(), P(), P(), P(), P(), P())
    out_specs = (grid, P(), P(), P(), P(), P(), P(), P())
    return jax.shard_map(local, mesh=mesh, in_specs=in_specs, out_specs=out_specs, check_vma=False)
```

```python
import functools

import jax
import jax.numpy as jnp
from jax import lax
from jax.experimental import pallas as pl
from jax.experimental.pallas import tpu as pltpu
from jax.sharding import PartitionSpec as P

HEADS = 8
WLAT = 6
WLON = 12
WT = 144
D = 512
QKV = 1536
FF = 2048
LEVELS = 2
HEIGHT = 12
BREADTH = 48
WINDOWS = 8
ROWS = WINDOWS * WT
EPSILON = 1e-05
MASKED = -1e30
F32 = jnp.float32
BF16 = jnp.bfloat16
PIECES = 32
BAND_ROWS = 512
PROJ_ROWS = 64
ONE_ROWS = BAND_ROWS + PROJ_ROWS
QKV_ROWS = 192
REST_ROWS = 48
TWO_ROWS = QKV_ROWS + REST_ROWS
ALL_ROWS = ONE_ROWS + TWO_ROWS
GAIN_AT = (HEADS + 1) * WT
MIB = 1024 * 1024
M_NORM = 576
M_UP = 1152
M_BACK = 576
M_BRANCH = 576
G_FORWARD = 4
G_BACKWARD = 2
F_STEP = 512

NN = (((1,), (0,)), ((), ()))
NT = (((1,), (1,)), ((), ()))
TN = (((0,), (0,)), ((), ()))


def mm(a, b, dims=NN):
    return lax.dot_general(a, b, dims, preferred_element_type=F32)


def stats_of(values):
    average = jnp.mean(values, -1, keepdims=True)
    centred = values - average
    variance = jnp.mean(centred * centred, -1, keepdims=True)
    inv_std = lax.rsqrt(variance + EPSILON)
    return centred * inv_std, inv_std


def back_of(grad_out, gain_vec, normed, inv_std):
    scaled = grad_out * gain_vec
    return (
        scaled
        - jnp.mean(scaled, -1, keepdims=True)
        - normed * jnp.mean(scaled * normed, -1, keepdims=True)
    ) * inv_std


def run_at(level, row, column):
    window = (row // WLAT) * 4 + column
    return window * WT + level * (WT // 2) + (row % WLAT) * WLON


def gather_windows(main_ref, lon_ref, lat_ref, both_ref, line, wide, out_ref):
    for level in range(LEVELS):
        for row in range(HEIGHT):
            if row < HEIGHT - WLAT // 2:
                line[0:BREADTH] = main_ref[level, row + WLAT // 2].astype(F32)
                line[BREADTH : BREADTH + 6] = lon_ref[level, row + WLAT // 2].astype(F32)
            else:
                line[0:BREADTH] = lat_ref[level, row - (HEIGHT - WLAT // 2)].astype(F32)
                line[BREADTH : BREADTH + 6] = both_ref[level, row - (HEIGHT - WLAT // 2)].astype(F32)
            for column in range(4):
                at = run_at(level, row, column)
                wide[at : at + WLON] = line[6 + WLON * column : 18 + WLON * column]

    def narrow(window, _):
        rows = pl.ds(pl.multiple_of(window * WT, 16), WT)
        out_ref[rows] = wide[rows].astype(BF16)
        return 0

    lax.fori_loop(0, WINDOWS, narrow, 0)


def position(lat, lon):
    return lat % 2, (lon // 2, (lat // 2) % 2 * 2 + lon % 2, lat // 4)


ORDERS = ((0, 1, 2), (1, 2, 0))


def here():
    return position(lax.axis_index("lat"), lax.axis_index("lon"))


def slot_of(core, block):
    _, chip = here()
    first, second = chip[ORDERS[core][0]], chip[ORDERS[core][1]]
    return (block // 4 + 4 - first) % 4 * 4 + (block % 4 + 4 - second) % 4


def block_at(core, first_by, second_by):
    _, chip = here()
    first = jnp.where(core == 0, chip[ORDERS[0][0]], chip[ORDERS[1][0]])
    second = jnp.where(core == 0, chip[ORDERS[0][1]], chip[ORDERS[1][1]])
    return (first + 4 - first_by) % 4 * 4 + (second + 4 - second_by) % 4


def window_rows(window):
    return pl.ds(pl.multiple_of(window * WT, 16), WT)


def softmax_first(scores):
    top = jnp.max(scores, 0, keepdims=True)
    exponent = jnp.exp(scores - top)
    total = jnp.sum(exponent, 0, keepdims=True)
    return (exponent * (1.0 / total)).astype(BF16)


def head_masks():
    lane = lax.broadcasted_iota(jnp.int32, (1, 128), 1)
    first = lane < 64
    row = lax.broadcasted_iota(jnp.int32, (128, D), 0) // 16
    column = lax.broadcasted_iota(jnp.int32, (128, D), 1) // 64
    halves = (first.astype(F32).astype(BF16), (lane >= 64).astype(F32).astype(BF16))
    return first, halves, (row == column).astype(F32)


def tiled(block):
    return jnp.concatenate([block] * HEADS, 0)


def pair_of(head):
    return slice(head // 2 * 128, head // 2 * 128 + 128)


def tail_sum(block, tail):
    return jnp.sum((block * tail).reshape(HEADS, 16, D), 0)


def pack_kernel(ref, lon, lat, both):
    edge, top = WLON // 2, WLAT // 2
    lat[...] = ref[:, :top]
    for level in range(LEVELS):
        for row in range(HEIGHT):
            lon[level, row] = ref[level, row, :edge]
        for row in range(top):
            both[level, row] = ref[level, row, :edge]


def attention_kernel(
    tok, tok_lon, tok_lat, tok_both, w_qkv, pair_bias, gain_one,
    xw, mix, act_t, qkv_out, probs_out,
    line, wide, act, qkv, probs, bias, sent,
):
    gather_windows(tok, tok_lon, tok_lat, tok_both, line, wide, xw)

    def norm_one(window, _):
        rows = window_rows(window)
        values, _ = stats_of(xw[rows].astype(F32))
        act[rows] = (values * gain_one[...]).astype(BF16)
        return 0

    lax.fori_loop(0, WINDOWS, norm_one, 0)

    def project(n, _):
        cols = pl.ds(pl.multiple_of(n * 256, 256), 256)
        qkv[:, cols] = mm(act[...], w_qkv[:, cols]).astype(BF16)
        return 0

    lax.fori_loop(0, QKV // 256, project, 0)
    copies = [pltpu.make_async_copy(qkv, qkv_out, sent.at[WINDOWS])]
    copies[0].start()
    act_t[...] = act[...].T

    is_last = lax.axis_index("lat") == lax.axis_size("lat") - 1
    key_at = lax.broadcasted_iota(jnp.int32, (WT, 128), 0)
    query_at = lax.broadcasted_iota(jnp.int32, (WT, 128), 1)

    def masked(query_at):
        apart = (key_at // WLON % WLAT >= WLAT // 2) != (query_at // WLON % WLAT >= WLAT // 2)
        return jnp.where(apart & is_last, MASKED, 0.0)

    mask_main = masked(query_at)
    mask_tail = masked(128 + query_at % 16)
    for head in range(HEADS):
        block = pair_bias[head, 0:128].T
        bias[0, head] = block
        bias[1, head] = block + mask_main
    block = jnp.concatenate([pair_bias[head, 128:WT] for head in range(HEADS)], 0).T
    bias[0, HEADS] = block
    bias[1, HEADS] = block + mask_tail

    first, halves, tail = head_masks()
    halves = [half * 0.125 for half in halves]
    tail_low = (tail * 0.125).astype(BF16)

    def attend(group, _):
        windows = [group * G_FORWARD + i for i in range(G_FORWARD)]
        heads = [(i, head) for i in range(G_FORWARD) for head in range(HEADS)]
        rows = [window_rows(window) for window in windows]
        main = [pl.ds(pl.multiple_of(window * WT, 16), 128) for window in windows]
        last = [pl.ds(pl.multiple_of(window * WT + 128, 16), 16) for window in windows]
        key = [qkv[r, D : 2 * D] for r in rows]
        val = [qkv[r, 2 * D : 3 * D] for r in rows]
        tail_scores = [
            mm(k, tiled(qkv[r, 0:D]) * tail_low, NT) for k, r in zip(key, last)
        ]
        scores = [
            mm(key[i][:, pair_of(head)], qkv[main[i], pair_of(head)] * halves[head % 2], NT)
            for i, head in heads
        ]
        tail_weights = [
            softmax_first(t + bias[window // 4, HEADS]) for t, window in zip(tail_scores, windows)
        ]
        weights = [
            softmax_first(t + bias[windows[i] // 4, head]) for t, (i, head) in zip(scores, heads)
        ]
        tail_mixed = [mm(w, v, TN) for w, v in zip(tail_weights, val)]
        mixed = [mm(w, val[i][:, pair_of(head)], TN) for w, (i, head) in zip(weights, heads)]
        for i, window in enumerate(windows):
            probs[window, HEADS] = tail_weights[i]
            mix[last[i]] = tail_sum(tail_mixed[i], tail).astype(BF16)
        for w, (i, head) in zip(weights, heads):
            probs[windows[i], head] = w
        for n, (i, head) in enumerate(heads):
            if head % 2 == 0:
                mix[main[i], pair_of(head)] = jnp.where(first, mixed[n], mixed[n + 1]).astype(BF16)
        for window in windows:
            pltpu.make_async_copy(probs.at[window], probs_out.at[window], sent.at[window]).start()
        return 0

    lax.fori_loop(0, WINDOWS // G_FORWARD, attend, 0)
    copies[0].wait()
    for window in range(WINDOWS):
        pltpu.make_async_copy(probs.at[window], probs_out.at[window], sent.at[window]).wait()


def mlp_kernel(
    xw, mix, cot, cot_lon, cot_lat, cot_both, w_proj, w_up_in, w_down_in, gain_two,
    grad_mixed, grad_res, keep_one, send_one, sum_gain,
    line, wide, cotw, act, normed, inv_two, act_t, activated, grad_hidden, sums, w_up, w_down,
    got, sent,
):
    loads = [
        pltpu.make_async_copy(w_up_in, w_up, got.at[0]),
        pltpu.make_async_copy(w_down_in, w_down, got.at[1]),
    ]
    for load in loads:
        load.start()
    gather_windows(cot, cot_lon, cot_lat, cot_both, line, wide, cotw)

    def norm_two(part, _):
        rows = pl.ds(pl.multiple_of(part * M_NORM, 16), M_NORM)
        residual = xw[rows].astype(F32) + mm(mix[rows], w_proj[...])
        values, inv_std = stats_of(residual)
        normed[rows] = values
        inv_two[rows] = inv_std
        act[rows] = (values * gain_two[...]).astype(BF16)
        return 0

    lax.fori_loop(0, ROWS // M_NORM, norm_two, 0)
    act_t[...] = act[...].T
    for load in loads:
        load.wait()

    c0 = 0.7978845608028654
    c1 = c0 * 0.044715

    def mlp(f, _):
        cols = pl.ds(pl.multiple_of(f * F_STEP, F_STEP), F_STEP)

        def rows_of(r, _):
            rows = pl.ds(pl.multiple_of(r * M_UP, 16), M_UP)
            u = mm(act[rows], w_up[:, cols])
            grad_act = mm(cotw[rows], w_down[cols, :], NT)
            square = u * u
            gate = 0.5 + 0.5 * jnp.tanh(u * (c0 + c1 * square))
            value = u * gate
            activated[rows] = value.astype(BF16)
            slope = gate + value * (1.0 - gate) * (2.0 * c0 + 6.0 * c1 * square)
            grad_hidden[rows, cols] = (grad_act * slope).astype(BF16)
            return 0

        lax.fori_loop(0, ROWS // M_UP, rows_of, 0)
        up = mm(act_t[...], grad_hidden[:, cols]).astype(BF16)
        for j in range(4):
            at = pl.ds(pl.multiple_of(f * 128 + 32 * j, 32), 32)
            sums[0:16, at] = up[:, 128 * j : 128 * j + 128].reshape(16, 32, 128)
        down = mm(activated[...], cotw[...], TN).astype(BF16)
        for i in range(4):
            for j in range(4):
                part = down[128 * i : 128 * i + 128, 128 * j : 128 * j + 128]
                sums[16 + f * 4 + i, 128 * j : 128 * j + 128] = part
        return 0

    lax.fori_loop(0, FF // F_STEP, mlp, 0)

    core, _ = here()

    def send(rows, at, act_on):
        for owner in range(2):
            for block in range(16):
                piece = owner * 16 + block
                slot = slot_of(owner, block)

                def copy_to(out):
                    return pltpu.make_async_copy(
                        sums.at[piece, rows], out.at[slot, rows], sent.at[at, piece]
                    )

                @pl.when(core == owner)
                def _():
                    act_on(copy_to(keep_one))

                @pl.when(core != owner)
                def _():
                    act_on(copy_to(send_one))

    bands, tails = pl.ds(0, BAND_ROWS), pl.ds(BAND_ROWS, PROJ_ROWS)
    send(bands, 0, lambda copy: copy.start())

    def back(part, total):
        rows = pl.ds(pl.multiple_of(part * M_BACK, 16), M_BACK)
        grads = mm(grad_hidden[rows], w_up[...], NT)
        values = normed[rows]
        total = total + jnp.sum(grads * values, 0, keepdims=True)
        residual = cotw[rows].astype(F32) + back_of(grads, gain_two[...], values, inv_two[rows])
        grad_res[rows] = residual
        low = residual.astype(BF16)
        act[rows] = low
        grad_mixed[rows] = mm(low, w_proj[...], NT).astype(BF16)
        return total

    sum_gain[...] = lax.fori_loop(0, ROWS // M_BACK, back, jnp.zeros((1, D), F32))
    proj = mm(mix[...], act[...], TN).astype(BF16)
    for j in range(4):
        at = slice(BAND_ROWS + 16 * j, BAND_ROWS + 16 * j + 16)
        sums[:, at] = proj[:, 128 * j : 128 * j + 128].reshape(PIECES, 16, 128)
    send(tails, 1, lambda copy: copy.start())
    send(bands, 0, lambda copy: copy.wait())
    send(tails, 1, lambda copy: copy.wait())


def first_back_kernel(qkv, probs, grad_mixed, grad_qkv, bias):
    window_back(qkv, probs, grad_mixed, grad_qkv, bias, None)


def second_back_kernel(
    qkv, probs, grad_mixed, act_t, sum_gain_two, bias_before, grads_before,
    grad_qkv, keep_two, send_two,
    grads_all, bias, flat,
):
    step = pl.program_id(0)

    @pl.when(step == 0)
    def _():
        grads_all[0 : ROWS // 2] = grads_before[...]

    window_back(qkv, probs, grad_mixed, grad_qkv, bias, bias_before)
    size = G_BACKWARD * WT
    at = pl.multiple_of(ROWS // 2 + step * size, 16)
    grads_all[pl.ds(at, size)] = grad_qkv[...]

    @pl.when(step == WINDOWS // 2 // G_BACKWARD - 1)
    def _():
        for n in range(QKV // 512):
            part = mm(act_t[...], grads_all[:, 512 * n : 512 * n + 512]).astype(BF16)
            for j in range(4):
                at = (n * 4 + j) * 16
                flat[:, at : at + 16] = part[:, 128 * j : 128 * j + 128].reshape(PIECES, 16, 128)
        gains = [sum_gain_two[:, 128 * j : 128 * j + 128] for j in range(4)]
        gains = jnp.concatenate(gains + [jnp.zeros((12, 128), F32)], 0)
        rest = [bias[block].astype(BF16) for block in range(HEADS + 1)] + [gains.astype(BF16)]
        rest.append(jnp.zeros((PIECES * REST_ROWS - GAIN_AT - 16, 128), BF16))
        rest = jnp.concatenate(rest, 0)
        flat[:, QKV_ROWS:TWO_ROWS] = rest.reshape(PIECES, REST_ROWS, 128)
        core, _ = here()
        for owner in range(2):
            for block in range(16):
                slot = slot_of(owner, block)
                piece = flat[owner * 16 + block]

                @pl.when(core == owner)
                def _():
                    keep_two[slot] = piece

                @pl.when(core != owner)
                def _():
                    send_two[slot] = piece


def window_back(qkv, probs, grad_mixed, grad_qkv, bias, bias_before):
    step = pl.program_id(0)
    first, halves, tail = head_masks()
    tail_low = tail.astype(BF16)

    @pl.when(step == 0)
    def _():
        bias[...] = jnp.zeros_like(bias) if bias_before is None else bias_before[...]

    group = range(G_BACKWARD)
    heads = [(i, head) for i in group for head in range(HEADS)]
    rows = [slice(i * WT, i * WT + WT) for i in group]
    main = [slice(i * WT, i * WT + 128) for i in group]
    last = [slice(i * WT + 128, i * WT + WT) for i in group]
    key = [qkv[r, D : 2 * D] for r in rows]
    val = [qkv[r, 2 * D : 3 * D] for r in rows]
    query_tail = [tiled(qkv[r, 0:D]) * tail_low for r in last]
    out_tail = [tiled(grad_mixed[r]) * tail_low for r in last]
    query = [qkv[main[i], pair_of(head)] * halves[head % 2] for i, head in heads]
    out = [grad_mixed[main[i], pair_of(head)] * halves[head % 2] for i, head in heads]

    tail_probs = [mm(v, o, NT) for v, o in zip(val, out_tail)]
    grad_probs = [mm(val[i][:, pair_of(head)], o, NT) for o, (i, head) in zip(out, heads)]

    def score_grads(low_probs, grad_probs):
        weights = low_probs.astype(F32)
        product = grad_probs * weights
        return product - weights * jnp.sum(product, 0, keepdims=True)

    tail_low_probs = [probs[i, HEADS] for i in group]
    low_probs = [probs[i, head] for i, head in heads]
    tail_grads = [score_grads(p, g) for p, g in zip(tail_low_probs, tail_probs)]
    grads = [score_grads(p, g) for p, g in zip(low_probs, grad_probs)]
    bias[HEADS] += sum(tail_grads[1:], tail_grads[0])
    for head in range(HEADS):
        mine = grads[head::HEADS]
        bias[head] += sum(mine[1:], mine[0])
    tail_grads = [g.astype(BF16) for g in tail_grads]
    grads = [g.astype(BF16) for g in grads]

    query_last = [mm(g, k, TN) for g, k in zip(tail_grads, key)]
    key_more = [mm(g, q) for g, q in zip(tail_grads, query_tail)]
    val_more = [mm(p, o) for p, o in zip(tail_low_probs, out_tail)]
    query_parts = [mm(g, key[i][:, pair_of(head)], TN) for g, (i, head) in zip(grads, heads)]
    key_parts = [mm(g, q) for g, q in zip(grads, query)]
    val_parts = [mm(p, o) for p, o in zip(low_probs, out)]
    for i in group:
        grad_qkv[last[i], 0:D] = (tail_sum(query_last[i], tail) * 0.125).astype(BF16)
    for n, (i, head) in enumerate(heads):
        if head % 2:
            continue
        cols = pair_of(head)
        at = head // 2 * 128
        part = jnp.where(first, query_parts[n], query_parts[n + 1]) * 0.125
        grad_qkv[main[i], cols] = part.astype(BF16)
        part = (key_parts[n] + key_parts[n + 1] + key_more[i][:, cols]) * 0.125
        grad_qkv[rows[i], D + at : D + at + 128] = part.astype(BF16)
        part = val_parts[n] + val_parts[n + 1] + val_more[i][:, cols]
        grad_qkv[rows[i], 2 * D + at : 2 * D + at + 128] = part.astype(BF16)

def branch_kernel(xw, grads_first, grads_second, grad_res, w_qkv, gain_one, main, lon, lat, both, wide, line):
    for part, grad_qkv in enumerate((grads_first, grads_second)):
        rows = slice(part * ROWS // 2, (part + 1) * ROWS // 2)
        values, inv_std = stats_of(xw[rows].astype(F32))
        grads = mm(grad_qkv[...], w_qkv[...], NT)
        low = back_of(grads, gain_one[...], values, inv_std).astype(BF16)
        wide[rows] = grad_res[rows] + low.astype(F32)

    for level in range(LEVELS):
        for row in range(HEIGHT):
            for column in range(4):
                at = run_at(level, row, column)
                line[WLON * column : WLON * column + WLON] = wide[at : at + WLON]
            inner, outer = (main, lon) if row < HEIGHT - WLAT // 2 else (lat, both)
            at = row if row < HEIGHT - WLAT // 2 else row - (HEIGHT - WLAT // 2)
            inner[level, at] = line[0 : BREADTH - 6].astype(BF16)
            outer[level, at] = line[BREADTH - 6 : BREADTH].astype(BF16)


def write_bands(scale, owner, pieces, up_out, down_out, buffer_up, buffer_down, sent):
    depth = buffer_up.shape[0]

    def run(buffer, rows, fill, out):
        def copy(n, block):
            at = pl.ds(pl.multiple_of(block * rows, rows), rows)
            return pltpu.make_async_copy(buffer.at[n % depth], out.at[at], sent.at[n % depth])

        for n in range(16):
            block = block_at(owner, n // 4, n % 4)
            if n >= depth:
                copy(n, block).wait()
            fill(n)
            copy(n, block).start()
        for n in range(16 - depth, 16):
            copy(n, block_at(owner, n // 4, n % 4)).wait()

    def fill_up(n):
        for j in range(16):
            part = pieces[n // 4][n % 4, 32 * j : 32 * j + 32]
            buffer_up[n % depth, :, 128 * j : 128 * j + 128] = part.astype(F32) * scale

    def fill_down(n):
        for j in range(4):
            part = pieces[n // 4][n % 4, 128 * j : 128 * j + 128]
            buffer_down[n % depth, :, 128 * j : 128 * j + 128] = part.astype(F32) * scale

    @pl.when(owner == 0)
    def _():
        run(buffer_up, 32, fill_up, up_out)

    @pl.when(owner == 1)
    def _():
        run(buffer_down, 128, fill_down, down_out)


def finish_own_kernel(scale, *refs):
    pieces, (up_out, down_out, buffer_up, buffer_down, sent) = refs[:4], refs[4:]
    write_bands(scale, here()[0], pieces, up_out, down_out, buffer_up, buffer_down, sent)


def finish_kernel(scale, *refs):
    own, other, (up_in, down_in, w_qkv, gain_vec) = refs[:4], refs[4:8], refs[8:12]
    up_out, down_out, qkv, proj, bias, gain_one, gain_two = refs[12:19]
    buffer_up, buffer_down, sent, rest, sums = refs[19:]
    core, _ = here()
    write_bands(scale, 1 - core, other, up_out, down_out, buffer_up, buffer_down, sent)
    for owner, pieces in ((core, own), (1 - core, other)):
        for n in range(16):
            piece = owner * 16 + block_at(owner, n // 4, n % 4)
            rows = pl.ds(pl.multiple_of(piece * 16, 16), 16)
            held = pieces[n // 4]
            for j in range(4):
                at = BAND_ROWS + 16 * j
                part = held[n % 4, at : at + 16].astype(F32) * scale
                proj[rows, 128 * j : 128 * j + 128] = part
            total = jnp.zeros((16, 128), F32)
            for j in range(12):
                cols = slice(128 * j, 128 * j + 128)
                at = ONE_ROWS + 16 * j
                part = held[n % 4, at : at + 16].astype(F32) * scale
                qkv[rows, cols] = part
                total = total + part * w_qkv[rows, cols].astype(F32)
            sums[rows] = total
            rest[piece] = held[n % 4, ONE_ROWS + QKV_ROWS : ALL_ROWS]
    gain_one[...] = jnp.sum(sums[...].T, 0, keepdims=True) / gain_vec[...]
    flat = rest[...].reshape(PIECES * REST_ROWS, 128).astype(F32)
    last = flat[HEADS * WT : GAIN_AT].T * (scale * WT)
    for head in range(HEADS):
        bias[head, 0:128] = flat[head * WT : head * WT + WT].T * (scale * WT)
        bias[head, 128:WT] = last[16 * head : 16 * head + 16]
    for j in range(4):
        part = flat[GAIN_AT + j : GAIN_AT + j + 1] * scale
        gain_two[:, 128 * j : 128 * j + 128] = part


def shape(*dims, dtype=BF16):
    return jax.ShapeDtypeStruct(dims, dtype)


def params(mib):
    return pltpu.CompilerParams(vmem_limit_bytes=mib * MIB)


def vmem(*dims, dtype=BF16):
    return pltpu.VMEM(dims, dtype)


def cost(flops, moved):
    return pl.CostEstimate(flops=flops, bytes_accessed=moved, transcendentals=0)


ANY = pl.BlockSpec(memory_space=pl.ANY)
INSIDE = pl.BlockSpec(memory_space=pltpu.VMEM)
SCALARS = pl.BlockSpec(memory_space=pltpu.SMEM)


def pack(grid):
    edge, top = WLON // 2, WLAT // 2
    return pl.pallas_call(
        pack_kernel,
        out_shape=(
            shape(LEVELS, HEIGHT, edge, D), shape(LEVELS, top, BREADTH, D),
            shape(LEVELS, top, edge, D),
        ),
        in_specs=[INSIDE],
        out_specs=[INSIDE] * 3,
        compiler_params=params(16),
        name="pack",
    )(grid)


def attention(*operands):
    return pl.pallas_call(
        attention_kernel,
        out_shape=(
            shape(ROWS, D), shape(ROWS, D), shape(D, ROWS), shape(ROWS, QKV),
            shape(WINDOWS, HEADS + 1, WT, 128),
        ),
        in_specs=[INSIDE] * len(operands),
        out_specs=[INSIDE, INSIDE, INSIDE, ANY, ANY],
        scratch_shapes=[
            vmem(56, D, dtype=F32), vmem(ROWS, D, dtype=F32), vmem(ROWS, D), vmem(ROWS, QKV),
            vmem(WINDOWS, HEADS + 1, WT, 128), vmem(2, HEADS + 1, WT, 128, dtype=F32),
            pltpu.SemaphoreType.DMA((WINDOWS + 1,)),
        ],
        compiler_params=params(48),
        cost_estimate=cost(ROWS * D * QKV * 2 * 4, 20_000_000),
        name="attention",
    )(*operands)


def mlp_call(*operands):
    return pl.pallas_call(
        mlp_kernel,
        out_shape=(
            shape(ROWS, D), shape(ROWS, D, dtype=F32), shape(16, ONE_ROWS, 128),
            shape(16, ONE_ROWS, 128), shape(1, D, dtype=F32),
        ),
        in_specs=[INSIDE] * 7 + [ANY, ANY, INSIDE],
        out_specs=[INSIDE, INSIDE, ANY, ANY, INSIDE],
        scratch_shapes=[
            vmem(56, D, dtype=F32), vmem(ROWS, D, dtype=F32), vmem(ROWS, D), vmem(ROWS, D),
            vmem(ROWS, D, dtype=F32), vmem(ROWS, 1, dtype=F32), vmem(D, ROWS),
            vmem(ROWS, F_STEP), vmem(ROWS, FF), vmem(PIECES, ONE_ROWS, 128),
            vmem(D, FF), vmem(FF, D),
            pltpu.SemaphoreType.DMA((2,)), pltpu.SemaphoreType.DMA((2, PIECES)),
        ],
        compiler_params=params(56),
        cost_estimate=cost(ROWS * D * FF * 2 * 8, 40_000_000),
        name="mlp",
    )(*operands)


def back_specs(half):
    start = half * (WINDOWS // 2 // G_BACKWARD)
    return [
        pl.BlockSpec((G_BACKWARD * WT, QKV), lambda i: (start + i, 0)),
        pl.BlockSpec((G_BACKWARD, HEADS + 1, WT, 128), lambda i: (start + i, 0, 0, 0)),
        pl.BlockSpec((G_BACKWARD * WT, D), lambda i: (start + i, 0)),
    ]


def first_back(qkv, probs, grad_mixed):
    return pl.pallas_call(
        first_back_kernel,
        out_shape=(shape(ROWS // 2, QKV), shape(HEADS + 1, WT, 128, dtype=F32)),
        grid=(WINDOWS // 2 // G_BACKWARD,),
        in_specs=back_specs(0),
        out_specs=[
            pl.BlockSpec((G_BACKWARD * WT, QKV), lambda i: (i, 0)),
            pl.BlockSpec((HEADS + 1, WT, 128), lambda i: (0, 0, 0)),
        ],
        compiler_params=params(32),
        cost_estimate=cost(ROWS * D * QKV * 2 * 3, 10_000_000),
        name="first_back",
    )(qkv, probs, grad_mixed)


def second_back(*operands):
    return pl.pallas_call(
        second_back_kernel,
        out_shape=(
            shape(ROWS // 2, QKV), shape(16, TWO_ROWS, 128), shape(16, TWO_ROWS, 128),
        ),
        grid=(WINDOWS // 2 // G_BACKWARD,),
        in_specs=back_specs(1) + [INSIDE] * 4,
        out_specs=[pl.BlockSpec((G_BACKWARD * WT, QKV), lambda i: (i, 0)), INSIDE, INSIDE],
        scratch_shapes=[
            vmem(ROWS, QKV), vmem(HEADS + 1, WT, 128, dtype=F32), vmem(PIECES, TWO_ROWS, 128),
        ],
        compiler_params=params(40),
        cost_estimate=cost(ROWS * D * QKV * 2 * 4, 10_000_000),
        name="second_back",
    )(*operands)


def branch(*operands):
    return pl.pallas_call(
        branch_kernel,
        out_shape=(
            shape(LEVELS, 9, 42, D), shape(LEVELS, 9, 6, D), shape(LEVELS, 3, 42, D),
            shape(LEVELS, 3, 6, D),
        ),
        in_specs=[INSIDE] * len(operands),
        out_specs=[INSIDE] * 4,
        scratch_shapes=[vmem(ROWS, D, dtype=F32), vmem(48, D, dtype=F32)],
        compiler_params=params(24),
        cost_estimate=cost(ROWS * D * QKV * 2 * 4, 10_000_000),
        name="branch",
    )(*operands)


BUFFERS = 4


def finish_scratch():
    return [
        vmem(BUFFERS, 32, FF, dtype=F32), vmem(BUFFERS, 128, D, dtype=F32),
        pltpu.SemaphoreType.DMA((BUFFERS,)),
    ]


def finish_own(pieces, scale):
    return pl.pallas_call(
        functools.partial(finish_own_kernel, scale),
        out_shape=(shape(D, FF, dtype=F32), shape(FF, D, dtype=F32)),
        in_specs=[INSIDE] * 4,
        out_specs=[ANY, ANY],
        scratch_shapes=finish_scratch(),
        compiler_params=params(24),
        cost_estimate=cost(10_000_000, 10_000_000),
        name="finish_own",
    )(*pieces)


def finish(own, other, up, down, w_qkv, gain_one, scale):
    return pl.pallas_call(
        functools.partial(finish_kernel, scale),
        out_shape=(
            shape(D, FF, dtype=F32), shape(FF, D, dtype=F32), shape(D, QKV, dtype=F32),
            shape(D, D, dtype=F32), shape(HEADS, WT, WT, dtype=F32), shape(1, D, dtype=F32),
            shape(1, D, dtype=F32),
        ),
        in_specs=[INSIDE] * 8 + [ANY, ANY, INSIDE, INSIDE],
        out_specs=[ANY, ANY] + [INSIDE] * 5,
        input_output_aliases={8: 0, 9: 1},
        scratch_shapes=finish_scratch() + [vmem(PIECES, REST_ROWS, 128), vmem(D, 128, dtype=F32)],
        compiler_params=params(40),
        cost_estimate=cost(10_000_000, 20_000_000),
        name="finish",
    )(*own, *other, up, down, w_qkv, gain_one)


def neighbour(array, lat_by, lon_by):
    lat_count, lon_count = lax.axis_size("lat"), lax.axis_size("lon")
    pairs = []
    for i in range(lat_count):
        for j in range(lon_count):
            to = ((i + lat_by) % lat_count) * lon_count + (j + lon_by) % lon_count
            pairs.append((i * lon_count + j, to))
    return lax.ppermute(array, ("lat", "lon"), pairs)


def halos(grid):
    lon, lat, both = pack(grid)
    return neighbour(lat, -1, 0), neighbour(lon, 0, -1), neighbour(both, -1, -1)


def send_home(main, lon, lat, both):
    return main, neighbour(lon, 0, 1), neighbour(lat, 1, 0), neighbour(both, 1, 1)


def assemble(main, lon, lat, both):
    upper = jnp.concatenate([both, lat], 2)
    lower = jnp.concatenate([lon, main], 2)
    return jnp.concatenate([upper, lower], 1)


def along(array, stage, by):
    pairs = []
    for lat in range(16):
        for lon in range(8):
            core, chip = position(lat, lon)
            chip = list(chip)
            axis = ORDERS[core][stage]
            chip[axis] = (chip[axis] + by) % 4
            x, y, z = chip
            to = (z * 4 + y // 2 * 2 + core) * 8 + x * 2 + y % 2
            pairs.append((lat * 8 + lon, to))
    return lax.ppermute(array, ("lat", "lon"), pairs)


def other_core(array):
    return lax.ppermute(array, "lat", [(i, i ^ 1) for i in range(16)])


def added(*terms):
    total = terms[0].astype(F32)
    for term in terms[1:]:
        total = total + term.astype(F32)
    return total.astype(BF16)


def after(value, *others):
    return lax.optimization_barrier((value, others))[0]


def core_sum(keep, send):
    return added(keep, other_core(send))


def first_sum(held):
    return added(held[:4], *[along(held[4 * k : 4 * k + 4], 0, k) for k in (1, 2, 3)])


def second_sum(held):
    return added(held[0], *[along(held[k], 1, k) for k in (1, 2, 3)])


def last_sum(share):
    share = lax.optimization_barrier(share)
    one, two, three = [along(share, 2, k).astype(F32) for k in (1, 2, 3)]
    return ((share.astype(F32) + two) + (one + three)).astype(BF16)


def spread(share, before):
    held = jnp.stack([share] + [along(share, 1, k) for k in (1, 2, 3)])
    held = after(held, before)
    own = [held] + [along(held, 0, k) for k in (1, 2, 3)]
    return own, [other_core(piece) for piece in own]


def local(tokens, cotangent, w_qkv, w_proj, w_up, w_down, pair_bias, gain_one, gain_two):
    total_tokens = ROWS * lax.axis_size("lat") * lax.axis_size("lon")
    scale = total_tokens ** (-0.5)
    gain_one = gain_one.reshape(1, D)
    gain_two = gain_two.reshape(1, D)
    lat_edge, lon_edge, corner = halos(tokens)
    cot_lat, cot_lon, cot_corner = halos(cotangent)
    xw, mix, act_t, qkv, probs = attention(
        tokens, lon_edge, lat_edge, corner, w_qkv, pair_bias, gain_one
    )
    grad_mixed, grad_res, keep_one, send_one, sum_gain_two = mlp_call(
        xw, mix, cotangent, cot_lon, cot_lat, cot_corner, w_proj, w_up, w_down, gain_two
    )
    grads_first, bias = first_back(qkv, probs, grad_mixed)
    held_one = core_sum(keep_one, send_one)
    grads_second, keep_two, send_two = second_back(
        qkv, probs, grad_mixed, act_t, sum_gain_two, after(bias, held_one), grads_first
    )
    held_one = first_sum(held_one)
    held_two = first_sum(core_sum(keep_two, after(send_two, held_one)))
    share = second_sum(jnp.concatenate([held_one, held_two], 1))
    home = branch(xw, after(grads_first, share), grads_second, grad_res, w_qkv, gain_one)
    share = after(last_sum(share), home)
    home = send_home(*home)
    own, other = spread(share, home)
    up, down = finish_own(own, scale)
    sum_up, sum_down, sum_qkv, sum_proj, sum_bias, sum_one, sum_two = finish(
        own, other, up, down, w_qkv, gain_one, scale
    )
    return (
        assemble(*[after(piece, up) for piece in home]),
        sum_qkv,
        sum_proj,
        sum_up,
        sum_down,
        sum_bias,
        sum_one.reshape(D),
        sum_two.reshape(D),
    )


def solution(mesh):
    grid = P(None, "lat", "lon", None)
    in_specs = (grid, grid, P(), P(), P(), P(), P(), P(), P())
    out_specs = (grid, P(), P(), P(), P(), P(), P(), P())
    return jax.shard_map(local, mesh=mesh, in_specs=in_specs, out_specs=out_specs, check_vma=False)
```

```python
import functools

import jax
import jax.numpy as jnp
from jax import lax
from jax.experimental import pallas as pl
from jax.experimental.pallas import tpu as pltpu
from jax.sharding import PartitionSpec as P

HEADS = 8
WLAT = 6
WLON = 12
WT = 144
D = 512
QKV = 1536
FF = 2048
LEVELS = 2
HEIGHT = 12
BREADTH = 48
WINDOWS = 8
ROWS = WINDOWS * WT
EPSILON = 1e-05
MASKED = -1e30
F32 = jnp.float32
BF16 = jnp.bfloat16
PIECES = 32
BAND_ROWS = 512
PROJ_ROWS = 64
ONE_ROWS = BAND_ROWS + PROJ_ROWS
QKV_ROWS = 192
REST_ROWS = 48
TWO_ROWS = QKV_ROWS + REST_ROWS
ALL_ROWS = ONE_ROWS + TWO_ROWS
GAIN_AT = (HEADS + 1) * WT
MIB = 1024 * 1024
M_NORM = 576
M_UP = 1152
M_BACK = 576
M_BRANCH = 576
G_FORWARD = 4
G_BACKWARD = 2
F_STEP = 512

NN = (((1,), (0,)), ((), ()))
NT = (((1,), (1,)), ((), ()))
TN = (((0,), (0,)), ((), ()))


def mm(a, b, dims=NN):
    return lax.dot_general(a, b, dims, preferred_element_type=F32)


def stats_of(values):
    average = jnp.mean(values, -1, keepdims=True)
    centred = values - average
    variance = jnp.mean(centred * centred, -1, keepdims=True)
    inv_std = lax.rsqrt(variance + EPSILON)
    return centred * inv_std, inv_std


def back_of(grad_out, gain_vec, normed, inv_std):
    scaled = grad_out * gain_vec
    return (
        scaled
        - jnp.mean(scaled, -1, keepdims=True)
        - normed * jnp.mean(scaled * normed, -1, keepdims=True)
    ) * inv_std


def run_at(level, row, column):
    window = (row // WLAT) * 4 + column
    return window * WT + level * (WT // 2) + (row % WLAT) * WLON


def gather_windows(main_ref, lon_ref, lat_ref, both_ref, line, wide, out_ref):
    for level in range(LEVELS):
        for row in range(HEIGHT):
            if row < HEIGHT - WLAT // 2:
                line[0:BREADTH] = main_ref[level, row + WLAT // 2].astype(F32)
                line[BREADTH : BREADTH + 6] = lon_ref[level, row + WLAT // 2].astype(F32)
            else:
                line[0:BREADTH] = lat_ref[level, row - (HEIGHT - WLAT // 2)].astype(F32)
                line[BREADTH : BREADTH + 6] = both_ref[level, row - (HEIGHT - WLAT // 2)].astype(F32)
            for column in range(4):
                at = run_at(level, row, column)
                wide[at : at + WLON] = line[6 + WLON * column : 18 + WLON * column]

    def narrow(window, _):
        rows = pl.ds(pl.multiple_of(window * WT, 16), WT)
        out_ref[rows] = wide[rows].astype(BF16)
        return 0

    lax.fori_loop(0, WINDOWS, narrow, 0)


def position(lat, lon):
    return lat % 2, (lon // 2, (lat // 2) % 2 * 2 + lon % 2, lat // 4)


ORDERS = ((0, 1, 2), (1, 2, 0))


def here():
    return position(lax.axis_index("lat"), lax.axis_index("lon"))


def slot_of(core, block):
    _, chip = here()
    first, second = chip[ORDERS[core][0]], chip[ORDERS[core][1]]
    return (block // 4 + 4 - first) % 4 * 4 + (block % 4 + 4 - second) % 4


def block_at(core, first_by, second_by):
    _, chip = here()
    first = jnp.where(core == 0, chip[ORDERS[0][0]], chip[ORDERS[1][0]])
    second = jnp.where(core == 0, chip[ORDERS[0][1]], chip[ORDERS[1][1]])
    return (first + 4 - first_by) % 4 * 4 + (second + 4 - second_by) % 4


def window_rows(window):
    return pl.ds(pl.multiple_of(window * WT, 16), WT)


def softmax_first(scores):
    top = jnp.max(scores, 0, keepdims=True)
    exponent = jnp.exp(scores - top)
    total = jnp.sum(exponent, 0, keepdims=True)
    return (exponent * (1.0 / total)).astype(BF16)


def head_masks():
    lane = lax.broadcasted_iota(jnp.int32, (1, 128), 1)
    first = lane < 64
    row = lax.broadcasted_iota(jnp.int32, (128, D), 0) // 16
    column = lax.broadcasted_iota(jnp.int32, (128, D), 1) // 64
    halves = (first.astype(F32).astype(BF16), (lane >= 64).astype(F32).astype(BF16))
    return first, halves, (row == column).astype(F32)


def tiled(block):
    return jnp.concatenate([block] * HEADS, 0)


def pair_of(head):
    return slice(head // 2 * 128, head // 2 * 128 + 128)


def tail_sum(block, tail):
    return jnp.sum((block * tail).reshape(HEADS, 16, D), 0)


def pack_kernel(ref, lon, lat, both):
    edge, top = WLON // 2, WLAT // 2
    lat[...] = ref[:, :top]
    for level in range(LEVELS):
        for row in range(HEIGHT):
            lon[level, row] = ref[level, row, :edge]
        for row in range(top):
            both[level, row] = ref[level, row, :edge]


def attention_kernel(
    tok, tok_lon, tok_lat, tok_both, w_qkv, pair_bias, gain_one,
    xw_out, mix_out, act_t_out, qkv_out, probs_out,
    line, wide, act, qkv, probs, bias, xw, mix, act_t, sent,
):
    gather_windows(tok, tok_lon, tok_lat, tok_both, line, wide, xw)
    copies = [pltpu.make_async_copy(xw, xw_out, sent.at[WINDOWS + 1])]
    copies[0].start()

    def norm_one(window, _):
        rows = window_rows(window)
        values, _ = stats_of(xw[rows].astype(F32))
        act[rows] = (values * gain_one[...]).astype(BF16)
        return 0

    lax.fori_loop(0, WINDOWS, norm_one, 0)

    def project(n, _):
        cols = pl.ds(pl.multiple_of(n * 256, 256), 256)
        qkv[:, cols] = mm(act[...], w_qkv[:, cols]).astype(BF16)
        return 0

    lax.fori_loop(0, QKV // 256, project, 0)
    act_t[...] = act[...].T
    copies.append(pltpu.make_async_copy(qkv, qkv_out, sent.at[WINDOWS]))
    copies.append(pltpu.make_async_copy(act_t, act_t_out, sent.at[WINDOWS + 2]))
    for copy in copies[1:]:
        copy.start()

    is_last = lax.axis_index("lat") == lax.axis_size("lat") - 1
    key_at = lax.broadcasted_iota(jnp.int32, (WT, 128), 0)
    query_at = lax.broadcasted_iota(jnp.int32, (WT, 128), 1)

    def masked(query_at):
        apart = (key_at // WLON % WLAT >= WLAT // 2) != (query_at // WLON % WLAT >= WLAT // 2)
        return jnp.where(apart & is_last, MASKED, 0.0)

    mask_main = masked(query_at)
    mask_tail = masked(128 + query_at % 16)
    for head in range(HEADS):
        block = pair_bias[head, 0:128].T
        bias[0, head] = block
        bias[1, head] = block + mask_main
    block = jnp.concatenate([pair_bias[head, 128:WT] for head in range(HEADS)], 0).T
    bias[0, HEADS] = block
    bias[1, HEADS] = block + mask_tail

    first, halves, tail = head_masks()
    halves = [half * 0.125 for half in halves]
    tail_low = (tail * 0.125).astype(BF16)

    def mix_copy(group):
        at = pl.ds(pl.multiple_of(group * G_FORWARD * WT, 16), G_FORWARD * WT)
        return pltpu.make_async_copy(mix.at[at], mix_out.at[at], sent.at[WINDOWS + 3 + group])

    def attend(group, _):
        windows = [group * G_FORWARD + i for i in range(G_FORWARD)]
        heads = [(i, head) for i in range(G_FORWARD) for head in range(HEADS)]
        rows = [window_rows(window) for window in windows]
        main = [pl.ds(pl.multiple_of(window * WT, 16), 128) for window in windows]
        last = [pl.ds(pl.multiple_of(window * WT + 128, 16), 16) for window in windows]
        key = [qkv[r, D : 2 * D] for r in rows]
        val = [qkv[r, 2 * D : 3 * D] for r in rows]
        tail_scores = [
            mm(k, tiled(qkv[r, 0:D]) * tail_low, NT) for k, r in zip(key, last)
        ]
        scores = [
            mm(key[i][:, pair_of(head)], qkv[main[i], pair_of(head)] * halves[head % 2], NT)
            for i, head in heads
        ]
        tail_weights = [
            softmax_first(t + bias[window // 4, HEADS]) for t, window in zip(tail_scores, windows)
        ]
        weights = [
            softmax_first(t + bias[windows[i] // 4, head]) for t, (i, head) in zip(scores, heads)
        ]
        tail_mixed = [mm(w, v, TN) for w, v in zip(tail_weights, val)]
        mixed = [mm(w, val[i][:, pair_of(head)], TN) for w, (i, head) in zip(weights, heads)]
        for i, window in enumerate(windows):
            probs[window, HEADS] = tail_weights[i]
            mix[last[i]] = tail_sum(tail_mixed[i], tail).astype(BF16)
        for w, (i, head) in zip(weights, heads):
            probs[windows[i], head] = w
        for n, (i, head) in enumerate(heads):
            if head % 2 == 0:
                mix[main[i], pair_of(head)] = jnp.where(first, mixed[n], mixed[n + 1]).astype(BF16)
        for window in windows:
            pltpu.make_async_copy(probs.at[window], probs_out.at[window], sent.at[window]).start()
        mix_copy(group).start()
        return 0

    lax.fori_loop(0, WINDOWS // G_FORWARD, attend, 0)
    for copy in copies + [mix_copy(group) for group in range(WINDOWS // G_FORWARD)]:
        copy.wait()
    for window in range(WINDOWS):
        pltpu.make_async_copy(probs.at[window], probs_out.at[window], sent.at[window]).wait()


def mlp_kernel(
    xw, mix, cot, cot_lon, cot_lat, cot_both, w_proj, w_up_in, w_down_in, gain_two,
    grad_mixed, grad_res, keep_one, send_one, sum_gain,
    line, wide, cotw, act, normed, inv_two, act_t, activated, grad_hidden, sums, w_up, w_down,
    got, sent,
):
    loads = [
        pltpu.make_async_copy(w_up_in, w_up, got.at[0]),
        pltpu.make_async_copy(w_down_in, w_down, got.at[1]),
    ]
    for load in loads:
        load.start()
    gather_windows(cot, cot_lon, cot_lat, cot_both, line, wide, cotw)

    def norm_two(part, _):
        rows = pl.ds(pl.multiple_of(part * M_NORM, 16), M_NORM)
        residual = xw[rows].astype(F32) + mm(mix[rows], w_proj[...])
        values, inv_std = stats_of(residual)
        normed[rows] = values
        inv_two[rows] = inv_std
        act[rows] = (values * gain_two[...]).astype(BF16)
        return 0

    lax.fori_loop(0, ROWS // M_NORM, norm_two, 0)
    act_t[...] = act[...].T
    for load in loads:
        load.wait()

    c0 = 0.7978845608028654
    c1 = c0 * 0.044715

    def mlp(f, _):
        cols = pl.ds(pl.multiple_of(f * F_STEP, F_STEP), F_STEP)

        def rows_of(r, _):
            rows = pl.ds(pl.multiple_of(r * M_UP, 16), M_UP)
            u = mm(act[rows], w_up[:, cols])
            grad_act = mm(cotw[rows], w_down[cols, :], NT)
            square = u * u
            gate = 0.5 + 0.5 * jnp.tanh(u * (c0 + c1 * square))
            value = u * gate
            activated[rows] = value.astype(BF16)
            slope = gate + value * (1.0 - gate) * (2.0 * c0 + 6.0 * c1 * square)
            grad_hidden[rows, cols] = (grad_act * slope).astype(BF16)
            return 0

        lax.fori_loop(0, ROWS // M_UP, rows_of, 0)
        up = mm(act_t[...], grad_hidden[:, cols]).astype(BF16)
        for j in range(4):
            at = pl.ds(pl.multiple_of(f * 128 + 32 * j, 32), 32)
            sums[0:16, at] = up[:, 128 * j : 128 * j + 128].reshape(16, 32, 128)
        down = mm(activated[...], cotw[...], TN).astype(BF16)
        for i in range(4):
            for j in range(4):
                part = down[128 * i : 128 * i + 128, 128 * j : 128 * j + 128]
                sums[16 + f * 4 + i, 128 * j : 128 * j + 128] = part
        return 0

    lax.fori_loop(0, FF // F_STEP, mlp, 0)

    core, _ = here()

    def send(rows, at, act_on):
        for owner in range(2):
            for block in range(16):
                piece = owner * 16 + block
                slot = slot_of(owner, block)

                def copy_to(out):
                    return pltpu.make_async_copy(
                        sums.at[piece, rows], out.at[slot, rows], sent.at[at, piece]
                    )

                @pl.when(core == owner)
                def _():
                    act_on(copy_to(keep_one))

                @pl.when(core != owner)
                def _():
                    act_on(copy_to(send_one))

    bands, tails = pl.ds(0, BAND_ROWS), pl.ds(BAND_ROWS, PROJ_ROWS)
    send(bands, 0, lambda copy: copy.start())

    def back(part, total):
        rows = pl.ds(pl.multiple_of(part * M_BACK, 16), M_BACK)
        grads = mm(grad_hidden[rows], w_up[...], NT)
        values = normed[rows]
        total = total + jnp.sum(grads * values, 0, keepdims=True)
        residual = cotw[rows].astype(F32) + back_of(grads, gain_two[...], values, inv_two[rows])
        grad_res[rows] = residual
        low = residual.astype(BF16)
        act[rows] = low
        grad_mixed[rows] = mm(low, w_proj[...], NT).astype(BF16)
        return total

    sum_gain[...] = lax.fori_loop(0, ROWS // M_BACK, back, jnp.zeros((1, D), F32))
    proj = mm(mix[...], act[...], TN).astype(BF16)
    for j in range(4):
        at = slice(BAND_ROWS + 16 * j, BAND_ROWS + 16 * j + 16)
        sums[:, at] = proj[:, 128 * j : 128 * j + 128].reshape(PIECES, 16, 128)
    send(tails, 1, lambda copy: copy.start())
    send(bands, 0, lambda copy: copy.wait())
    send(tails, 1, lambda copy: copy.wait())


def first_back_kernel(qkv, probs, grad_mixed, grad_qkv, bias):
    window_back(qkv, probs, grad_mixed, grad_qkv, bias, None)


def second_back_kernel(
    qkv, probs, grad_mixed, act_t, sum_gain_two, bias_before, grads_before,
    grad_qkv, keep_two, send_two,
    grads_all, bias, flat,
):
    step = pl.program_id(0)

    @pl.when(step == 0)
    def _():
        grads_all[0 : ROWS // 2] = grads_before[...]

    window_back(qkv, probs, grad_mixed, grad_qkv, bias, bias_before)
    size = G_BACKWARD * WT
    at = pl.multiple_of(ROWS // 2 + step * size, 16)
    grads_all[pl.ds(at, size)] = grad_qkv[...]

    @pl.when(step == WINDOWS // 2 // G_BACKWARD - 1)
    def _():
        for n in range(QKV // 512):
            part = mm(act_t[...], grads_all[:, 512 * n : 512 * n + 512]).astype(BF16)
            for j in range(4):
                at = (n * 4 + j) * 16
                flat[:, at : at + 16] = part[:, 128 * j : 128 * j + 128].reshape(PIECES, 16, 128)
        gains = [sum_gain_two[:, 128 * j : 128 * j + 128] for j in range(4)]
        gains = jnp.concatenate(gains + [jnp.zeros((12, 128), F32)], 0)
        rest = [bias[block].astype(BF16) for block in range(HEADS + 1)] + [gains.astype(BF16)]
        rest.append(jnp.zeros((PIECES * REST_ROWS - GAIN_AT - 16, 128), BF16))
        rest = jnp.concatenate(rest, 0)
        flat[:, QKV_ROWS:TWO_ROWS] = rest.reshape(PIECES, REST_ROWS, 128)
        core, _ = here()
        for owner in range(2):
            for block in range(16):
                slot = slot_of(owner, block)
                piece = flat[owner * 16 + block]

                @pl.when(core == owner)
                def _():
                    keep_two[slot] = piece

                @pl.when(core != owner)
                def _():
                    send_two[slot] = piece


def window_back(qkv, probs, grad_mixed, grad_qkv, bias, bias_before):
    step = pl.program_id(0)
    first, halves, tail = head_masks()
    tail_low = tail.astype(BF16)

    @pl.when(step == 0)
    def _():
        bias[...] = jnp.zeros_like(bias) if bias_before is None else bias_before[...]

    group = range(G_BACKWARD)
    heads = [(i, head) for i in group for head in range(HEADS)]
    rows = [slice(i * WT, i * WT + WT) for i in group]
    main = [slice(i * WT, i * WT + 128) for i in group]
    last = [slice(i * WT + 128, i * WT + WT) for i in group]
    key = [qkv[r, D : 2 * D] for r in rows]
    val = [qkv[r, 2 * D : 3 * D] for r in rows]
    query_tail = [tiled(qkv[r, 0:D]) * tail_low for r in last]
    out_tail = [tiled(grad_mixed[r]) * tail_low for r in last]
    query = [qkv[main[i], pair_of(head)] * halves[head % 2] for i, head in heads]
    out = [grad_mixed[main[i], pair_of(head)] * halves[head % 2] for i, head in heads]

    tail_probs = [mm(v, o, NT) for v, o in zip(val, out_tail)]
    grad_probs = [mm(val[i][:, pair_of(head)], o, NT) for o, (i, head) in zip(out, heads)]

    def score_grads(low_probs, grad_probs):
        weights = low_probs.astype(F32)
        product = grad_probs * weights
        return product - weights * jnp.sum(product, 0, keepdims=True)

    tail_low_probs = [probs[i, HEADS] for i in group]
    low_probs = [probs[i, head] for i, head in heads]
    tail_grads = [score_grads(p, g) for p, g in zip(tail_low_probs, tail_probs)]
    grads = [score_grads(p, g) for p, g in zip(low_probs, grad_probs)]
    bias[HEADS] += sum(tail_grads[1:], tail_grads[0])
    for head in range(HEADS):
        mine = grads[head::HEADS]
        bias[head] += sum(mine[1:], mine[0])
    tail_grads = [g.astype(BF16) for g in tail_grads]
    grads = [g.astype(BF16) for g in grads]

    query_last = [mm(g, k, TN) for g, k in zip(tail_grads, key)]
    key_more = [mm(g, q) for g, q in zip(tail_grads, query_tail)]
    val_more = [mm(p, o) for p, o in zip(tail_low_probs, out_tail)]
    query_parts = [mm(g, key[i][:, pair_of(head)], TN) for g, (i, head) in zip(grads, heads)]
    key_parts = [mm(g, q) for g, q in zip(grads, query)]
    val_parts = [mm(p, o) for p, o in zip(low_probs, out)]
    for i in group:
        grad_qkv[last[i], 0:D] = (tail_sum(query_last[i], tail) * 0.125).astype(BF16)
    for n, (i, head) in enumerate(heads):
        if head % 2:
            continue
        cols = pair_of(head)
        at = head // 2 * 128
        part = jnp.where(first, query_parts[n], query_parts[n + 1]) * 0.125
        grad_qkv[main[i], cols] = part.astype(BF16)
        part = (key_parts[n] + key_parts[n + 1] + key_more[i][:, cols]) * 0.125
        grad_qkv[rows[i], D + at : D + at + 128] = part.astype(BF16)
        part = val_parts[n] + val_parts[n + 1] + val_more[i][:, cols]
        grad_qkv[rows[i], 2 * D + at : 2 * D + at + 128] = part.astype(BF16)

def branch_kernel(xw, grads_first, grads_second, grad_res, w_qkv, gain_one, main, lon, lat, both, wide, line):
    for part, grad_qkv in enumerate((grads_first, grads_second)):
        rows = slice(part * ROWS // 2, (part + 1) * ROWS // 2)
        values, inv_std = stats_of(xw[rows].astype(F32))
        grads = mm(grad_qkv[...], w_qkv[...], NT)
        low = back_of(grads, gain_one[...], values, inv_std).astype(BF16)
        wide[rows] = grad_res[rows] + low.astype(F32)

    for level in range(LEVELS):
        for row in range(HEIGHT):
            for column in range(4):
                at = run_at(level, row, column)
                line[WLON * column : WLON * column + WLON] = wide[at : at + WLON]
            inner, outer = (main, lon) if row < HEIGHT - WLAT // 2 else (lat, both)
            at = row if row < HEIGHT - WLAT // 2 else row - (HEIGHT - WLAT // 2)
            inner[level, at] = line[0 : BREADTH - 6].astype(BF16)
            outer[level, at] = line[BREADTH - 6 : BREADTH].astype(BF16)


def write_pieces(scale, owner, pieces, w_qkv, outs, sums, rest, buffers, sent):
    up_out, down_out, qkv_out, proj_out = outs
    buffer_up, buffer_down, buffer_qkv, buffer_proj = buffers

    def run(buffer_band, band, fill_band, band_out):
        def copies(n):
            block = block_at(owner, n // 4, n % 4)
            piece = owner * 16 + block
            slot = n % BUFFERS
            targets = ((buffer_band, band_out, band, block), (buffer_qkv, qkv_out, 16, piece),
                       (buffer_proj, proj_out, 16, piece))
            return [
                pltpu.make_async_copy(
                    buffer.at[slot],
                    out.at[pl.ds(pl.multiple_of(at * size, size), size)],
                    sent.at[i, slot],
                )
                for i, (buffer, out, size, at) in enumerate(targets)
            ]

        for n in range(16):
            if n >= BUFFERS:
                for copy in copies(n - BUFFERS):
                    copy.wait()
            slot = n % BUFFERS
            piece = owner * 16 + block_at(owner, n // 4, n % 4)
            rows = pl.ds(pl.multiple_of(piece * 16, 16), 16)
            held = pieces[n // 4]
            fill_band(held, n % 4, slot)
            for j in range(4):
                at = BAND_ROWS + 16 * j
                part = held[n % 4, at : at + 16].astype(F32) * scale
                buffer_proj[slot, :, 128 * j : 128 * j + 128] = part
            total = jnp.zeros((16, 128), F32)
            for j in range(12):
                cols = slice(128 * j, 128 * j + 128)
                at = ONE_ROWS + 16 * j
                part = held[n % 4, at : at + 16].astype(F32) * scale
                buffer_qkv[slot, :, cols] = part
                total = total + part * w_qkv[rows, cols].astype(F32)
            sums[rows] = total
            rest[piece] = held[n % 4, ONE_ROWS + QKV_ROWS : ALL_ROWS]
            for copy in copies(n):
                copy.start()
        for n in range(16 - BUFFERS, 16):
            for copy in copies(n):
                copy.wait()

    def fill_up(held, at, slot):
        for j in range(16):
            part = held[at, 32 * j : 32 * j + 32].astype(F32) * scale
            buffer_up[slot, :, 128 * j : 128 * j + 128] = part

    def fill_down(held, at, slot):
        for j in range(4):
            part = held[at, 128 * j : 128 * j + 128].astype(F32) * scale
            buffer_down[slot, :, 128 * j : 128 * j + 128] = part

    @pl.when(owner == 0)
    def _():
        run(buffer_up, 32, fill_up, up_out)

    @pl.when(owner == 1)
    def _():
        run(buffer_down, 128, fill_down, down_out)


def finish_own_kernel(scale, *refs):
    pieces, w_qkv, outs, sums, rest = refs[:4], refs[4], refs[5:9], refs[9], refs[10]
    write_pieces(scale, here()[0], pieces, w_qkv, outs, sums, rest, refs[11:15], refs[15])


def finish_kernel(scale, *refs):
    pieces, w_qkv, gain_vec, sums_own, rest_own = refs[:4], refs[4], refs[5], refs[6], refs[7]
    outs, (bias, gain_one, gain_two) = refs[12:16], refs[16:19]
    buffers, sent, sums, rest = refs[19:23], refs[23], refs[24], refs[25]
    sums[...] = sums_own[...]
    rest[...] = rest_own[...]
    write_pieces(scale, 1 - here()[0], pieces, w_qkv, outs, sums, rest, buffers, sent)
    gain_one[...] = jnp.sum(sums[...].T, 0, keepdims=True) / gain_vec[...]
    flat = rest[...].reshape(PIECES * REST_ROWS, 128).astype(F32)
    last = flat[HEADS * WT : GAIN_AT].T * (scale * WT)
    for head in range(HEADS):
        bias[head, 0:128] = flat[head * WT : head * WT + WT].T * (scale * WT)
        bias[head, 128:WT] = last[16 * head : 16 * head + 16]
    for j in range(4):
        part = flat[GAIN_AT + j : GAIN_AT + j + 1] * scale
        gain_two[:, 128 * j : 128 * j + 128] = part


def shape(*dims, dtype=BF16):
    return jax.ShapeDtypeStruct(dims, dtype)


def params(mib):
    return pltpu.CompilerParams(vmem_limit_bytes=mib * MIB)


def vmem(*dims, dtype=BF16):
    return pltpu.VMEM(dims, dtype)


def cost(flops, moved):
    return pl.CostEstimate(flops=flops, bytes_accessed=moved, transcendentals=0)


ANY = pl.BlockSpec(memory_space=pl.ANY)
INSIDE = pl.BlockSpec(memory_space=pltpu.VMEM)
SCALARS = pl.BlockSpec(memory_space=pltpu.SMEM)


def pack(grid):
    edge, top = WLON // 2, WLAT // 2
    return pl.pallas_call(
        pack_kernel,
        out_shape=(
            shape(LEVELS, HEIGHT, edge, D), shape(LEVELS, top, BREADTH, D),
            shape(LEVELS, top, edge, D),
        ),
        in_specs=[INSIDE],
        out_specs=[INSIDE] * 3,
        compiler_params=params(16),
        name="pack",
    )(grid)


def attention(*operands):
    return pl.pallas_call(
        attention_kernel,
        out_shape=(
            shape(ROWS, D), shape(ROWS, D), shape(D, ROWS), shape(ROWS, QKV),
            shape(WINDOWS, HEADS + 1, WT, 128),
        ),
        in_specs=[INSIDE] * len(operands),
        out_specs=[ANY] * 5,
        scratch_shapes=[
            vmem(56, D, dtype=F32), vmem(ROWS, D, dtype=F32), vmem(ROWS, D), vmem(ROWS, QKV),
            vmem(WINDOWS, HEADS + 1, WT, 128), vmem(2, HEADS + 1, WT, 128, dtype=F32),
            vmem(ROWS, D), vmem(ROWS, D), vmem(D, ROWS),
            pltpu.SemaphoreType.DMA((WINDOWS + 3 + WINDOWS // G_FORWARD,)),
        ],
        compiler_params=params(60),
        cost_estimate=cost(ROWS * D * QKV * 2 * 4, 20_000_000),
        name="attention",
    )(*operands)


def mlp_call(*operands):
    return pl.pallas_call(
        mlp_kernel,
        out_shape=(
            shape(ROWS, D), shape(ROWS, D, dtype=F32), shape(16, ONE_ROWS, 128),
            shape(16, ONE_ROWS, 128), shape(1, D, dtype=F32),
        ),
        in_specs=[INSIDE] * 7 + [ANY, ANY, INSIDE],
        out_specs=[INSIDE, INSIDE, ANY, ANY, INSIDE],
        scratch_shapes=[
            vmem(56, D, dtype=F32), vmem(ROWS, D, dtype=F32), vmem(ROWS, D), vmem(ROWS, D),
            vmem(ROWS, D, dtype=F32), vmem(ROWS, 1, dtype=F32), vmem(D, ROWS),
            vmem(ROWS, F_STEP), vmem(ROWS, FF), vmem(PIECES, ONE_ROWS, 128),
            vmem(D, FF), vmem(FF, D),
            pltpu.SemaphoreType.DMA((2,)), pltpu.SemaphoreType.DMA((2, PIECES)),
        ],
        compiler_params=params(56),
        cost_estimate=cost(ROWS * D * FF * 2 * 8, 40_000_000),
        name="mlp",
    )(*operands)


def back_specs(half):
    start = half * (WINDOWS // 2 // G_BACKWARD)
    return [
        pl.BlockSpec((G_BACKWARD * WT, QKV), lambda i: (start + i, 0)),
        pl.BlockSpec((G_BACKWARD, HEADS + 1, WT, 128), lambda i: (start + i, 0, 0, 0)),
        pl.BlockSpec((G_BACKWARD * WT, D), lambda i: (start + i, 0)),
    ]


def first_back(qkv, probs, grad_mixed):
    return pl.pallas_call(
        first_back_kernel,
        out_shape=(shape(ROWS // 2, QKV), shape(HEADS + 1, WT, 128, dtype=F32)),
        grid=(WINDOWS // 2 // G_BACKWARD,),
        in_specs=back_specs(0),
        out_specs=[
            pl.BlockSpec((G_BACKWARD * WT, QKV), lambda i: (i, 0)),
            pl.BlockSpec((HEADS + 1, WT, 128), lambda i: (0, 0, 0)),
        ],
        compiler_params=params(32),
        cost_estimate=cost(ROWS * D * QKV * 2 * 3, 10_000_000),
        name="first_back",
    )(qkv, probs, grad_mixed)


def second_back(*operands):
    return pl.pallas_call(
        second_back_kernel,
        out_shape=(
            shape(ROWS // 2, QKV), shape(16, TWO_ROWS, 128), shape(16, TWO_ROWS, 128),
        ),
        grid=(WINDOWS // 2 // G_BACKWARD,),
        in_specs=back_specs(1) + [INSIDE] * 4,
        out_specs=[pl.BlockSpec((G_BACKWARD * WT, QKV), lambda i: (i, 0)), INSIDE, INSIDE],
        scratch_shapes=[
            vmem(ROWS, QKV), vmem(HEADS + 1, WT, 128, dtype=F32), vmem(PIECES, TWO_ROWS, 128),
        ],
        compiler_params=params(40),
        cost_estimate=cost(ROWS * D * QKV * 2 * 4, 10_000_000),
        name="second_back",
    )(*operands)


def branch(*operands):
    return pl.pallas_call(
        branch_kernel,
        out_shape=(
            shape(LEVELS, 9, 42, D), shape(LEVELS, 9, 6, D), shape(LEVELS, 3, 42, D),
            shape(LEVELS, 3, 6, D),
        ),
        in_specs=[INSIDE] * len(operands),
        out_specs=[INSIDE] * 4,
        scratch_shapes=[vmem(ROWS, D, dtype=F32), vmem(48, D, dtype=F32)],
        compiler_params=params(24),
        cost_estimate=cost(ROWS * D * QKV * 2 * 4, 10_000_000),
        name="branch",
    )(*operands)


BUFFERS = 4


def finish_scratch():
    return [
        vmem(BUFFERS, 32, FF, dtype=F32), vmem(BUFFERS, 128, D, dtype=F32),
        vmem(BUFFERS, 16, QKV, dtype=F32), vmem(BUFFERS, 16, D, dtype=F32),
        pltpu.SemaphoreType.DMA((3, BUFFERS)),
    ]


WEIGHT_SHAPES = (
    shape(D, FF, dtype=F32), shape(FF, D, dtype=F32), shape(D, QKV, dtype=F32),
    shape(D, D, dtype=F32),
)


def finish_own(pieces, w_qkv, scale):
    return pl.pallas_call(
        functools.partial(finish_own_kernel, scale),
        out_shape=WEIGHT_SHAPES + (shape(D, 128, dtype=F32), shape(PIECES, REST_ROWS, 128)),
        in_specs=[INSIDE] * 5,
        out_specs=[ANY] * 4 + [INSIDE] * 2,
        scratch_shapes=finish_scratch(),
        compiler_params=params(24),
        cost_estimate=cost(10_000_000, 10_000_000),
        name="finish_own",
    )(*pieces, w_qkv)


def finish(pieces, w_qkv, gain_one, sums, rest, weights, scale):
    return pl.pallas_call(
        functools.partial(finish_kernel, scale),
        out_shape=WEIGHT_SHAPES + (
            shape(HEADS, WT, WT, dtype=F32), shape(1, D, dtype=F32), shape(1, D, dtype=F32),
        ),
        in_specs=[INSIDE] * 8 + [ANY] * 4,
        out_specs=[ANY] * 4 + [INSIDE] * 3,
        input_output_aliases={8: 0, 9: 1, 10: 2, 11: 3},
        scratch_shapes=finish_scratch() + [
            vmem(D, 128, dtype=F32), vmem(PIECES, REST_ROWS, 128),
        ],
        compiler_params=params(24),
        cost_estimate=cost(10_000_000, 10_000_000),
        name="finish",
    )(*pieces, w_qkv, gain_one, sums, rest, *weights)


def neighbour(array, lat_by, lon_by):
    lat_count, lon_count = lax.axis_size("lat"), lax.axis_size("lon")
    pairs = []
    for i in range(lat_count):
        for j in range(lon_count):
            to = ((i + lat_by) % lat_count) * lon_count + (j + lon_by) % lon_count
            pairs.append((i * lon_count + j, to))
    return lax.ppermute(array, ("lat", "lon"), pairs)


def halos(grid):
    lon, lat, both = pack(grid)
    return neighbour(lat, -1, 0), neighbour(lon, 0, -1), neighbour(both, -1, -1)


def send_home(main, lon, lat, both):
    return main, neighbour(lon, 0, 1), neighbour(lat, 1, 0), neighbour(both, 1, 1)


def assemble(main, lon, lat, both):
    upper = jnp.concatenate([both, lat], 2)
    lower = jnp.concatenate([lon, main], 2)
    return jnp.concatenate([upper, lower], 1)


def along(array, stage, by):
    pairs = []
    for lat in range(16):
        for lon in range(8):
            core, chip = position(lat, lon)
            chip = list(chip)
            axis = ORDERS[core][stage]
            chip[axis] = (chip[axis] + by) % 4
            x, y, z = chip
            to = (z * 4 + y // 2 * 2 + core) * 8 + x * 2 + y % 2
            pairs.append((lat * 8 + lon, to))
    return lax.ppermute(array, ("lat", "lon"), pairs)


def other_core(array):
    return lax.ppermute(array, "lat", [(i, i ^ 1) for i in range(16)])


def added(*terms):
    total = terms[0].astype(F32)
    for term in terms[1:]:
        total = total + term.astype(F32)
    return total.astype(BF16)


def after(value, *others):
    return lax.optimization_barrier((value, others))[0]


def core_sum(keep, send):
    return added(keep, other_core(send))


def first_sum(held):
    return added(held[:4], *[along(held[4 * k : 4 * k + 4], 0, k) for k in (1, 2, 3)])


def second_sum(held):
    return added(held[0], *[along(held[k], 1, k) for k in (1, 2, 3)])


def last_sum(share):
    share = lax.optimization_barrier(share)
    one, two, three = [along(share, 2, k).astype(F32) for k in (1, 2, 3)]
    return ((share.astype(F32) + two) + (one + three)).astype(BF16)


def spread(share, before):
    held = jnp.stack([share] + [along(share, 1, k) for k in (1, 2, 3)])
    held = after(held, before)
    own = [held] + [along(held, 0, k) for k in (1, 2, 3)]
    return own, [other_core(piece) for piece in own]


def local(tokens, cotangent, w_qkv, w_proj, w_up, w_down, pair_bias, gain_one, gain_two):
    total_tokens = ROWS * lax.axis_size("lat") * lax.axis_size("lon")
    scale = total_tokens ** (-0.5)
    gain_one = gain_one.reshape(1, D)
    gain_two = gain_two.reshape(1, D)
    lat_edge, lon_edge, corner = halos(tokens)
    cot_lat, cot_lon, cot_corner = halos(cotangent)
    xw, mix, act_t, qkv, probs = attention(
        tokens, lon_edge, lat_edge, corner, w_qkv, pair_bias, gain_one
    )
    grad_mixed, grad_res, keep_one, send_one, sum_gain_two = mlp_call(
        xw, mix, cotangent, cot_lon, cot_lat, cot_corner, w_proj, w_up, w_down, gain_two
    )
    grads_first, bias = first_back(qkv, probs, grad_mixed)
    held_one = core_sum(keep_one, send_one)
    grads_second, keep_two, send_two = second_back(
        qkv, probs, grad_mixed, act_t, sum_gain_two, after(bias, held_one), grads_first
    )
    held_one = first_sum(held_one)
    held_two = first_sum(core_sum(keep_two, after(send_two, held_one)))
    share = second_sum(jnp.concatenate([held_one, held_two], 1))
    home = branch(xw, after(grads_first, share), grads_second, grad_res, w_qkv, gain_one)
    share = after(last_sum(share), home)
    home = send_home(*home)
    own, other = spread(share, home)
    *weights, sums, rest = finish_own(own, w_qkv, scale)
    sum_up, sum_down, sum_qkv, sum_proj, sum_bias, sum_one, sum_two = finish(
        other, w_qkv, gain_one, sums, rest, weights, scale
    )
    return (
        assemble(*[after(piece, sums) for piece in home]),
        sum_qkv,
        sum_proj,
        sum_up,
        sum_down,
        sum_bias,
        sum_one.reshape(D),
        sum_two.reshape(D),
    )


def solution(mesh):
    grid = P(None, "lat", "lon", None)
    in_specs = (grid, grid, P(), P(), P(), P(), P(), P(), P())
    out_specs = (grid, P(), P(), P(), P(), P(), P(), P())
    return jax.shard_map(local, mesh=mesh, in_specs=in_specs, out_specs=out_specs, check_vma=False)
```

```python
import functools

import jax
import jax.numpy as jnp
from jax import lax
from jax.experimental import pallas as pl
from jax.experimental.pallas import tpu as pltpu
from jax.sharding import PartitionSpec as P

HEADS = 8
WLAT = 6
WLON = 12
WT = 144
D = 512
QKV = 1536
FF = 2048
LEVELS = 2
HEIGHT = 12
BREADTH = 48
WINDOWS = 8
ROWS = WINDOWS * WT
EPSILON = 1e-05
MASKED = -1e30
F32 = jnp.float32
BF16 = jnp.bfloat16
PIECES = 32
BAND_ROWS = 512
PROJ_ROWS = 64
ONE_ROWS = BAND_ROWS + PROJ_ROWS
QKV_ROWS = 192
REST_ROWS = 48
TWO_ROWS = QKV_ROWS + REST_ROWS
ALL_ROWS = ONE_ROWS + TWO_ROWS
GAIN_AT = (HEADS + 1) * WT
MIB = 1024 * 1024
M_NORM = 576
M_UP = 1152
M_BACK = 576
M_BRANCH = 576
G_FORWARD = 4
G_BACKWARD = 2
F_STEP = 512

NN = (((1,), (0,)), ((), ()))
NT = (((1,), (1,)), ((), ()))
TN = (((0,), (0,)), ((), ()))


def mm(a, b, dims=NN):
    return lax.dot_general(a, b, dims, preferred_element_type=F32)


def stats_of(values):
    average = jnp.mean(values, -1, keepdims=True)
    centred = values - average
    variance = jnp.mean(centred * centred, -1, keepdims=True)
    inv_std = lax.rsqrt(variance + EPSILON)
    return centred * inv_std, inv_std


def back_of(grad_out, gain_vec, normed, inv_std):
    scaled = grad_out * gain_vec
    return (
        scaled
        - jnp.mean(scaled, -1, keepdims=True)
        - normed * jnp.mean(scaled * normed, -1, keepdims=True)
    ) * inv_std


def run_at(level, row, column):
    window = (row // WLAT) * 4 + column
    return window * WT + level * (WT // 2) + (row % WLAT) * WLON


def gather_windows(main_ref, lon_ref, lat_ref, both_ref, line, wide, out_ref):
    for level in range(LEVELS):
        for row in range(HEIGHT):
            if row < HEIGHT - WLAT // 2:
                line[0:BREADTH] = main_ref[level, row + WLAT // 2].astype(F32)
                line[BREADTH : BREADTH + 6] = lon_ref[level, row + WLAT // 2].astype(F32)
            else:
                line[0:BREADTH] = lat_ref[level, row - (HEIGHT - WLAT // 2)].astype(F32)
                line[BREADTH : BREADTH + 6] = both_ref[level, row - (HEIGHT - WLAT // 2)].astype(F32)
            for column in range(4):
                at = run_at(level, row, column)
                wide[at : at + WLON] = line[6 + WLON * column : 18 + WLON * column]

    def narrow(window, _):
        rows = pl.ds(pl.multiple_of(window * WT, 16), WT)
        out_ref[rows] = wide[rows].astype(BF16)
        return 0

    lax.fori_loop(0, WINDOWS, narrow, 0)


def position(lat, lon):
    return lat % 2, (lon // 2, (lat // 2) % 2 * 2 + lon % 2, lat // 4)


ORDERS = ((0, 1, 2), (1, 2, 0))


def here():
    return position(lax.axis_index("lat"), lax.axis_index("lon"))


def slot_of(core, block):
    _, chip = here()
    first, second = chip[ORDERS[core][0]], chip[ORDERS[core][1]]
    return (block // 4 + 4 - first) % 4 * 4 + (block % 4 + 4 - second) % 4


def block_at(core, first_by, second_by):
    _, chip = here()
    first = jnp.where(core == 0, chip[ORDERS[0][0]], chip[ORDERS[1][0]])
    second = jnp.where(core == 0, chip[ORDERS[0][1]], chip[ORDERS[1][1]])
    return (first + 4 - first_by) % 4 * 4 + (second + 4 - second_by) % 4


def window_rows(window):
    return pl.ds(pl.multiple_of(window * WT, 16), WT)


def softmax_first(scores):
    top = jnp.max(scores, 0, keepdims=True)
    exponent = jnp.exp(scores - top)
    total = jnp.sum(exponent, 0, keepdims=True)
    return (exponent * (1.0 / total)).astype(BF16)


def head_masks():
    lane = lax.broadcasted_iota(jnp.int32, (1, 128), 1)
    first = lane < 64
    row = lax.broadcasted_iota(jnp.int32, (128, D), 0) // 16
    column = lax.broadcasted_iota(jnp.int32, (128, D), 1) // 64
    halves = (first.astype(F32).astype(BF16), (lane >= 64).astype(F32).astype(BF16))
    return first, halves, (row == column).astype(F32)


def tiled(block):
    return jnp.concatenate([block] * HEADS, 0)


def pair_of(head):
    return slice(head // 2 * 128, head // 2 * 128 + 128)


def tail_sum(block, tail):
    return jnp.sum((block * tail).reshape(HEADS, 16, D), 0)


def pack_kernel(tok, cot, *refs):
    edge, top = WLON // 2, WLAT // 2
    outs, (sides, tops, got) = (refs[0:3], refs[3:6]), refs[6:]
    loads = []
    for i, ref in enumerate((tok, cot)):
        loads.append(pltpu.make_async_copy(ref.at[:, :, pl.ds(0, 16)], sides.at[i], got.at[i, 0]))
        loads.append(pltpu.make_async_copy(ref.at[:, pl.ds(0, top)], tops.at[i], got.at[i, 1]))
    for load in loads:
        load.start()
    for load in loads:
        load.wait()
    for i, (lon, lat, both) in enumerate(outs):
        lat[...] = tops[i]
        for level in range(LEVELS):
            for row in range(HEIGHT):
                lon[level, row] = sides[i, level, row, :edge]
            for row in range(top):
                both[level, row] = sides[i, level, row, :edge]


def attention_kernel(
    tok, tok_lon, tok_lat, tok_both, w_qkv, pair_bias, gain_one,
    xw_out, mix_out, act_t_out, qkv_out, probs_out,
    line, wide, act, qkv, probs, bias, xw, mix, act_t, sent,
):
    gather_windows(tok, tok_lon, tok_lat, tok_both, line, wide, xw)
    copies = [pltpu.make_async_copy(xw, xw_out, sent.at[WINDOWS + 1])]
    copies[0].start()

    def norm_one(window, _):
        rows = window_rows(window)
        values, _ = stats_of(xw[rows].astype(F32))
        act[rows] = (values * gain_one[...]).astype(BF16)
        return 0

    lax.fori_loop(0, WINDOWS, norm_one, 0)

    def project(n, _):
        cols = pl.ds(pl.multiple_of(n * 256, 256), 256)
        qkv[:, cols] = mm(act[...], w_qkv[:, cols]).astype(BF16)
        return 0

    lax.fori_loop(0, QKV // 256, project, 0)
    act_t[...] = act[...].T
    copies.append(pltpu.make_async_copy(qkv, qkv_out, sent.at[WINDOWS]))
    copies.append(pltpu.make_async_copy(act_t, act_t_out, sent.at[WINDOWS + 2]))
    for copy in copies[1:]:
        copy.start()

    is_last = lax.axis_index("lat") == lax.axis_size("lat") - 1
    key_at = lax.broadcasted_iota(jnp.int32, (WT, 128), 0)
    query_at = lax.broadcasted_iota(jnp.int32, (WT, 128), 1)

    def masked(query_at):
        apart = (key_at // WLON % WLAT >= WLAT // 2) != (query_at // WLON % WLAT >= WLAT // 2)
        return jnp.where(apart & is_last, MASKED, 0.0)

    mask_main = masked(query_at)
    mask_tail = masked(128 + query_at % 16)
    for head in range(HEADS):
        block = pair_bias[head, 0:128].T
        bias[0, head] = block
        bias[1, head] = block + mask_main
    block = jnp.concatenate([pair_bias[head, 128:WT] for head in range(HEADS)], 0).T
    bias[0, HEADS] = block
    bias[1, HEADS] = block + mask_tail

    first, halves, tail = head_masks()
    halves = [half * 0.125 for half in halves]
    tail_low = (tail * 0.125).astype(BF16)

    def mix_copy(group):
        at = pl.ds(pl.multiple_of(group * G_FORWARD * WT, 16), G_FORWARD * WT)
        return pltpu.make_async_copy(mix.at[at], mix_out.at[at], sent.at[WINDOWS + 3 + group])

    def attend(group, _):
        windows = [group * G_FORWARD + i for i in range(G_FORWARD)]
        heads = [(i, head) for i in range(G_FORWARD) for head in range(HEADS)]
        rows = [window_rows(window) for window in windows]
        main = [pl.ds(pl.multiple_of(window * WT, 16), 128) for window in windows]
        last = [pl.ds(pl.multiple_of(window * WT + 128, 16), 16) for window in windows]
        key = [qkv[r, D : 2 * D] for r in rows]
        val = [qkv[r, 2 * D : 3 * D] for r in rows]
        tail_scores = [
            mm(k, tiled(qkv[r, 0:D]) * tail_low, NT) for k, r in zip(key, last)
        ]
        scores = [
            mm(key[i][:, pair_of(head)], qkv[main[i], pair_of(head)] * halves[head % 2], NT)
            for i, head in heads
        ]
        tail_weights = [
            softmax_first(t + bias[window // 4, HEADS]) for t, window in zip(tail_scores, windows)
        ]
        weights = [
            softmax_first(t + bias[windows[i] // 4, head]) for t, (i, head) in zip(scores, heads)
        ]
        tail_mixed = [mm(w, v, TN) for w, v in zip(tail_weights, val)]
        mixed = [mm(w, val[i][:, pair_of(head)], TN) for w, (i, head) in zip(weights, heads)]
        for i, window in enumerate(windows):
            probs[window, HEADS] = tail_weights[i]
            mix[last[i]] = tail_sum(tail_mixed[i], tail).astype(BF16)
        for w, (i, head) in zip(weights, heads):
            probs[windows[i], head] = w
        for n, (i, head) in enumerate(heads):
            if head % 2 == 0:
                mix[main[i], pair_of(head)] = jnp.where(first, mixed[n], mixed[n + 1]).astype(BF16)
        for window in windows:
            pltpu.make_async_copy(probs.at[window], probs_out.at[window], sent.at[window]).start()
        mix_copy(group).start()
        return 0

    lax.fori_loop(0, WINDOWS // G_FORWARD, attend, 0)
    for copy in copies + [mix_copy(group) for group in range(WINDOWS // G_FORWARD)]:
        copy.wait()
    for window in range(WINDOWS):
        pltpu.make_async_copy(probs.at[window], probs_out.at[window], sent.at[window]).wait()


def mlp_kernel(
    xw, mix, cot, cot_lon, cot_lat, cot_both, w_proj, w_up_in, w_down_in, gain_two,
    grad_mixed, grad_res, keep_one, send_one, sum_gain,
    line, wide, cotw, act, normed, inv_two, act_t, activated, grad_hidden, sums, w_up, w_down,
    got, sent,
):
    loads = [
        pltpu.make_async_copy(w_up_in, w_up, got.at[0]),
        pltpu.make_async_copy(w_down_in, w_down, got.at[1]),
    ]
    for load in loads:
        load.start()
    gather_windows(cot, cot_lon, cot_lat, cot_both, line, wide, cotw)

    def norm_two(part, _):
        rows = pl.ds(pl.multiple_of(part * M_NORM, 16), M_NORM)
        residual = xw[rows].astype(F32) + mm(mix[rows], w_proj[...])
        values, inv_std = stats_of(residual)
        normed[rows] = values
        inv_two[rows] = inv_std
        act[rows] = (values * gain_two[...]).astype(BF16)
        return 0

    lax.fori_loop(0, ROWS // M_NORM, norm_two, 0)
    act_t[...] = act[...].T
    for load in loads:
        load.wait()

    c0 = 0.7978845608028654
    c1 = c0 * 0.044715

    def mlp(f, _):
        cols = pl.ds(pl.multiple_of(f * F_STEP, F_STEP), F_STEP)

        def rows_of(r, _):
            rows = pl.ds(pl.multiple_of(r * M_UP, 16), M_UP)
            u = mm(act[rows], w_up[:, cols])
            grad_act = mm(cotw[rows], w_down[cols, :], NT)
            square = u * u
            gate = 0.5 + 0.5 * jnp.tanh(u * (c0 + c1 * square))
            value = u * gate
            activated[rows] = value.astype(BF16)
            slope = gate + value * (1.0 - gate) * (2.0 * c0 + 6.0 * c1 * square)
            grad_hidden[rows, cols] = (grad_act * slope).astype(BF16)
            return 0

        lax.fori_loop(0, ROWS // M_UP, rows_of, 0)
        up = mm(act_t[...], grad_hidden[:, cols]).astype(BF16)
        for j in range(4):
            at = pl.ds(pl.multiple_of(f * 128 + 32 * j, 32), 32)
            sums[0:16, at] = up[:, 128 * j : 128 * j + 128].reshape(16, 32, 128)
        down = mm(activated[...], cotw[...], TN).astype(BF16)
        for i in range(4):
            for j in range(4):
                part = down[128 * i : 128 * i + 128, 128 * j : 128 * j + 128]
                sums[16 + f * 4 + i, 128 * j : 128 * j + 128] = part
        return 0

    lax.fori_loop(0, FF // F_STEP, mlp, 0)

    core, _ = here()

    def send(rows, at, act_on):
        for owner in range(2):
            for block in range(16):
                piece = owner * 16 + block
                slot = slot_of(owner, block)

                def copy_to(out):
                    return pltpu.make_async_copy(
                        sums.at[piece, rows], out.at[slot, rows], sent.at[at, piece]
                    )

                @pl.when(core == owner)
                def _():
                    act_on(copy_to(keep_one))

                @pl.when(core != owner)
                def _():
                    act_on(copy_to(send_one))

    bands, tails = pl.ds(0, BAND_ROWS), pl.ds(BAND_ROWS, PROJ_ROWS)
    send(bands, 0, lambda copy: copy.start())

    def back(part, total):
        rows = pl.ds(pl.multiple_of(part * M_BACK, 16), M_BACK)
        grads = mm(grad_hidden[rows], w_up[...], NT)
        values = normed[rows]
        total = total + jnp.sum(grads * values, 0, keepdims=True)
        residual = cotw[rows].astype(F32) + back_of(grads, gain_two[...], values, inv_two[rows])
        grad_res[rows] = residual
        low = residual.astype(BF16)
        act[rows] = low
        grad_mixed[rows] = mm(low, w_proj[...], NT).astype(BF16)
        return total

    sum_gain[...] = lax.fori_loop(0, ROWS // M_BACK, back, jnp.zeros((1, D), F32))
    proj = mm(mix[...], act[...], TN).astype(BF16)
    for j in range(4):
        at = slice(BAND_ROWS + 16 * j, BAND_ROWS + 16 * j + 16)
        sums[:, at] = proj[:, 128 * j : 128 * j + 128].reshape(PIECES, 16, 128)
    send(tails, 1, lambda copy: copy.start())
    send(bands, 0, lambda copy: copy.wait())
    send(tails, 1, lambda copy: copy.wait())


def first_back_kernel(qkv, probs, grad_mixed, grad_qkv, bias):
    window_back(qkv, probs, grad_mixed, grad_qkv, bias, None)


def second_back_kernel(
    qkv, probs, grad_mixed, act_t, sum_gain_two, bias_before, grads_before,
    grad_qkv, keep_two, send_two,
    grads_all, bias, flat,
):
    step = pl.program_id(0)

    @pl.when(step == 0)
    def _():
        grads_all[0 : ROWS // 2] = grads_before[...]

    window_back(qkv, probs, grad_mixed, grad_qkv, bias, bias_before)
    size = G_BACKWARD * WT
    at = pl.multiple_of(ROWS // 2 + step * size, 16)
    grads_all[pl.ds(at, size)] = grad_qkv[...]

    @pl.when(step == WINDOWS // 2 // G_BACKWARD - 1)
    def _():
        for n in range(QKV // 512):
            part = mm(act_t[...], grads_all[:, 512 * n : 512 * n + 512]).astype(BF16)
            for j in range(4):
                at = (n * 4 + j) * 16
                flat[:, at : at + 16] = part[:, 128 * j : 128 * j + 128].reshape(PIECES, 16, 128)
        gains = [sum_gain_two[:, 128 * j : 128 * j + 128] for j in range(4)]
        gains = jnp.concatenate(gains + [jnp.zeros((12, 128), F32)], 0)
        rest = [bias[block].astype(BF16) for block in range(HEADS + 1)] + [gains.astype(BF16)]
        rest.append(jnp.zeros((PIECES * REST_ROWS - GAIN_AT - 16, 128), BF16))
        rest = jnp.concatenate(rest, 0)
        flat[:, QKV_ROWS:TWO_ROWS] = rest.reshape(PIECES, REST_ROWS, 128)
        core, _ = here()
        for owner in range(2):
            for block in range(16):
                slot = slot_of(owner, block)
                piece = flat[owner * 16 + block]

                @pl.when(core == owner)
                def _():
                    keep_two[slot] = piece

                @pl.when(core != owner)
                def _():
                    send_two[slot] = piece


def window_back(qkv, probs, grad_mixed, grad_qkv, bias, bias_before):
    step = pl.program_id(0)
    first, halves, tail = head_masks()
    tail_low = tail.astype(BF16)

    @pl.when(step == 0)
    def _():
        bias[...] = jnp.zeros_like(bias) if bias_before is None else bias_before[...]

    group = range(G_BACKWARD)
    heads = [(i, head) for i in group for head in range(HEADS)]
    rows = [slice(i * WT, i * WT + WT) for i in group]
    main = [slice(i * WT, i * WT + 128) for i in group]
    last = [slice(i * WT + 128, i * WT + WT) for i in group]
    key = [qkv[r, D : 2 * D] for r in rows]
    val = [qkv[r, 2 * D : 3 * D] for r in rows]
    query_tail = [tiled(qkv[r, 0:D]) * tail_low for r in last]
    out_tail = [tiled(grad_mixed[r]) * tail_low for r in last]
    query = [qkv[main[i], pair_of(head)] * halves[head % 2] for i, head in heads]
    out = [grad_mixed[main[i], pair_of(head)] * halves[head % 2] for i, head in heads]

    tail_probs = [mm(v, o, NT) for v, o in zip(val, out_tail)]
    grad_probs = [mm(val[i][:, pair_of(head)], o, NT) for o, (i, head) in zip(out, heads)]

    def score_grads(low_probs, grad_probs):
        weights = low_probs.astype(F32)
        product = grad_probs * weights
        return product - weights * jnp.sum(product, 0, keepdims=True)

    tail_low_probs = [probs[i, HEADS] for i in group]
    low_probs = [probs[i, head] for i, head in heads]
    tail_grads = [score_grads(p, g) for p, g in zip(tail_low_probs, tail_probs)]
    grads = [score_grads(p, g) for p, g in zip(low_probs, grad_probs)]
    bias[HEADS] += sum(tail_grads[1:], tail_grads[0])
    for head in range(HEADS):
        mine = grads[head::HEADS]
        bias[head] += sum(mine[1:], mine[0])
    tail_grads = [g.astype(BF16) for g in tail_grads]
    grads = [g.astype(BF16) for g in grads]

    query_last = [mm(g, k, TN) for g, k in zip(tail_grads, key)]
    key_more = [mm(g, q) for g, q in zip(tail_grads, query_tail)]
    val_more = [mm(p, o) for p, o in zip(tail_low_probs, out_tail)]
    query_parts = [mm(g, key[i][:, pair_of(head)], TN) for g, (i, head) in zip(grads, heads)]
    key_parts = [mm(g, q) for g, q in zip(grads, query)]
    val_parts = [mm(p, o) for p, o in zip(low_probs, out)]
    for i in group:
        grad_qkv[last[i], 0:D] = (tail_sum(query_last[i], tail) * 0.125).astype(BF16)
    for n, (i, head) in enumerate(heads):
        if head % 2:
            continue
        cols = pair_of(head)
        at = head // 2 * 128
        part = jnp.where(first, query_parts[n], query_parts[n + 1]) * 0.125
        grad_qkv[main[i], cols] = part.astype(BF16)
        part = (key_parts[n] + key_parts[n + 1] + key_more[i][:, cols]) * 0.125
        grad_qkv[rows[i], D + at : D + at + 128] = part.astype(BF16)
        part = val_parts[n] + val_parts[n + 1] + val_more[i][:, cols]
        grad_qkv[rows[i], 2 * D + at : 2 * D + at + 128] = part.astype(BF16)

def branch_kernel(xw, grads_first, grads_second, grad_res, w_qkv, gain_one, main, lon, lat, both, wide, line):
    for part, grad_qkv in enumerate((grads_first, grads_second)):
        rows = slice(part * ROWS // 2, (part + 1) * ROWS // 2)
        values, inv_std = stats_of(xw[rows].astype(F32))
        grads = mm(grad_qkv[...], w_qkv[...], NT)
        low = back_of(grads, gain_one[...], values, inv_std).astype(BF16)
        wide[rows] = grad_res[rows] + low.astype(F32)

    for level in range(LEVELS):
        for row in range(HEIGHT):
            for column in range(4):
                at = run_at(level, row, column)
                line[WLON * column : WLON * column + WLON] = wide[at : at + WLON]
            inner, outer = (main, lon) if row < HEIGHT - WLAT // 2 else (lat, both)
            at = row if row < HEIGHT - WLAT // 2 else row - (HEIGHT - WLAT // 2)
            inner[level, at] = line[0 : BREADTH - 6].astype(BF16)
            outer[level, at] = line[BREADTH - 6 : BREADTH].astype(BF16)


def write_pieces(scale, owner, pieces, w_qkv, outs, sums, rest, buffers, sent):
    up_out, down_out, qkv_out, proj_out = outs
    buffer_up, buffer_down, buffer_qkv, buffer_proj = buffers

    def run(buffer_band, band, fill_band, band_out):
        def copies(n):
            block = block_at(owner, n // 4, n % 4)
            piece = owner * 16 + block
            slot = n % BUFFERS
            targets = ((buffer_band, band_out, band, block), (buffer_qkv, qkv_out, 16, piece),
                       (buffer_proj, proj_out, 16, piece))
            return [
                pltpu.make_async_copy(
                    buffer.at[slot],
                    out.at[pl.ds(pl.multiple_of(at * size, size), size)],
                    sent.at[i, slot],
                )
                for i, (buffer, out, size, at) in enumerate(targets)
            ]

        for n in range(16):
            if n >= BUFFERS:
                for copy in copies(n - BUFFERS):
                    copy.wait()
            slot = n % BUFFERS
            piece = owner * 16 + block_at(owner, n // 4, n % 4)
            rows = pl.ds(pl.multiple_of(piece * 16, 16), 16)
            held = pieces[n // 4]
            fill_band(held, n % 4, slot)
            for j in range(4):
                at = BAND_ROWS + 16 * j
                part = held[n % 4, at : at + 16].astype(F32) * scale
                buffer_proj[slot, :, 128 * j : 128 * j + 128] = part
            total = jnp.zeros((16, 128), F32)
            for j in range(12):
                cols = slice(128 * j, 128 * j + 128)
                at = ONE_ROWS + 16 * j
                part = held[n % 4, at : at + 16].astype(F32) * scale
                buffer_qkv[slot, :, cols] = part
                total = total + part * w_qkv[rows, cols].astype(F32)
            sums[rows] = total
            rest[piece] = held[n % 4, ONE_ROWS + QKV_ROWS : ALL_ROWS]
            for copy in copies(n):
                copy.start()
        for n in range(16 - BUFFERS, 16):
            for copy in copies(n):
                copy.wait()

    def fill_up(held, at, slot):
        for j in range(16):
            part = held[at, 32 * j : 32 * j + 32].astype(F32) * scale
            buffer_up[slot, :, 128 * j : 128 * j + 128] = part

    def fill_down(held, at, slot):
        for j in range(4):
            part = held[at, 128 * j : 128 * j + 128].astype(F32) * scale
            buffer_down[slot, :, 128 * j : 128 * j + 128] = part

    @pl.when(owner == 0)
    def _():
        run(buffer_up, 32, fill_up, up_out)

    @pl.when(owner == 1)
    def _():
        run(buffer_down, 128, fill_down, down_out)


def finish_own_kernel(scale, *refs):
    pieces, w_qkv, outs, sums, rest = refs[:4], refs[4], refs[5:9], refs[9], refs[10]
    write_pieces(scale, here()[0], pieces, w_qkv, outs, sums, rest, refs[11:15], refs[15])


def finish_kernel(scale, *refs):
    pieces, w_qkv, gain_vec, sums_own, rest_own = refs[:4], refs[4], refs[5], refs[6], refs[7]
    outs, (bias, gain_one, gain_two) = refs[12:16], refs[16:19]
    buffers, sent, sums, rest = refs[19:23], refs[23], refs[24], refs[25]
    sums[...] = sums_own[...]
    rest[...] = rest_own[...]
    write_pieces(scale, 1 - here()[0], pieces, w_qkv, outs, sums, rest, buffers, sent)
    gain_one[...] = jnp.sum(sums[...].T, 0, keepdims=True) / gain_vec[...]
    flat = rest[...].reshape(PIECES * REST_ROWS, 128).astype(F32)
    last = flat[HEADS * WT : GAIN_AT].T * (scale * WT)
    for head in range(HEADS):
        bias[head, 0:128] = flat[head * WT : head * WT + WT].T * (scale * WT)
        bias[head, 128:WT] = last[16 * head : 16 * head + 16]
    for j in range(4):
        part = flat[GAIN_AT + j : GAIN_AT + j + 1] * scale
        gain_two[:, 128 * j : 128 * j + 128] = part


def shape(*dims, dtype=BF16):
    return jax.ShapeDtypeStruct(dims, dtype)


def params(mib):
    return pltpu.CompilerParams(vmem_limit_bytes=mib * MIB)


def vmem(*dims, dtype=BF16):
    return pltpu.VMEM(dims, dtype)


def cost(flops, moved):
    return pl.CostEstimate(flops=flops, bytes_accessed=moved, transcendentals=0)


ANY = pl.BlockSpec(memory_space=pl.ANY)
INSIDE = pl.BlockSpec(memory_space=pltpu.VMEM)
SCALARS = pl.BlockSpec(memory_space=pltpu.SMEM)


def pack(tokens, cotangent):
    edge, top = WLON // 2, WLAT // 2
    return pl.pallas_call(
        pack_kernel,
        out_shape=(
            shape(LEVELS, HEIGHT, edge, D), shape(LEVELS, top, BREADTH, D),
            shape(LEVELS, top, edge, D),
        ) * 2,
        in_specs=[ANY] * 2,
        out_specs=[INSIDE] * 6,
        scratch_shapes=[
            vmem(2, LEVELS, HEIGHT, 16, D), vmem(2, LEVELS, top, BREADTH, D),
            pltpu.SemaphoreType.DMA((2, 2)),
        ],
        compiler_params=params(60),
        name="pack",
    )(tokens, cotangent)


def attention(*operands):
    return pl.pallas_call(
        attention_kernel,
        out_shape=(
            shape(ROWS, D), shape(ROWS, D), shape(D, ROWS), shape(ROWS, QKV),
            shape(WINDOWS, HEADS + 1, WT, 128),
        ),
        in_specs=[INSIDE] * len(operands),
        out_specs=[ANY] * 5,
        scratch_shapes=[
            vmem(56, D, dtype=F32), vmem(ROWS, D, dtype=F32), vmem(ROWS, D), vmem(ROWS, QKV),
            vmem(WINDOWS, HEADS + 1, WT, 128), vmem(2, HEADS + 1, WT, 128, dtype=F32),
            vmem(ROWS, D), vmem(ROWS, D), vmem(D, ROWS),
            pltpu.SemaphoreType.DMA((WINDOWS + 3 + WINDOWS // G_FORWARD,)),
        ],
        compiler_params=params(60),
        cost_estimate=cost(ROWS * D * QKV * 2 * 4, 20_000_000),
        name="attention",
    )(*operands)


def mlp_call(*operands):
    return pl.pallas_call(
        mlp_kernel,
        out_shape=(
            shape(ROWS, D), shape(ROWS, D, dtype=F32), shape(16, ONE_ROWS, 128),
            shape(16, ONE_ROWS, 128), shape(1, D, dtype=F32),
        ),
        in_specs=[INSIDE] * 7 + [ANY, ANY, INSIDE],
        out_specs=[INSIDE, INSIDE, ANY, ANY, INSIDE],
        scratch_shapes=[
            vmem(56, D, dtype=F32), vmem(ROWS, D, dtype=F32), vmem(ROWS, D), vmem(ROWS, D),
            vmem(ROWS, D, dtype=F32), vmem(ROWS, 1, dtype=F32), vmem(D, ROWS),
            vmem(ROWS, F_STEP), vmem(ROWS, FF), vmem(PIECES, ONE_ROWS, 128),
            vmem(D, FF), vmem(FF, D),
            pltpu.SemaphoreType.DMA((2,)), pltpu.SemaphoreType.DMA((2, PIECES)),
        ],
        compiler_params=params(56),
        cost_estimate=cost(ROWS * D * FF * 2 * 8, 40_000_000),
        name="mlp",
    )(*operands)


def back_specs(half):
    start = half * (WINDOWS // 2 // G_BACKWARD)
    return [
        pl.BlockSpec((G_BACKWARD * WT, QKV), lambda i: (start + i, 0)),
        pl.BlockSpec((G_BACKWARD, HEADS + 1, WT, 128), lambda i: (start + i, 0, 0, 0)),
        pl.BlockSpec((G_BACKWARD * WT, D), lambda i: (start + i, 0)),
    ]


def first_back(qkv, probs, grad_mixed):
    return pl.pallas_call(
        first_back_kernel,
        out_shape=(shape(ROWS // 2, QKV), shape(HEADS + 1, WT, 128, dtype=F32)),
        grid=(WINDOWS // 2 // G_BACKWARD,),
        in_specs=back_specs(0),
        out_specs=[
            pl.BlockSpec((G_BACKWARD * WT, QKV), lambda i: (i, 0)),
            pl.BlockSpec((HEADS + 1, WT, 128), lambda i: (0, 0, 0)),
        ],
        compiler_params=params(32),
        cost_estimate=cost(ROWS * D * QKV * 2 * 3, 10_000_000),
        name="first_back",
    )(qkv, probs, grad_mixed)


def second_back(*operands):
    return pl.pallas_call(
        second_back_kernel,
        out_shape=(
            shape(ROWS // 2, QKV), shape(16, TWO_ROWS, 128), shape(16, TWO_ROWS, 128),
        ),
        grid=(WINDOWS // 2 // G_BACKWARD,),
        in_specs=back_specs(1) + [INSIDE] * 4,
        out_specs=[pl.BlockSpec((G_BACKWARD * WT, QKV), lambda i: (i, 0)), INSIDE, INSIDE],
        scratch_shapes=[
            vmem(ROWS, QKV), vmem(HEADS + 1, WT, 128, dtype=F32), vmem(PIECES, TWO_ROWS, 128),
        ],
        compiler_params=params(40),
        cost_estimate=cost(ROWS * D * QKV * 2 * 4, 10_000_000),
        name="second_back",
    )(*operands)


def branch(*operands):
    return pl.pallas_call(
        branch_kernel,
        out_shape=(
            shape(LEVELS, 9, 42, D), shape(LEVELS, 9, 6, D), shape(LEVELS, 3, 42, D),
            shape(LEVELS, 3, 6, D),
        ),
        in_specs=[INSIDE] * len(operands),
        out_specs=[INSIDE] * 4,
        scratch_shapes=[vmem(ROWS, D, dtype=F32), vmem(48, D, dtype=F32)],
        compiler_params=params(24),
        cost_estimate=cost(ROWS * D * QKV * 2 * 4, 10_000_000),
        name="branch",
    )(*operands)


BUFFERS = 4


def finish_scratch():
    return [
        vmem(BUFFERS, 32, FF, dtype=F32), vmem(BUFFERS, 128, D, dtype=F32),
        vmem(BUFFERS, 16, QKV, dtype=F32), vmem(BUFFERS, 16, D, dtype=F32),
        pltpu.SemaphoreType.DMA((3, BUFFERS)),
    ]


WEIGHT_SHAPES = (
    shape(D, FF, dtype=F32), shape(FF, D, dtype=F32), shape(D, QKV, dtype=F32),
    shape(D, D, dtype=F32),
)


def finish_own(pieces, w_qkv, scale):
    return pl.pallas_call(
        functools.partial(finish_own_kernel, scale),
        out_shape=WEIGHT_SHAPES + (shape(D, 128, dtype=F32), shape(PIECES, REST_ROWS, 128)),
        in_specs=[INSIDE] * 5,
        out_specs=[ANY] * 4 + [INSIDE] * 2,
        scratch_shapes=finish_scratch(),
        compiler_params=params(24),
        cost_estimate=cost(10_000_000, 10_000_000),
        name="finish_own",
    )(*pieces, w_qkv)


def finish(pieces, w_qkv, gain_one, sums, rest, weights, scale):
    return pl.pallas_call(
        functools.partial(finish_kernel, scale),
        out_shape=WEIGHT_SHAPES + (
            shape(HEADS, WT, WT, dtype=F32), shape(1, D, dtype=F32), shape(1, D, dtype=F32),
        ),
        in_specs=[INSIDE] * 8 + [ANY] * 4,
        out_specs=[ANY] * 4 + [INSIDE] * 3,
        input_output_aliases={8: 0, 9: 1, 10: 2, 11: 3},
        scratch_shapes=finish_scratch() + [
            vmem(D, 128, dtype=F32), vmem(PIECES, REST_ROWS, 128),
        ],
        compiler_params=params(24),
        cost_estimate=cost(10_000_000, 10_000_000),
        name="finish",
    )(*pieces, w_qkv, gain_one, sums, rest, *weights)


def neighbour(array, lat_by, lon_by):
    lat_count, lon_count = lax.axis_size("lat"), lax.axis_size("lon")
    pairs = []
    for i in range(lat_count):
        for j in range(lon_count):
            to = ((i + lat_by) % lat_count) * lon_count + (j + lon_by) % lon_count
            pairs.append((i * lon_count + j, to))
    return lax.ppermute(array, ("lat", "lon"), pairs)


def halos(lon, lat, both):
    return neighbour(lat, -1, 0), neighbour(lon, 0, -1), neighbour(both, -1, -1)


def send_home(main, lon, lat, both):
    return main, neighbour(lon, 0, 1), neighbour(lat, 1, 0), neighbour(both, 1, 1)


def assemble(main, lon, lat, both):
    upper = jnp.concatenate([both, lat], 2)
    lower = jnp.concatenate([lon, main], 2)
    return jnp.concatenate([upper, lower], 1)


def along(array, stage, by):
    pairs = []
    for lat in range(16):
        for lon in range(8):
            core, chip = position(lat, lon)
            chip = list(chip)
            axis = ORDERS[core][stage]
            chip[axis] = (chip[axis] + by) % 4
            x, y, z = chip
            to = (z * 4 + y // 2 * 2 + core) * 8 + x * 2 + y % 2
            pairs.append((lat * 8 + lon, to))
    return lax.ppermute(array, ("lat", "lon"), pairs)


def other_core(array):
    return lax.ppermute(array, "lat", [(i, i ^ 1) for i in range(16)])


def added(*terms):
    total = terms[0].astype(F32)
    for term in terms[1:]:
        total = total + term.astype(F32)
    return total.astype(BF16)


def after(value, *others):
    return lax.optimization_barrier((value, others))[0]


def core_sum(keep, send):
    return added(keep, other_core(send))


def first_sum(held):
    return added(held[:4], *[along(held[4 * k : 4 * k + 4], 0, k) for k in (1, 2, 3)])


def second_sum(held):
    return added(held[0], *[along(held[k], 1, k) for k in (1, 2, 3)])


def last_sum(share):
    share = lax.optimization_barrier(share)
    one, two, three = [along(share, 2, k).astype(F32) for k in (1, 2, 3)]
    return ((share.astype(F32) + two) + (one + three)).astype(BF16)


def spread(share, before):
    held = jnp.stack([share] + [along(share, 1, k) for k in (1, 2, 3)])
    held = after(held, before)
    own = [held] + [along(held, 0, k) for k in (1, 2, 3)]
    return own, [other_core(piece) for piece in own]


def local(tokens, cotangent, w_qkv, w_proj, w_up, w_down, pair_bias, gain_one, gain_two):
    total_tokens = ROWS * lax.axis_size("lat") * lax.axis_size("lon")
    scale = total_tokens ** (-0.5)
    gain_one = gain_one.reshape(1, D)
    gain_two = gain_two.reshape(1, D)
    edges = pack(tokens, cotangent)
    lat_edge, lon_edge, corner = halos(*edges[:3])
    cot_lat, cot_lon, cot_corner = halos(*edges[3:])
    xw, mix, act_t, qkv, probs = attention(
        tokens, lon_edge, lat_edge, corner, w_qkv, pair_bias, gain_one
    )
    grad_mixed, grad_res, keep_one, send_one, sum_gain_two = mlp_call(
        xw, mix, cotangent, cot_lon, cot_lat, cot_corner, w_proj, w_up, w_down, gain_two
    )
    grads_first, bias = first_back(qkv, probs, grad_mixed)
    held_one = core_sum(keep_one, send_one)
    grads_second, keep_two, send_two = second_back(
        qkv, probs, grad_mixed, act_t, sum_gain_two, after(bias, held_one), grads_first
    )
    held_one = first_sum(held_one)
    held_two = first_sum(core_sum(keep_two, after(send_two, held_one)))
    share = second_sum(jnp.concatenate([held_one, held_two], 1))
    home = branch(xw, after(grads_first, share), grads_second, grad_res, w_qkv, gain_one)
    share = after(last_sum(share), home)
    home = send_home(*home)
    own, other = spread(share, home)
    *weights, sums, rest = finish_own(own, w_qkv, scale)
    sum_up, sum_down, sum_qkv, sum_proj, sum_bias, sum_one, sum_two = finish(
        other, w_qkv, gain_one, sums, rest, weights, scale
    )
    return (
        assemble(*[after(piece, sums) for piece in home]),
        sum_qkv,
        sum_proj,
        sum_up,
        sum_down,
        sum_bias,
        sum_one.reshape(D),
        sum_two.reshape(D),
    )


def solution(mesh):
    grid = P(None, "lat", "lon", None)
    in_specs = (grid, grid, P(), P(), P(), P(), P(), P(), P())
    out_specs = (grid, P(), P(), P(), P(), P(), P(), P())
    return jax.shard_map(local, mesh=mesh, in_specs=in_specs, out_specs=out_specs, check_vma=False)
```

```python
import functools

import jax
import jax.numpy as jnp
from jax import lax
from jax.experimental import pallas as pl
from jax.experimental.pallas import tpu as pltpu
from jax.sharding import PartitionSpec as P

HEADS = 8
WLAT = 6
WLON = 12
WT = 144
D = 512
QKV = 1536
FF = 2048
LEVELS = 2
HEIGHT = 12
BREADTH = 48
WINDOWS = 8
ROWS = WINDOWS * WT
EPSILON = 1e-05
MASKED = -1e30
F32 = jnp.float32
BF16 = jnp.bfloat16
PIECES = 32
BAND_ROWS = 512
PROJ_ROWS = 64
ONE_ROWS = BAND_ROWS + PROJ_ROWS
QKV_ROWS = 192
REST_ROWS = 48
TWO_ROWS = QKV_ROWS + REST_ROWS
ALL_ROWS = ONE_ROWS + TWO_ROWS
GAIN_AT = (HEADS + 1) * WT
MIB = 1024 * 1024
M_NORM = 576
M_UP = 1152
M_BACK = 576
M_BRANCH = 576
G_FORWARD = 4
G_BACKWARD = 2
F_STEP = 512

NN = (((1,), (0,)), ((), ()))
NT = (((1,), (1,)), ((), ()))
TN = (((0,), (0,)), ((), ()))


def mm(a, b, dims=NN):
    return lax.dot_general(a, b, dims, preferred_element_type=F32)


def stats_of(values):
    average = jnp.mean(values, -1, keepdims=True)
    centred = values - average
    variance = jnp.mean(centred * centred, -1, keepdims=True)
    inv_std = lax.rsqrt(variance + EPSILON)
    return centred * inv_std, inv_std


def back_of(grad_out, gain_vec, normed, inv_std):
    scaled = grad_out * gain_vec
    return (
        scaled
        - jnp.mean(scaled, -1, keepdims=True)
        - normed * jnp.mean(scaled * normed, -1, keepdims=True)
    ) * inv_std


def run_at(level, row, column):
    window = (row // WLAT) * 4 + column
    return window * WT + level * (WT // 2) + (row % WLAT) * WLON


def gather_windows(main_ref, lon_ref, lat_ref, both_ref, line, wide, out_ref):
    for level in range(LEVELS):
        for row in range(HEIGHT):
            if row < HEIGHT - WLAT // 2:
                line[0:BREADTH] = main_ref[level, row + WLAT // 2].astype(F32)
                line[BREADTH : BREADTH + 6] = lon_ref[level, row + WLAT // 2].astype(F32)
            else:
                line[0:BREADTH] = lat_ref[level, row - (HEIGHT - WLAT // 2)].astype(F32)
                line[BREADTH : BREADTH + 6] = both_ref[level, row - (HEIGHT - WLAT // 2)].astype(F32)
            for column in range(4):
                at = run_at(level, row, column)
                wide[at : at + WLON] = line[6 + WLON * column : 18 + WLON * column]

    def narrow(window, _):
        rows = pl.ds(pl.multiple_of(window * WT, 16), WT)
        out_ref[rows] = wide[rows].astype(BF16)
        return 0

    lax.fori_loop(0, WINDOWS, narrow, 0)


def position(lat, lon):
    return lat % 2, (lon // 2, (lat // 2) % 2 * 2 + lon % 2, lat // 4)


ORDERS = ((0, 1, 2), (1, 2, 0))


def here():
    return position(lax.axis_index("lat"), lax.axis_index("lon"))


def slot_of(core, block):
    _, chip = here()
    first, second = chip[ORDERS[core][0]], chip[ORDERS[core][1]]
    return (block // 4 + 4 - first) % 4 * 4 + (block % 4 + 4 - second) % 4


def block_at(core, first_by, second_by):
    _, chip = here()
    first = jnp.where(core == 0, chip[ORDERS[0][0]], chip[ORDERS[1][0]])
    second = jnp.where(core == 0, chip[ORDERS[0][1]], chip[ORDERS[1][1]])
    return (first + 4 - first_by) % 4 * 4 + (second + 4 - second_by) % 4


def window_rows(window):
    return pl.ds(pl.multiple_of(window * WT, 16), WT)


def softmax_first(scores):
    top = jnp.max(scores, 0, keepdims=True)
    exponent = jnp.exp(scores - top)
    total = jnp.sum(exponent, 0, keepdims=True)
    return (exponent * (1.0 / total)).astype(BF16)


def head_masks():
    lane = lax.broadcasted_iota(jnp.int32, (1, 128), 1)
    first = lane < 64
    row = lax.broadcasted_iota(jnp.int32, (128, D), 0) // 16
    column = lax.broadcasted_iota(jnp.int32, (128, D), 1) // 64
    halves = (first.astype(F32).astype(BF16), (lane >= 64).astype(F32).astype(BF16))
    return first, halves, (row == column).astype(F32)


def tiled(block):
    return jnp.concatenate([block] * HEADS, 0)


def pair_of(head):
    return slice(head // 2 * 128, head // 2 * 128 + 128)


def tail_sum(block, tail):
    return jnp.sum((block * tail).reshape(HEADS, 16, D), 0)


def pack_kernel(ref, lon, lat, both):
    edge, top = WLON // 2, WLAT // 2
    lat[...] = ref[:, :top]
    for level in range(LEVELS):
        for row in range(HEIGHT):
            lon[level, row] = ref[level, row, :edge]
        for row in range(top):
            both[level, row] = ref[level, row, :edge]


def attention_kernel(
    tok, tok_lon, tok_lat, tok_both, w_qkv, pair_bias, gain_one,
    xw_out, mix_out, act_t_out, qkv_out, probs_out,
    line, wide, act, qkv, probs, bias, xw, mix, act_t, sent,
):
    gather_windows(tok, tok_lon, tok_lat, tok_both, line, wide, xw)
    copies = [pltpu.make_async_copy(xw, xw_out, sent.at[WINDOWS + 1])]
    copies[0].start()

    def norm_one(window, _):
        rows = window_rows(window)
        values, _ = stats_of(xw[rows].astype(F32))
        act[rows] = (values * gain_one[...]).astype(BF16)
        return 0

    lax.fori_loop(0, WINDOWS, norm_one, 0)

    def project(n, _):
        cols = pl.ds(pl.multiple_of(n * 256, 256), 256)
        qkv[:, cols] = mm(act[...], w_qkv[:, cols]).astype(BF16)
        return 0

    lax.fori_loop(0, QKV // 256, project, 0)
    act_t[...] = act[...].T
    copies.append(pltpu.make_async_copy(qkv, qkv_out, sent.at[WINDOWS]))
    copies.append(pltpu.make_async_copy(act_t, act_t_out, sent.at[WINDOWS + 2]))
    for copy in copies[1:]:
        copy.start()

    is_last = lax.axis_index("lat") == lax.axis_size("lat") - 1
    key_at = lax.broadcasted_iota(jnp.int32, (WT, 128), 0)
    query_at = lax.broadcasted_iota(jnp.int32, (WT, 128), 1)

    def masked(query_at):
        apart = (key_at // WLON % WLAT >= WLAT // 2) != (query_at // WLON % WLAT >= WLAT // 2)
        return jnp.where(apart & is_last, MASKED, 0.0)

    mask_main = masked(query_at)
    mask_tail = masked(128 + query_at % 16)
    for head in range(HEADS):
        block = pair_bias[head, 0:128].T
        bias[0, head] = block
        bias[1, head] = block + mask_main
    block = jnp.concatenate([pair_bias[head, 128:WT] for head in range(HEADS)], 0).T
    bias[0, HEADS] = block
    bias[1, HEADS] = block + mask_tail

    first, halves, tail = head_masks()
    halves = [half * 0.125 for half in halves]
    tail_low = (tail * 0.125).astype(BF16)

    def mix_copy(group):
        at = pl.ds(pl.multiple_of(group * G_FORWARD * WT, 16), G_FORWARD * WT)
        return pltpu.make_async_copy(mix.at[at], mix_out.at[at], sent.at[WINDOWS + 3 + group])

    def attend(group, _):
        windows = [group * G_FORWARD + i for i in range(G_FORWARD)]
        heads = [(i, head) for i in range(G_FORWARD) for head in range(HEADS)]
        rows = [window_rows(window) for window in windows]
        main = [pl.ds(pl.multiple_of(window * WT, 16), 128) for window in windows]
        last = [pl.ds(pl.multiple_of(window * WT + 128, 16), 16) for window in windows]
        key = [qkv[r, D : 2 * D] for r in rows]
        val = [qkv[r, 2 * D : 3 * D] for r in rows]
        tail_scores = [
            mm(k, tiled(qkv[r, 0:D]) * tail_low, NT) for k, r in zip(key, last)
        ]
        scores = [
            mm(key[i][:, pair_of(head)], qkv[main[i], pair_of(head)] * halves[head % 2], NT)
            for i, head in heads
        ]
        tail_weights = [
            softmax_first(t + bias[window // 4, HEADS]) for t, window in zip(tail_scores, windows)
        ]
        weights = [
            softmax_first(t + bias[windows[i] // 4, head]) for t, (i, head) in zip(scores, heads)
        ]
        tail_mixed = [mm(w, v, TN) for w, v in zip(tail_weights, val)]
        mixed = [mm(w, val[i][:, pair_of(head)], TN) for w, (i, head) in zip(weights, heads)]
        for i, window in enumerate(windows):
            probs[window, HEADS] = tail_weights[i]
            mix[last[i]] = tail_sum(tail_mixed[i], tail).astype(BF16)
        for w, (i, head) in zip(weights, heads):
            probs[windows[i], head] = w
        for n, (i, head) in enumerate(heads):
            if head % 2 == 0:
                mix[main[i], pair_of(head)] = jnp.where(first, mixed[n], mixed[n + 1]).astype(BF16)
        for window in windows:
            pltpu.make_async_copy(probs.at[window], probs_out.at[window], sent.at[window]).start()
        mix_copy(group).start()
        return 0

    lax.fori_loop(0, WINDOWS // G_FORWARD, attend, 0)
    for copy in copies + [mix_copy(group) for group in range(WINDOWS // G_FORWARD)]:
        copy.wait()
    for window in range(WINDOWS):
        pltpu.make_async_copy(probs.at[window], probs_out.at[window], sent.at[window]).wait()


def mlp_kernel(
    xw, mix, cot, cot_lon, cot_lat, cot_both, w_proj, w_up_in, w_down_in, gain_two,
    grad_mixed, grad_res, keep_one, send_one, sum_gain,
    line, wide, cotw, act, normed, inv_two, act_t, activated, grad_hidden, sums, w_up, w_down,
    got, sent,
):
    loads = [
        pltpu.make_async_copy(w_up_in, w_up, got.at[0]),
        pltpu.make_async_copy(w_down_in, w_down, got.at[1]),
    ]
    for load in loads:
        load.start()
    gather_windows(cot, cot_lon, cot_lat, cot_both, line, wide, cotw)

    def norm_two(part, _):
        rows = pl.ds(pl.multiple_of(part * M_NORM, 16), M_NORM)
        residual = xw[rows].astype(F32) + mm(mix[rows], w_proj[...])
        values, inv_std = stats_of(residual)
        normed[rows] = values
        inv_two[rows] = inv_std
        act[rows] = (values * gain_two[...]).astype(BF16)
        return 0

    lax.fori_loop(0, ROWS // M_NORM, norm_two, 0)
    act_t[...] = act[...].T
    for load in loads:
        load.wait()

    c0 = 0.7978845608028654
    c1 = c0 * 0.044715

    def mlp(f, _):
        cols = pl.ds(pl.multiple_of(f * F_STEP, F_STEP), F_STEP)

        def rows_of(r, _):
            rows = pl.ds(pl.multiple_of(r * M_UP, 16), M_UP)
            u = mm(act[rows], w_up[:, cols])
            grad_act = mm(cotw[rows], w_down[cols, :], NT)
            square = u * u
            gate = 0.5 + 0.5 * jnp.tanh(u * (c0 + c1 * square))
            value = u * gate
            activated[rows] = value.astype(BF16)
            slope = gate + value * (1.0 - gate) * (2.0 * c0 + 6.0 * c1 * square)
            grad_hidden[rows, cols] = (grad_act * slope).astype(BF16)
            return 0

        lax.fori_loop(0, ROWS // M_UP, rows_of, 0)
        up = mm(act_t[...], grad_hidden[:, cols]).astype(BF16)
        for j in range(4):
            at = pl.ds(pl.multiple_of(f * 128 + 32 * j, 32), 32)
            sums[0:16, at] = up[:, 128 * j : 128 * j + 128].reshape(16, 32, 128)
        down = mm(activated[...], cotw[...], TN).astype(BF16)
        for i in range(4):
            for j in range(4):
                part = down[128 * i : 128 * i + 128, 128 * j : 128 * j + 128]
                sums[16 + f * 4 + i, 128 * j : 128 * j + 128] = part
        return 0

    lax.fori_loop(0, FF // F_STEP, mlp, 0)

    core, _ = here()

    def send(rows, at, act_on):
        for owner in range(2):
            for block in range(16):
                piece = owner * 16 + block
                slot = slot_of(owner, block)

                def copy_to(out):
                    return pltpu.make_async_copy(
                        sums.at[piece, rows], out.at[slot, rows], sent.at[at, piece]
                    )

                @pl.when(core == owner)
                def _():
                    act_on(copy_to(keep_one))

                @pl.when(core != owner)
                def _():
                    act_on(copy_to(send_one))

    bands, tails = pl.ds(0, BAND_ROWS), pl.ds(BAND_ROWS, PROJ_ROWS)
    send(bands, 0, lambda copy: copy.start())

    def back(part, total):
        rows = pl.ds(pl.multiple_of(part * M_BACK, 16), M_BACK)
        grads = mm(grad_hidden[rows], w_up[...], NT)
        values = normed[rows]
        total = total + jnp.sum(grads * values, 0, keepdims=True)
        residual = cotw[rows].astype(F32) + back_of(grads, gain_two[...], values, inv_two[rows])
        grad_res[rows] = residual
        low = residual.astype(BF16)
        act[rows] = low
        grad_mixed[rows] = mm(low, w_proj[...], NT).astype(BF16)
        return total

    sum_gain[...] = lax.fori_loop(0, ROWS // M_BACK, back, jnp.zeros((1, D), F32))
    proj = mm(mix[...], act[...], TN).astype(BF16)
    for j in range(4):
        at = slice(BAND_ROWS + 16 * j, BAND_ROWS + 16 * j + 16)
        sums[:, at] = proj[:, 128 * j : 128 * j + 128].reshape(PIECES, 16, 128)
    send(tails, 1, lambda copy: copy.start())
    send(bands, 0, lambda copy: copy.wait())
    send(tails, 1, lambda copy: copy.wait())


def first_back_kernel(qkv, probs, grad_mixed, grad_qkv, bias):
    window_back(qkv, probs, grad_mixed, grad_qkv, bias, None)


def second_back_kernel(
    qkv, probs, grad_mixed, act_t, sum_gain_two, bias_before, grads_before,
    grad_qkv, keep_two, send_two,
    grads_all, bias, flat,
):
    step = pl.program_id(0)

    @pl.when(step == 0)
    def _():
        grads_all[0 : ROWS // 2] = grads_before[...]

    window_back(qkv, probs, grad_mixed, grad_qkv, bias, bias_before)
    size = G_BACKWARD * WT
    at = pl.multiple_of(ROWS // 2 + step * size, 16)
    grads_all[pl.ds(at, size)] = grad_qkv[...]

    @pl.when(step == WINDOWS // 2 // G_BACKWARD - 1)
    def _():
        for n in range(QKV // 512):
            part = mm(act_t[...], grads_all[:, 512 * n : 512 * n + 512]).astype(BF16)
            for j in range(4):
                at = (n * 4 + j) * 16
                flat[:, at : at + 16] = part[:, 128 * j : 128 * j + 128].reshape(PIECES, 16, 128)
        gains = [sum_gain_two[:, 128 * j : 128 * j + 128] for j in range(4)]
        gains = jnp.concatenate(gains + [jnp.zeros((12, 128), F32)], 0)
        rest = [bias[block].astype(BF16) for block in range(HEADS + 1)] + [gains.astype(BF16)]
        rest.append(jnp.zeros((PIECES * REST_ROWS - GAIN_AT - 16, 128), BF16))
        rest = jnp.concatenate(rest, 0)
        flat[:, QKV_ROWS:TWO_ROWS] = rest.reshape(PIECES, REST_ROWS, 128)
        core, _ = here()
        for owner in range(2):
            for block in range(16):
                slot = slot_of(owner, block)
                piece = flat[owner * 16 + block]

                @pl.when(core == owner)
                def _():
                    keep_two[slot] = piece

                @pl.when(core != owner)
                def _():
                    send_two[slot] = piece


def window_back(qkv, probs, grad_mixed, grad_qkv, bias, bias_before):
    step = pl.program_id(0)
    first, halves, tail = head_masks()
    tail_low = tail.astype(BF16)

    @pl.when(step == 0)
    def _():
        bias[...] = jnp.zeros_like(bias) if bias_before is None else bias_before[...]

    group = range(G_BACKWARD)
    heads = [(i, head) for i in group for head in range(HEADS)]
    rows = [slice(i * WT, i * WT + WT) for i in group]
    main = [slice(i * WT, i * WT + 128) for i in group]
    last = [slice(i * WT + 128, i * WT + WT) for i in group]
    key = [qkv[r, D : 2 * D] for r in rows]
    val = [qkv[r, 2 * D : 3 * D] for r in rows]
    query_tail = [tiled(qkv[r, 0:D]) * tail_low for r in last]
    out_tail = [tiled(grad_mixed[r]) * tail_low for r in last]
    query = [qkv[main[i], pair_of(head)] * halves[head % 2] for i, head in heads]
    out = [grad_mixed[main[i], pair_of(head)] * halves[head % 2] for i, head in heads]

    tail_probs = [mm(v, o, NT) for v, o in zip(val, out_tail)]
    grad_probs = [mm(val[i][:, pair_of(head)], o, NT) for o, (i, head) in zip(out, heads)]

    def score_grads(low_probs, grad_probs):
        weights = low_probs.astype(F32)
        product = grad_probs * weights
        return product - weights * jnp.sum(product, 0, keepdims=True)

    tail_low_probs = [probs[i, HEADS] for i in group]
    low_probs = [probs[i, head] for i, head in heads]
    tail_grads = [score_grads(p, g) for p, g in zip(tail_low_probs, tail_probs)]
    grads = [score_grads(p, g) for p, g in zip(low_probs, grad_probs)]
    bias[HEADS] += sum(tail_grads[1:], tail_grads[0])
    for head in range(HEADS):
        mine = grads[head::HEADS]
        bias[head] += sum(mine[1:], mine[0])
    tail_grads = [g.astype(BF16) for g in tail_grads]
    grads = [g.astype(BF16) for g in grads]

    query_last = [mm(g, k, TN) for g, k in zip(tail_grads, key)]
    key_more = [mm(g, q) for g, q in zip(tail_grads, query_tail)]
    val_more = [mm(p, o) for p, o in zip(tail_low_probs, out_tail)]
    query_parts = [mm(g, key[i][:, pair_of(head)], TN) for g, (i, head) in zip(grads, heads)]
    key_parts = [mm(g, q) for g, q in zip(grads, query)]
    val_parts = [mm(p, o) for p, o in zip(low_probs, out)]
    for i in group:
        grad_qkv[last[i], 0:D] = (tail_sum(query_last[i], tail) * 0.125).astype(BF16)
    for n, (i, head) in enumerate(heads):
        if head % 2:
            continue
        cols = pair_of(head)
        at = head // 2 * 128
        part = jnp.where(first, query_parts[n], query_parts[n + 1]) * 0.125
        grad_qkv[main[i], cols] = part.astype(BF16)
        part = (key_parts[n] + key_parts[n + 1] + key_more[i][:, cols]) * 0.125
        grad_qkv[rows[i], D + at : D + at + 128] = part.astype(BF16)
        part = val_parts[n] + val_parts[n + 1] + val_more[i][:, cols]
        grad_qkv[rows[i], 2 * D + at : 2 * D + at + 128] = part.astype(BF16)

def branch_kernel(xw, grads_first, grads_second, grad_res, w_qkv, gain_one, main, lon, lat, both, wide, line):
    for part, grad_qkv in enumerate((grads_first, grads_second)):
        rows = slice(part * ROWS // 2, (part + 1) * ROWS // 2)
        values, inv_std = stats_of(xw[rows].astype(F32))
        grads = mm(grad_qkv[...], w_qkv[...], NT)
        low = back_of(grads, gain_one[...], values, inv_std).astype(BF16)
        wide[rows] = grad_res[rows] + low.astype(F32)

    for level in range(LEVELS):
        for row in range(HEIGHT):
            for column in range(4):
                at = run_at(level, row, column)
                line[WLON * column : WLON * column + WLON] = wide[at : at + WLON]
            inner, outer = (main, lon) if row < HEIGHT - WLAT // 2 else (lat, both)
            at = row if row < HEIGHT - WLAT // 2 else row - (HEIGHT - WLAT // 2)
            inner[level, at] = line[0 : BREADTH - 6].astype(BF16)
            outer[level, at] = line[BREADTH - 6 : BREADTH].astype(BF16)


def write_pieces(scale, owner, pieces, w_qkv, outs, sums, rest, buffers, sent):
    up_out, down_out, qkv_out, proj_out = outs
    buffer_up, buffer_down, buffer_qkv, buffer_proj = buffers

    def run(buffer_band, band, fill_band, band_out):
        def copies(n):
            block = block_at(owner, n // 4, n % 4)
            piece = owner * 16 + block
            slot = n % BUFFERS
            targets = ((buffer_band, band_out, band, block), (buffer_qkv, qkv_out, 16, piece),
                       (buffer_proj, proj_out, 16, piece))
            return [
                pltpu.make_async_copy(
                    buffer.at[slot],
                    out.at[pl.ds(pl.multiple_of(at * size, size), size)],
                    sent.at[i, slot],
                )
                for i, (buffer, out, size, at) in enumerate(targets)
            ]

        for n in range(16):
            if n >= BUFFERS:
                for copy in copies(n - BUFFERS):
                    copy.wait()
            slot = n % BUFFERS
            piece = owner * 16 + block_at(owner, n // 4, n % 4)
            rows = pl.ds(pl.multiple_of(piece * 16, 16), 16)
            held = pieces[n // 4]
            fill_band(held, n % 4, slot)
            for j in range(4):
                at = BAND_ROWS + 16 * j
                part = held[n % 4, at : at + 16].astype(F32) * scale
                buffer_proj[slot, :, 128 * j : 128 * j + 128] = part
            total = jnp.zeros((16, 128), F32)
            for j in range(12):
                cols = slice(128 * j, 128 * j + 128)
                at = ONE_ROWS + 16 * j
                part = held[n % 4, at : at + 16].astype(F32) * scale
                buffer_qkv[slot, :, cols] = part
                total = total + part * w_qkv[rows, cols].astype(F32)
            sums[rows] = total
            rest[piece] = held[n % 4, ONE_ROWS + QKV_ROWS : ALL_ROWS]
            for copy in copies(n):
                copy.start()
        for n in range(16 - BUFFERS, 16):
            for copy in copies(n):
                copy.wait()

    def fill_up(held, at, slot):
        for j in range(16):
            part = held[at, 32 * j : 32 * j + 32].astype(F32) * scale
            buffer_up[slot, :, 128 * j : 128 * j + 128] = part

    def fill_down(held, at, slot):
        for j in range(4):
            part = held[at, 128 * j : 128 * j + 128].astype(F32) * scale
            buffer_down[slot, :, 128 * j : 128 * j + 128] = part

    @pl.when(owner == 0)
    def _():
        run(buffer_up, 32, fill_up, up_out)

    @pl.when(owner == 1)
    def _():
        run(buffer_down, 128, fill_down, down_out)


def finish_own_kernel(scale, *refs):
    pieces, w_qkv, outs, sums, rest = refs[:4], refs[4], refs[5:9], refs[9], refs[10]
    write_pieces(scale, here()[0], pieces, w_qkv, outs, sums, rest, refs[11:15], refs[15])


def finish_kernel(scale, *refs):
    pieces, w_qkv, gain_vec, sums_own, rest_own = refs[:4], refs[4], refs[5], refs[6], refs[7]
    outs, (bias, gain_one, gain_two) = refs[12:16], refs[16:19]
    buffers, sent, sums, rest = refs[19:23], refs[23], refs[24], refs[25]
    sums[...] = sums_own[...]
    rest[...] = rest_own[...]
    write_pieces(scale, 1 - here()[0], pieces, w_qkv, outs, sums, rest, buffers, sent)
    gain_one[...] = jnp.sum(sums[...].T, 0, keepdims=True) / gain_vec[...]
    flat = rest[...].reshape(PIECES * REST_ROWS, 128).astype(F32)
    last = flat[HEADS * WT : GAIN_AT].T * (scale * WT)
    for head in range(HEADS):
        bias[head, 0:128] = flat[head * WT : head * WT + WT].T * (scale * WT)
        bias[head, 128:WT] = last[16 * head : 16 * head + 16]
    for j in range(4):
        part = flat[GAIN_AT + j : GAIN_AT + j + 1] * scale
        gain_two[:, 128 * j : 128 * j + 128] = part


def shape(*dims, dtype=BF16):
    return jax.ShapeDtypeStruct(dims, dtype)


def params(mib):
    return pltpu.CompilerParams(vmem_limit_bytes=mib * MIB)


def vmem(*dims, dtype=BF16):
    return pltpu.VMEM(dims, dtype)


def cost(flops, moved):
    return pl.CostEstimate(flops=flops, bytes_accessed=moved, transcendentals=0)


ANY = pl.BlockSpec(memory_space=pl.ANY)
INSIDE = pl.BlockSpec(memory_space=pltpu.VMEM)
SCALARS = pl.BlockSpec(memory_space=pltpu.SMEM)


def pack(grid):
    edge, top = WLON // 2, WLAT // 2
    return pl.pallas_call(
        pack_kernel,
        out_shape=(
            shape(LEVELS, HEIGHT, edge, D), shape(LEVELS, top, BREADTH, D),
            shape(LEVELS, top, edge, D),
        ),
        in_specs=[INSIDE],
        out_specs=[INSIDE] * 3,
        compiler_params=params(16),
        name="pack",
    )(grid)


def attention(*operands):
    return pl.pallas_call(
        attention_kernel,
        out_shape=(
            shape(ROWS, D), shape(ROWS, D), shape(D, ROWS), shape(ROWS, QKV),
            shape(WINDOWS, HEADS + 1, WT, 128),
        ),
        in_specs=[INSIDE] * len(operands),
        out_specs=[ANY] * 5,
        scratch_shapes=[
            vmem(56, D, dtype=F32), vmem(ROWS, D, dtype=F32), vmem(ROWS, D), vmem(ROWS, QKV),
            vmem(WINDOWS, HEADS + 1, WT, 128), vmem(2, HEADS + 1, WT, 128, dtype=F32),
            vmem(ROWS, D), vmem(ROWS, D), vmem(D, ROWS),
            pltpu.SemaphoreType.DMA((WINDOWS + 3 + WINDOWS // G_FORWARD,)),
        ],
        compiler_params=params(60),
        cost_estimate=cost(ROWS * D * QKV * 2 * 4, 20_000_000),
        name="attention",
    )(*operands)


def mlp_call(*operands):
    return pl.pallas_call(
        mlp_kernel,
        out_shape=(
            shape(ROWS, D), shape(ROWS, D, dtype=F32), shape(16, ONE_ROWS, 128),
            shape(16, ONE_ROWS, 128), shape(1, D, dtype=F32),
        ),
        in_specs=[INSIDE] * 7 + [ANY, ANY, INSIDE],
        out_specs=[INSIDE, INSIDE, ANY, ANY, INSIDE],
        scratch_shapes=[
            vmem(56, D, dtype=F32), vmem(ROWS, D, dtype=F32), vmem(ROWS, D), vmem(ROWS, D),
            vmem(ROWS, D, dtype=F32), vmem(ROWS, 1, dtype=F32), vmem(D, ROWS),
            vmem(ROWS, F_STEP), vmem(ROWS, FF), vmem(PIECES, ONE_ROWS, 128),
            vmem(D, FF), vmem(FF, D),
            pltpu.SemaphoreType.DMA((2,)), pltpu.SemaphoreType.DMA((2, PIECES)),
        ],
        compiler_params=params(56),
        cost_estimate=cost(ROWS * D * FF * 2 * 8, 40_000_000),
        name="mlp",
    )(*operands)


def back_specs(half):
    start = half * (WINDOWS // 2 // G_BACKWARD)
    return [
        pl.BlockSpec((G_BACKWARD * WT, QKV), lambda i: (start + i, 0)),
        pl.BlockSpec((G_BACKWARD, HEADS + 1, WT, 128), lambda i: (start + i, 0, 0, 0)),
        pl.BlockSpec((G_BACKWARD * WT, D), lambda i: (start + i, 0)),
    ]


def first_back(qkv, probs, grad_mixed):
    return pl.pallas_call(
        first_back_kernel,
        out_shape=(shape(ROWS // 2, QKV), shape(HEADS + 1, WT, 128, dtype=F32)),
        grid=(WINDOWS // 2 // G_BACKWARD,),
        in_specs=back_specs(0),
        out_specs=[
            pl.BlockSpec((G_BACKWARD * WT, QKV), lambda i: (i, 0)),
            pl.BlockSpec((HEADS + 1, WT, 128), lambda i: (0, 0, 0)),
        ],
        compiler_params=params(32),
        cost_estimate=cost(ROWS * D * QKV * 2 * 3, 10_000_000),
        name="first_back",
    )(qkv, probs, grad_mixed)


def second_back(*operands):
    return pl.pallas_call(
        second_back_kernel,
        out_shape=(
            shape(ROWS // 2, QKV), shape(16, TWO_ROWS, 128), shape(16, TWO_ROWS, 128),
        ),
        grid=(WINDOWS // 2 // G_BACKWARD,),
        in_specs=back_specs(1) + [INSIDE] * 4,
        out_specs=[pl.BlockSpec((G_BACKWARD * WT, QKV), lambda i: (i, 0)), INSIDE, INSIDE],
        scratch_shapes=[
            vmem(ROWS, QKV), vmem(HEADS + 1, WT, 128, dtype=F32), vmem(PIECES, TWO_ROWS, 128),
        ],
        compiler_params=params(40),
        cost_estimate=cost(ROWS * D * QKV * 2 * 4, 10_000_000),
        name="second_back",
    )(*operands)


def branch(*operands):
    return pl.pallas_call(
        branch_kernel,
        out_shape=(
            shape(LEVELS, 9, 42, D), shape(LEVELS, 9, 6, D), shape(LEVELS, 3, 42, D),
            shape(LEVELS, 3, 6, D),
        ),
        in_specs=[INSIDE] * len(operands),
        out_specs=[INSIDE] * 4,
        scratch_shapes=[vmem(ROWS, D, dtype=F32), vmem(48, D, dtype=F32)],
        compiler_params=params(24),
        cost_estimate=cost(ROWS * D * QKV * 2 * 4, 10_000_000),
        name="branch",
    )(*operands)


BUFFERS = 4


def finish_scratch():
    return [
        vmem(BUFFERS, 32, FF, dtype=F32), vmem(BUFFERS, 128, D, dtype=F32),
        vmem(BUFFERS, 16, QKV, dtype=F32), vmem(BUFFERS, 16, D, dtype=F32),
        pltpu.SemaphoreType.DMA((3, BUFFERS)),
    ]


WEIGHT_SHAPES = (
    shape(D, FF, dtype=F32), shape(FF, D, dtype=F32), shape(D, QKV, dtype=F32),
    shape(D, D, dtype=F32),
)


def finish_own(pieces, w_qkv, scale):
    return pl.pallas_call(
        functools.partial(finish_own_kernel, scale),
        out_shape=WEIGHT_SHAPES + (shape(D, 128, dtype=F32), shape(PIECES, REST_ROWS, 128)),
        in_specs=[INSIDE] * 5,
        out_specs=[ANY] * 4 + [INSIDE] * 2,
        scratch_shapes=finish_scratch(),
        compiler_params=params(24),
        cost_estimate=cost(10_000_000, 10_000_000),
        name="finish_own",
    )(*pieces, w_qkv)


def finish(pieces, w_qkv, gain_one, sums, rest, weights, scale):
    return pl.pallas_call(
        functools.partial(finish_kernel, scale),
        out_shape=WEIGHT_SHAPES + (
            shape(HEADS, WT, WT, dtype=F32), shape(1, D, dtype=F32), shape(1, D, dtype=F32),
        ),
        in_specs=[INSIDE] * 8 + [ANY] * 4,
        out_specs=[ANY] * 4 + [INSIDE] * 3,
        input_output_aliases={8: 0, 9: 1, 10: 2, 11: 3},
        scratch_shapes=finish_scratch() + [
            vmem(D, 128, dtype=F32), vmem(PIECES, REST_ROWS, 128),
        ],
        compiler_params=params(24),
        cost_estimate=cost(10_000_000, 10_000_000),
        name="finish",
    )(*pieces, w_qkv, gain_one, sums, rest, *weights)


def neighbour(array, lat_by, lon_by):
    lat_count, lon_count = lax.axis_size("lat"), lax.axis_size("lon")
    pairs = []
    for i in range(lat_count):
        for j in range(lon_count):
            to = ((i + lat_by) % lat_count) * lon_count + (j + lon_by) % lon_count
            pairs.append((i * lon_count + j, to))
    return lax.ppermute(array, ("lat", "lon"), pairs)


def halos(grid):
    lon, lat, both = pack(grid)
    return neighbour(lat, -1, 0), neighbour(lon, 0, -1), neighbour(both, -1, -1)


def send_home(main, lon, lat, both):
    return main, neighbour(lon, 0, 1), neighbour(lat, 1, 0), neighbour(both, 1, 1)


def assemble(main, lon, lat, both):
    upper = jnp.concatenate([both, lat], 2)
    lower = jnp.concatenate([lon, main], 2)
    return jnp.concatenate([upper, lower], 1)


def along(array, stage, by):
    pairs = []
    for lat in range(16):
        for lon in range(8):
            core, chip = position(lat, lon)
            chip = list(chip)
            axis = ORDERS[core][stage]
            chip[axis] = (chip[axis] + by) % 4
            x, y, z = chip
            to = (z * 4 + y // 2 * 2 + core) * 8 + x * 2 + y % 2
            pairs.append((lat * 8 + lon, to))
    return lax.ppermute(array, ("lat", "lon"), pairs)


def other_core(array):
    return lax.ppermute(array, "lat", [(i, i ^ 1) for i in range(16)])


def added(*terms):
    total = terms[0].astype(F32)
    for term in terms[1:]:
        total = total + term.astype(F32)
    return total.astype(BF16)


def after(value, *others):
    return lax.optimization_barrier((value, others))[0]


def core_sum(keep, send):
    return added(keep, other_core(send))


def first_sum(held):
    return added(held[:4], *[along(held[4 * k : 4 * k + 4], 0, k) for k in (1, 2, 3)])


def second_sum(held):
    return added(held[0], *[along(held[k], 1, k) for k in (1, 2, 3)])


def last_sum(share):
    share = lax.optimization_barrier(share)
    one, two, three = [along(share, 2, k).astype(F32) for k in (1, 2, 3)]
    return ((share.astype(F32) + two) + (one + three)).astype(BF16)


def spread(share, home):
    held = jnp.stack([share] + [along(share, 1, k) for k in (1, 2, 3)])
    held = after(held, home)
    grad_tokens = assemble(*[after(piece, held) for piece in home])
    own = [held] + [along(held, 0, k) for k in (1, 2, 3)]
    other = [other_core(held)] + [other_core(after(piece, grad_tokens)) for piece in own[1:]]
    return own, other, grad_tokens


def local(tokens, cotangent, w_qkv, w_proj, w_up, w_down, pair_bias, gain_one, gain_two):
    total_tokens = ROWS * lax.axis_size("lat") * lax.axis_size("lon")
    scale = total_tokens ** (-0.5)
    gain_one = gain_one.reshape(1, D)
    gain_two = gain_two.reshape(1, D)
    lat_edge, lon_edge, corner = halos(tokens)
    cot_lat, cot_lon, cot_corner = halos(cotangent)
    xw, mix, act_t, qkv, probs = attention(
        tokens, lon_edge, lat_edge, corner, w_qkv, pair_bias, gain_one
    )
    grad_mixed, grad_res, keep_one, send_one, sum_gain_two = mlp_call(
        xw, mix, cotangent, cot_lon, cot_lat, cot_corner, w_proj, w_up, w_down, gain_two
    )
    grads_first, bias = first_back(qkv, probs, grad_mixed)
    held_one = core_sum(keep_one, send_one)
    grads_second, keep_two, send_two = second_back(
        qkv, probs, grad_mixed, act_t, sum_gain_two, after(bias, held_one), grads_first
    )
    held_one = first_sum(held_one)
    held_two = first_sum(core_sum(keep_two, after(send_two, held_one)))
    share = second_sum(jnp.concatenate([held_one, held_two], 1))
    home = branch(xw, after(grads_first, share), grads_second, grad_res, w_qkv, gain_one)
    share = after(last_sum(share), home)
    home = send_home(*home)
    own, other, grad_tokens = spread(share, home)
    *weights, sums, rest = finish_own(own, w_qkv, scale)
    sum_up, sum_down, sum_qkv, sum_proj, sum_bias, sum_one, sum_two = finish(
        other, w_qkv, gain_one, sums, rest, weights, scale
    )
    return (
        grad_tokens,
        sum_qkv,
        sum_proj,
        sum_up,
        sum_down,
        sum_bias,
        sum_one.reshape(D),
        sum_two.reshape(D),
    )


def solution(mesh):
    grid = P(None, "lat", "lon", None)
    in_specs = (grid, grid, P(), P(), P(), P(), P(), P(), P())
    out_specs = (grid, P(), P(), P(), P(), P(), P(), P())
    return jax.shard_map(local, mesh=mesh, in_specs=in_specs, out_specs=out_specs, check_vma=False)
```
